128 devices in a mesh: grp: 8 (over y, core), leaf: 16 (over x, z).
Axes of the slice: x: 4, y: 4, z: 4, core: 2. Of those that a mesh axis runs over, the one named last changes fastest.
Arguments:
- points: bfloat16 [32, 262144], P(None, ('grp', 'leaf')), may hold values from -6 to 6
- right_side: float32 [8, 262144], P(None, ('grp', 'leaf')), may hold values from -6 to 6
- neighbours: int32 [256, 8], P(('grp', 'leaf')), may hold values from 0 to 31, as said below
- neighbour_count: int32 [256], P(('grp', 'leaf')), may hold values from 1 to 8, as said below
- mid_skeleton: int32 [128, 256], P(('grp', 'leaf')), may hold values from 0 to 2047, as said below
- top_skeleton: int32 [8, 256], P('grp'), may hold values from 0 to 32767, as said below
- mid_basis: float32 [256, 262144], P(None, ('grp', 'leaf')), may hold values from -0.125 to 0.125
- top_basis: float32 [256, 262144], P(None, ('grp', 'leaf')), may hold values from -0.125 to 0.125
- noise_level: float32 [1], replicated, may hold values from 1 to 2
Outputs:
- solution: float32 [8, 262144], P(None, ('grp', 'leaf'))
- residual: float32 [8, 262144], P(None, ('grp', 'leaf'))
The draws below stay inside these ranges and needn't reach their ends.
Inputs may be any that keep to these rules, and one draw needn't show every extreme that they name: `neighbours`: entry 0 of leaf l is l itself; entries 1 to neighbour_count[l] - 1 are distinct other leaves of the same subtree; later entries repeat l. Leaf j is listed by l exactly when l is listed by j. `neighbour_count`: the number of listed entries of each leaf, itself included. `mid_skeleton`: distinct positions within each block. `top_skeleton`: distinct positions within each subtree.
All inputs are finite; a program needn't handle non-finite values.
Results may differ from the reference program's by a relative error of at most 0.0003.
Values may be sent and summed in bfloat16 or wider, within the bound.
A program may use at most 128 MiB of HBM per device.

```python
import jax
import jax.numpy as jnp
from jax import lax

FEATURES = 32
TARGETS = 8
LEAF = 1024
RANK = 256
NEIGHBOURS = 8
ITERS = 2
LEAF_DEV = 2
POINTS_DEV = 2048
GROUP_LEAVES = 32
GROUP_POINTS = 32768
LEAVES = 256
POINTS = 262144
N_GRP = 8
N_LEAF = 16


def neighbour_tables(key):
    key = jax.random.fold_in(key, 11)
    key_mask, key_flag, key_level = jax.random.split(key, 3)
    mask_keys = jax.random.split(key_mask, N_GRP)
    xor_masks = jax.vmap(lambda item_key: jax.random.permutation(item_key, GROUP_LEAVES - 1)[:NEIGHBOURS - 1] + 1)(mask_keys).astype(jnp.int32)
    local_ids = jnp.arange(GROUP_LEAVES, dtype=jnp.int32)
    partner = jnp.bitwise_xor(local_ids[None, :, None], xor_masks[:, None, :])
    lower_ids = jnp.minimum(local_ids[None, :, None], partner)
    levels = jax.random.randint(key_level, (N_GRP, N_LEAF), 1, 5)
    flag_draws = jax.random.randint(key_flag, (N_GRP, GROUP_LEAVES, NEIGHBOURS - 1), 0, 4)
    group_ids = jnp.arange(N_GRP, dtype=jnp.int32)[:, None, None]
    slot_ids = jnp.arange(NEIGHBOURS - 1, dtype=jnp.int32)[None, None, :]
    active = (flag_draws[group_ids, lower_ids, slot_ids] < levels[group_ids, lower_ids // LEAF_DEV]) | (lower_ids == 0)
    listed_count = 1 + jnp.sum(active.astype(jnp.int32), axis=-1)
    slot_score = jnp.where(active, slot_ids, NEIGHBOURS + slot_ids)
    slot_order = jnp.argsort(slot_score, axis=-1, stable=True)
    partner_sorted = jnp.take_along_axis(partner, slot_order, axis=-1)
    active_sorted = jnp.take_along_axis(active, slot_order, axis=-1)
    own_ids = jnp.broadcast_to(local_ids[None, :, None], (N_GRP, GROUP_LEAVES, 1))
    listed = jnp.where(active_sorted, partner_sorted, own_ids)
    neighbour_table = jnp.concatenate([own_ids, listed], axis=-1).reshape(LEAVES, NEIGHBOURS)
    return (neighbour_table.astype(jnp.int32), listed_count.reshape(LEAVES).astype(jnp.int32))


def skeleton_positions(key, rows, extent):
    row_keys = jax.random.split(key, rows)
    ends = jnp.array([0, extent - 1], jnp.int32)

    def one_row(item_key):
        inner = jax.random.permutation(item_key, extent - 2)[:RANK - 2].astype(jnp.int32) + 1
        return jnp.concatenate([ends, inner])
    return jax.vmap(one_row)(row_keys)


def draw_neighbours(key, part):
    return neighbour_tables(key)[0]


def draw_neighbour_count(key, part):
    return neighbour_tables(key)[1]


def draw_mid_skeleton(key, part):
    key = jax.random.fold_in(key, 3)
    return skeleton_positions(key, N_GRP * N_LEAF, POINTS_DEV)


def draw_top_skeleton(key, part):
    key = jax.random.fold_in(key, 5)
    return skeleton_positions(key, N_GRP, GROUP_POINTS)


def shard_levels(stream_key, shape, cuts, low, largest):
    loudness, own = 1.0, jax.random.fold_in(stream_key, 6)
    for position, blocks in cuts:
        draws = jnp.exp(jax.random.uniform(jax.random.fold_in(own, position), (blocks,), jnp.float32, low / len(cuts), largest / len(cuts)))
        loudness = loudness * jnp.repeat(draws, shape[position] // blocks).reshape([-1 if axis == position else 1 for axis in range(len(shape))])
    return loudness


def normal_values(rng, dims, width, bound, shards=(), kind=jnp.bfloat16):
    drawn = jax.random.normal(rng, dims, jnp.float32) * width
    if len(shards) > 0:
        drawn = shard_levels(rng, dims, shards, -0.22, 0.18) * drawn
    return jnp.clip(drawn, min=-bound, max=bound).astype(kind)


def setup_inputs(seed: int = 0) -> dict:
    arg_keys = jax.random.split(jax.random.key(seed), 10)
    points = normal_values(arg_keys[0], (FEATURES, POINTS), 1.0, 6.0, ((1, 128),))
    right_side = normal_values(arg_keys[1], (TARGETS, POINTS), 1.0, 6.0, ((1, 128),), jnp.float32)
    neighbours = draw_neighbours(jax.random.fold_in(arg_keys[9], 71), 0)
    neighbour_count = draw_neighbour_count(jax.random.fold_in(arg_keys[9], 71), 0)
    mid_skeleton = draw_mid_skeleton(jax.random.fold_in(arg_keys[9], 71), 0)
    top_skeleton = draw_top_skeleton(jax.random.fold_in(arg_keys[9], 71), 0)
    mid_basis = normal_values(arg_keys[6], (RANK, POINTS), POINTS_DEV ** -0.5, 0.125, ((1, 128),), jnp.float32)
    top_basis = normal_values(arg_keys[7], (RANK, POINTS), POINTS_DEV ** -0.5, 0.125, ((1, 128),), jnp.float32)
    noise_level = jnp.clip(jax.random.uniform(arg_keys[8], (1,), jnp.float32, 1.0, 2.0), 1.0, 2.0)
    return dict(points=points, right_side=right_side, neighbours=neighbours, neighbour_count=neighbour_count, mid_skeleton=mid_skeleton, top_skeleton=top_skeleton, mid_basis=mid_basis, top_basis=top_basis, noise_level=noise_level)


def exact_dot(left_cols, right_cols):
    return jnp.dot(left_cols, right_cols, precision=lax.Precision.HIGHEST, preferred_element_type=jnp.float32)


def kernel(left_cols, right_cols):
    cross_terms = lax.dot_general(left_cols, right_cols, (((0,), (0,)), ((), ())), preferred_element_type=jnp.float32)
    left_sq = jnp.sum(jnp.square(left_cols.astype(jnp.float32)), axis=0)
    right_sq = jnp.sum(jnp.square(right_cols.astype(jnp.float32)), axis=0)
    return jnp.exp((2.0 * cross_terms - left_sq[:, None] - right_sq[None, :]) / FEATURES)


def near_field(vector, points, neighbours, neighbour_count):
    def one_leaf(leaf_id):
        group_start = (leaf_id // GROUP_LEAVES) * GROUP_LEAVES
        own_points = lax.dynamic_slice_in_dim(points, leaf_id * LEAF, LEAF, 1)
        own_vector = lax.dynamic_slice_in_dim(vector, leaf_id * LEAF, LEAF, 1)
        listed = neighbour_count[leaf_id]
        running = listed.astype(jnp.float32) * exact_dot(own_vector, kernel(own_points, own_points))

        def slot_step(carried, slot_index):
            partner = (group_start + neighbours[leaf_id, slot_index]).astype(jnp.int32)

            def compute(current):
                partner_points = lax.dynamic_slice_in_dim(points, partner * LEAF, LEAF, 1)
                partner_vector = lax.dynamic_slice_in_dim(vector, partner * LEAF, LEAF, 1)
                return current + exact_dot(partner_vector, kernel(partner_points, own_points))

            return lax.cond(slot_index < listed, compute, lambda current: current, carried), None

        running, _ = lax.scan(slot_step, running, jnp.arange(1, NEIGHBOURS, dtype=jnp.int32))
        return running

    blocks = lax.map(one_leaf, jnp.arange(LEAVES, dtype=jnp.int32))
    return (LEAF ** -0.5) * jnp.transpose(blocks, (1, 0, 2)).reshape(TARGETS, POINTS)


def skeleton_terms(vector, points, mid_skeleton, top_skeleton, mid_basis, top_basis):
    devices = N_GRP * N_LEAF
    highest = lax.Precision.HIGHEST
    vec_blocks = vector.reshape(TARGETS, devices, POINTS_DEV)
    mid_blocks = mid_basis.reshape(RANK, devices, POINTS_DEV)
    mid_weights = jnp.einsum("rdp,kdp->drk", vec_blocks, mid_blocks, precision=highest)
    point_blocks = points.reshape(FEATURES, devices, POINTS_DEV)
    mid_coords = jnp.take_along_axis(point_blocks, mid_skeleton[None, :, :], axis=2)
    group_weights = mid_weights.reshape(N_GRP, N_LEAF, TARGETS, RANK).transpose(0, 2, 1, 3).reshape(N_GRP, TARGETS, N_LEAF * RANK)
    group_coords = mid_coords.reshape(FEATURES, N_GRP, N_LEAF * RANK).transpose(1, 0, 2)

    def one_group(group_items):
        weights_here, coords_here = group_items
        return (RANK ** -0.5) * exact_dot(weights_here, kernel(coords_here, coords_here))

    mid_images = lax.map(one_group, (group_weights, group_coords))
    mid_images = mid_images.reshape(N_GRP, TARGETS, N_LEAF, RANK).transpose(0, 2, 1, 3).reshape(devices, TARGETS, RANK)
    mid_term = jnp.einsum("drk,kdp->rdp", mid_images, mid_blocks, precision=highest).reshape(TARGETS, POINTS)
    vec_groups = vector.reshape(TARGETS, N_GRP, GROUP_POINTS)
    top_groups = top_basis.reshape(RANK, N_GRP, GROUP_POINTS)
    top_weights = jnp.einsum("rgp,kgp->rgk", vec_groups, top_groups, precision=highest).reshape(TARGETS, N_GRP * RANK)
    top_coords = jnp.take_along_axis(points.reshape(FEATURES, N_GRP, GROUP_POINTS), top_skeleton[None, :, :], axis=2)
    top_coords = top_coords.reshape(FEATURES, N_GRP * RANK)
    top_images = (RANK ** -0.5) * exact_dot(top_weights, kernel(top_coords, top_coords))
    top_term = jnp.einsum("rgk,kgp->rgp", top_images.reshape(TARGETS, N_GRP, RANK), top_groups, precision=highest)
    return mid_term, top_term.reshape(TARGETS, POINTS)


def reference(points, right_side, neighbours, neighbour_count, mid_skeleton, top_skeleton, mid_basis, top_basis, noise_level):
    def operate(field):
        near_term = near_field(field, points, neighbours, neighbour_count)
        mid_term, top_term = skeleton_terms(field, points, mid_skeleton, top_skeleton, mid_basis, top_basis)
        return noise_level[0] * field + near_term + mid_term + top_term

    solution = jnp.zeros_like(right_side)
    residual = right_side
    direction = right_side
    norm_now = jnp.sum(residual * residual, axis=1)
    for step_index in range(ITERS):
        image = operate(direction)
        step_size = norm_now / jnp.sum(direction * image, axis=1)
        solution = solution + step_size[:, None] * direction
        residual = residual - step_size[:, None] * image
        norm_next = jnp.sum(residual * residual, axis=1)
        direction = residual + (norm_next / norm_now)[:, None] * direction
        norm_now = norm_next
    return solution, residual
```

```python
import math

import jax
import jax.numpy as jnp
from jax import lax
from jax.experimental import pallas as pl
from jax.experimental.pallas import tpu as pltpu
from jax.sharding import PartitionSpec as P

FEATURES = 32
TARGETS = 8
LEAF = 1024
RANK = 256
SLOTS = 8
SIDE = 4
N_LEAF = 16
N_GRP = 8
BLOCK = 2 * LEAF
CHUNK = 512
KEPT = 8
MESH = pl.DeviceIdType.MESH
F32 = jnp.float32
BF16 = jnp.bfloat16
SCALE = math.log2(math.e) / 16.0

LABELS = (
    [(1, 0, None), (3, 0, None), (2, 0, 0), (2, 0, 1)]
    + [(df, ds, None) for df in range(4) for ds in (1, 3)]
    + [(df, 2, part) for df in range(4) for part in (0, 1)]
)
PLACE = {label: i for i, label in enumerate(LABELS)}


def dot(left, right):
    return jnp.dot(left, right, preferred_element_type=F32)


def dot_tn(left, right):
    return lax.dot_general(left, right, (((0,), (0,)), ((), ())), preferred_element_type=F32)


def dot_nt(left, right):
    return lax.dot_general(left, right, (((1,), (1,)), ((), ())), preferred_element_type=F32)


def halves(value):
    high = value.astype(BF16)
    return high, (value - high.astype(F32)).astype(BF16)


def stacked(value):
    high = value.astype(BF16).astype(F32)
    return jnp.concatenate([high, value - high], axis=0).astype(BF16)


def folded(value):
    return value[:TARGETS] + value[TARGETS:]


def thirds(coords):
    scaled = coords.astype(F32) * SCALE
    first = scaled.astype(BF16)
    rest = scaled - first.astype(F32)
    second = rest.astype(BF16)
    third = (rest - second.astype(F32)).astype(BF16)
    return jnp.concatenate([first, second, third], axis=0)


def self_scale(coords):
    wide = coords.astype(F32)
    return jnp.exp2(jnp.sum(wide * wide, axis=0, keepdims=True) * (-0.5 * SCALE))


def kernel_halves(rows, columns3):
    return halves(jnp.exp2(dot_tn(jnp.concatenate([rows, rows, rows], axis=0), columns3)))


def applied(field16, high, low):
    return dot(field16, high) + dot(field16, low)


class Gather:
    def __init__(self, half, me, slot, part, send, recv):
        first, second = lax.div(me, SIDE), lax.rem(me, SIDE)
        if half == 1:
            first, second = second, first
        self.half, self.first, self.second = half, first, second
        self.slot, self.part, self.send, self.recv = slot, part, send, recv
        self.sent = []

    def device(self, df, ds):
        f = lax.rem(self.first + SIDE - df, SIDE)
        s = lax.rem(self.second + SIDE - ds, SIDE)
        return f * SIDE + s if self.half == 0 else s * SIDE + f

    def ref(self, df, ds, part):
        block = self.slot(2 * self.device(df, ds) + self.half)
        return block if part is None else self.part(block, part)

    def copy(self, mine, label, part, to):
        place = self.half * len(LABELS) + PLACE[label]
        ref = self.ref(mine[0], mine[1], part)
        return pltpu.make_async_remote_copy(
            src_ref=ref,
            dst_ref=ref,
            send_sem=self.send.at[place],
            recv_sem=self.recv.at[place],
            device_id={"leaf": to},
            device_id_type=MESH,
        )

    def push(self, mine, label, to):
        copy = self.copy(mine, label, label[2], to)
        copy.start()
        self.sent.append(copy)

    def wait(self, *labels):
        for label in labels:
            self.copy(label[:2], label, label[2], self.device(1, 0)).wait_recv()

    def along_first(self, ahead):
        return self.device(3 if ahead else 1, 0)

    def along_second(self, ahead):
        return self.device(0, 3 if ahead else 1)

    def spread(self, df):
        self.push((df, 0), (df, 1, None), self.along_second(True))
        self.push((df, 0), (df, 3, None), self.along_second(False))

    def relay(self, df):
        self.wait((df, 1, None))
        self.push((df, 1), (df, 2, 0), self.along_second(True))
        self.wait((df, 3, None))
        self.push((df, 3), (df, 2, 1), self.along_second(False))

    def step0(self):
        self.push((0, 0), (1, 0, None), self.along_first(True))
        self.push((0, 0), (3, 0, None), self.along_first(False))
        self.spread(0)

    def step1(self):
        self.wait((1, 0, None))
        self.push((1, 0), (2, 0, 0), self.along_first(True))
        self.spread(1)
        self.wait((3, 0, None))
        self.push((3, 0), (2, 0, 1), self.along_first(False))
        self.spread(3)
        self.relay(0)

    def step2(self):
        self.wait((2, 0, 0), (2, 0, 1))
        self.spread(2)
        self.relay(1)
        self.relay(3)

    def step3(self):
        self.relay(2)

    def step4(self):
        self.wait(*[(df, 2, part) for df in (0, 1, 3, 2) for part in (0, 1)])

    def finish(self):
        for copy in self.sent:
            copy.wait_send()


class Exchange:
    def __init__(self, axis, size, me, block, send, recv):
        self.axis, self.size, self.me, self.block = axis, size, me, block
        self.send, self.recv = send, recv
        self.sent = []

    def copy(self, owner, step, to):
        ref = self.block(owner)
        return pltpu.make_async_remote_copy(
            src_ref=ref,
            dst_ref=ref,
            send_sem=self.send.at[step],
            recv_sem=self.recv.at[step],
            device_id={self.axis: to},
            device_id_type=MESH,
        )

    def start(self):
        for step in range(1, self.size):
            copy = self.copy(self.me, step, lax.rem(self.me + step, self.size))
            copy.start()
            self.sent.append(copy)

    def wait(self):
        for step in range(1, self.size):
            owner = lax.rem(self.me + self.size - step, self.size)
            self.copy(owner, step, owner).wait_recv()

    def finish(self):
        for copy in self.sent:
            copy.wait_send()


def body(
    points_ref,
    right_ref,
    listed_ref,
    count_ref,
    mid_pick_ref,
    top_pick_ref,
    mid_basis_ref,
    top_basis_ref,
    noise_ref,
    solution_ref,
    residual_ref,
    all_points,
    fields0,
    fields1,
    own3,
    coords,
    roots,
    weights,
    tops,
    sums_leaf,
    sums_grp,
    basis,
    basis_high,
    basis_low,
    near_sum,
    image,
    term,
    kept,
    basis_sem,
    points_send,
    points_recv,
    field_send,
    field_recv,
    coords_send,
    coords_recv,
    roots_send,
    roots_recv,
    weights_send,
    weights_recv,
    tops_send,
    tops_recv,
    sums_leaf_send,
    sums_leaf_recv,
    sums_grp_send,
    sums_grp_recv,
):
    me, grp = lax.axis_index("leaf"), lax.axis_index("grp")
    all_fields = (fields0, fields1)

    loads = [
        pltpu.make_async_copy(ref, basis.at[i], basis_sem.at[i])
        for i, ref in enumerate((mid_basis_ref, top_basis_ref))
    ]
    for load in loads:
        load.start()

    barrier = pltpu.get_barrier_semaphore()
    for axis, own, size in (("leaf", me, N_LEAF), ("grp", grp, N_GRP)):
        for step in range(1, size):
            pl.semaphore_signal(
                barrier, inc=1, device_id={axis: lax.rem(own + step, size)}, device_id_type=MESH
            )

    points = points_ref[...]
    right = right_ref[...]
    scale = self_scale(points)
    field = right * scale
    for slot in range(2):
        columns = slice(slot * LEAF, (slot + 1) * LEAF)
        all_points[2 * me + slot] = points[:, columns]
        fields0[2 * me + slot] = field[:, columns]
        own3[slot] = thirds(points[:, columns])

    pl.semaphore_wait(barrier, N_LEAF + N_GRP - 2)

    def gathers(slot_of, part_of, send, recv):
        return [Gather(half, me, slot_of, part_of, send, recv) for half in range(2)]

    point_gathers = gathers(
        lambda leaf: all_points.at[leaf],
        lambda block, part: block.at[pl.ds(16 * part, 16)],
        points_send,
        points_recv,
    )
    field_gathers = [
        gathers(
            lambda leaf, it=it: all_fields[it].at[leaf],
            lambda block, part: block.at[:, pl.ds(512 * part, 512)],
            field_send.at[it],
            field_recv.at[it],
        )
        for it in range(2)
    ]
    first_gathers = [point_gathers[0], point_gathers[1], field_gathers[0][0], field_gathers[0][1]]
    coord_exchange = Exchange(
        "leaf", N_LEAF, me, lambda dev: coords.at[dev], coords_send, coords_recv
    )
    root_exchange = Exchange("grp", N_GRP, grp, lambda g: roots.at[g], roots_send, roots_recv)
    weight_exchange = [
        Exchange(
            "leaf",
            N_LEAF,
            me,
            lambda dev, it=it: weights.at[it, dev],
            weights_send.at[it],
            weights_recv.at[it],
        )
        for it in range(2)
    ]
    top_exchange = [
        Exchange(
            "grp", N_GRP, grp, lambda g, it=it: tops.at[it, g], tops_send.at[it], tops_recv.at[it]
        )
        for it in range(2)
    ]

    def step(gathered, name):
        for gather in gathered:
            getattr(gather, name)()

    def add_block(it, slot, place, rows_of, field16):
        total = None
        for start in range(0, LEAF, CHUNK):
            rows = pl.ds(start, CHUNK)
            if it == 1 and place is not None:
                high, low = kept[place, 0, rows, :], kept[place, 1, rows, :]
            else:
                high, low = kernel_halves(rows_of(rows), own3[slot])
                if place is not None:
                    kept[place, 0, rows, :] = high
                    kept[place, 1, rows, :] = low
            part = applied(field16[:, start : start + CHUNK], high, low)
            total = part if total is None else total + part
        near_sum[slot] += total

    def near_self(it, slot):
        near_sum[slot] = jnp.zeros((2 * TARGETS, LEAF), F32)
        field16 = stacked(all_fields[it][2 * me + slot] * count_ref[slot].astype(F32))
        columns = slot * LEAF
        add_block(
            it,
            slot,
            None,
            lambda rows: points_ref[:, pl.ds(columns + rows.start, CHUNK)],
            field16,
        )

    def near_listed(it, slot, begin, end):
        count = count_ref[slot]

        def run(low_end, high_end, keep):
            def one(k, carried):
                leaf = listed_ref[slot, k]
                active = jnp.where(k < count, 1.0, 0.0).astype(F32)
                field16 = stacked(all_fields[it][leaf] * active)
                place = slot * (SLOTS - 1) + k - 1 if keep else None
                rows_of = lambda rows: all_points[leaf, :, rows]
                add_block(it, slot, place, rows_of, field16)
                return carried

            if low_end < high_end:
                lax.fori_loop(low_end, high_end, one, 0)

        limit = min(max(KEPT - slot * (SLOTS - 1) + 1, 1), SLOTS)
        run(begin, min(end, limit), True)
        run(max(begin, limit), end, False)

    def near(slot):
        return folded(near_sum[slot]) * (scale[:, slot * LEAF : (slot + 1) * LEAF] * LEAF**-0.5)

    def project(value):
        value16 = stacked(value)
        return folded(dot_nt(value16, basis_high[...]) + dot_nt(value16, basis_low[...]))

    def side_by_side(blocks):
        return jnp.concatenate(blocks, axis=1)

    def skeleton_image(coords_of, weights_of, count, columns3):
        total = jnp.zeros((2 * TARGETS, RANK), F32)
        for start in range(0, count, 4):
            rows = side_by_side([coords_of(start + i) for i in range(4)])
            field16 = stacked(side_by_side([weights_of(start + i) for i in range(4)]))
            total = total + applied(field16, *kernel_halves(rows, columns3))
        return folded(total)

    step(first_gathers, "step0")

    def picked(pick, base):
        found = jnp.zeros((FEATURES, RANK), F32)
        for start in range(0, BLOCK, CHUNK):
            rows = lax.broadcasted_iota(jnp.int32, (CHUNK, RANK), 0) + (base + start)
            chosen = jnp.where(rows == pick, 1.0, 0.0).astype(BF16)
            found = found + dot(points[:, start : start + CHUNK], chosen)
        return found.astype(BF16)

    own_mid = picked(mid_pick_ref[...], 0)
    coords[me, 0:FEATURES, :] = own_mid
    coords[me, FEATURES : 2 * FEATURES, :] = picked(top_pick_ref[...], me * BLOCK)
    mid3, mid_scale = thirds(own_mid), self_scale(own_mid)

    step(first_gathers, "step1")
    coord_exchange.start()
    near_self(0, 0)
    step(first_gathers, "step2")

    for load in loads:
        load.wait()
    for i in range(2):
        for start in range(0, RANK, 64):
            high, low = halves(basis[i, start : start + 64, :])
            basis_high[i * RANK + start : i * RANK + start + 64, :] = high
            basis_low[i * RANK + start : i * RANK + start + 64, :] = low

    def send_weights(it, value, sums):
        parts = project(value)
        weights[it, me, 0] = parts[:, :RANK] * mid_scale
        weights[it, me, 1] = parts[:, RANK:]
        weights[it, me, 2] = sums
        weight_exchange[it].start()

    blank = jnp.zeros((TARGETS, RANK), F32)
    send_weights(0, right, blank)
    step(first_gathers, "step3")
    near_self(0, 1)

    coord_exchange.wait()
    own_root = jnp.zeros((FEATURES, RANK), F32)
    for dev in range(N_LEAF):
        own_root = own_root + coords[dev, FEATURES : 2 * FEATURES, :].astype(F32)
    own_root = own_root.astype(BF16)
    roots[grp] = own_root
    root_exchange.start()
    root3, root_scale = thirds(own_root), self_scale(own_root)

    def mid_image(it):
        weight_exchange[it].wait()
        top, sums = weights[it, 0, 1], weights[it, 0, 2]
        for dev in range(1, N_LEAF):
            top = top + weights[it, dev, 1]
            sums = sums + weights[it, dev, 2]
        tops[it, grp, 0] = top * root_scale
        tops[it, grp, 1] = sums
        top_exchange[it].start()
        found = skeleton_image(
            lambda dev: coords[dev, 0:FEATURES, :], lambda dev: weights[it, dev, 0], N_LEAF, mid3
        )
        return found * (mid_scale * RANK**-0.5)

    def expand(it, mid_part):
        top_exchange[it].wait()
        found = skeleton_image(lambda g: roots[g], lambda g: tops[it, g, 0], N_GRP, root3)
        top_part = found * (root_scale * RANK**-0.5)
        image16 = stacked(side_by_side([mid_part, top_part]))
        for start in range(0, BLOCK, CHUNK):
            columns = slice(start, start + CHUNK)
            term[:, columns] = folded(
                applied(image16, basis_high[:, columns], basis_low[:, columns])
            )

    mid_part = mid_image(0)
    step(first_gathers, "step4")
    noise = noise_ref[0]

    def finish_leaf(slot, value):
        columns = slice(slot * LEAF, (slot + 1) * LEAF)
        return noise * value[:, columns] + near(slot) + term[:, columns]

    near_listed(0, 0, 1, SLOTS)
    root_exchange.wait()
    expand(0, mid_part)
    second_gathers = field_gathers[1]

    def send_leaf(slot):
        columns = slice(slot * LEAF, (slot + 1) * LEAF)
        found = finish_leaf(slot, right)
        image[:, columns] = found
        fields1[2 * me + slot] = found * scale[:, columns]
        second_gathers[slot].step0()

    send_leaf(0)
    near_listed(0, 1, 1, 3)
    second_gathers[0].step1()
    near_listed(0, 1, 3, 5)
    second_gathers[0].step2()
    near_listed(0, 1, 5, 7)
    second_gathers[0].step3()
    near_listed(0, 1, 7, 8)
    send_leaf(1)

    lane = lax.broadcasted_iota(jnp.int32, (TARGETS, RANK), 1)

    def summed(value):
        return jnp.sum(value, axis=1, keepdims=True)

    first_image = image[...]
    sums = jnp.where(
        lane == 0,
        summed(right * right),
        jnp.where(lane == 1, summed(right * first_image), summed(first_image * first_image)),
    )
    send_weights(1, first_image, sums)
    second_gathers[1].step1()
    near_self(1, 0)
    second_gathers[1].step2()
    near_self(1, 1)
    second_gathers[1].step3()
    mid_part = mid_image(1)
    step(second_gathers, "step4")
    near_listed(1, 0, 1, SLOTS)
    expand(1, mid_part)
    near_listed(1, 1, 1, SLOTS)

    totals = tops[1, 0, 1]
    for g in range(1, N_GRP):
        totals = totals + tops[1, g, 1]
    norm0, curve0, square0 = totals[:, 0:1], totals[:, 1:2], totals[:, 2:3]
    alpha = norm0 / curve0
    norm1 = norm0 - 2.0 * alpha * curve0 + alpha * alpha * square0
    beta = norm1 / norm0
    second_image = jnp.concatenate(
        [finish_leaf(0, first_image), finish_leaf(1, first_image)], axis=1
    )
    residual = right - alpha * first_image
    direction = residual + beta * right
    image1 = (1.0 + beta) * first_image - alpha * second_image

    sums_leaf[me] = jnp.broadcast_to(summed(direction * image1), (TARGETS, 128))
    leaf_exchange = Exchange(
        "leaf", N_LEAF, me, lambda dev: sums_leaf.at[dev], sums_leaf_send, sums_leaf_recv
    )
    leaf_exchange.start()
    leaf_exchange.wait()
    total = sums_leaf[0]
    for dev in range(1, N_LEAF):
        total = total + sums_leaf[dev]
    sums_grp[grp] = total
    grp_exchange = Exchange(
        "grp", N_GRP, grp, lambda g: sums_grp.at[g], sums_grp_send, sums_grp_recv
    )
    grp_exchange.start()
    grp_exchange.wait()
    total = sums_grp[0]
    for g in range(1, N_GRP):
        total = total + sums_grp[g]
    alpha1 = norm1 / total[:, 0:1]
    solution_ref[...] = alpha * right + alpha1 * direction
    residual_ref[...] = residual - alpha1 * image1

    for sender in (
        *first_gathers,
        *second_gathers,
        coord_exchange,
        root_exchange,
        *weight_exchange,
        *top_exchange,
        leaf_exchange,
        grp_exchange,
    ):
        sender.finish()


def on_device(*operands):
    vmem, smem, anywhere = (
        pl.BlockSpec(memory_space=space) for space in (pltpu.VMEM, pltpu.SMEM, pl.ANY)
    )
    messages = 2 * len(LABELS)
    dma = pltpu.SemaphoreType.DMA
    out = jax.ShapeDtypeStruct((TARGETS, BLOCK), F32)
    return pl.pallas_call(
        body,
        out_shape=(out, out),
        in_specs=[vmem, vmem, smem, smem, vmem, vmem, anywhere, anywhere, smem],
        out_specs=(vmem, vmem),
        scratch_shapes=[
            pltpu.VMEM((2 * N_LEAF, FEATURES, LEAF), BF16),
            pltpu.VMEM((2 * N_LEAF, TARGETS, LEAF), F32),
            pltpu.VMEM((2 * N_LEAF, TARGETS, LEAF), F32),
            pltpu.VMEM((2, 3 * FEATURES, LEAF), BF16),
            pltpu.VMEM((N_LEAF, 2 * FEATURES, RANK), BF16),
            pltpu.VMEM((N_GRP, FEATURES, RANK), BF16),
            pltpu.VMEM((2, N_LEAF, 3, TARGETS, RANK), F32),
            pltpu.VMEM((2, N_GRP, 2, TARGETS, RANK), F32),
            pltpu.VMEM((N_LEAF, TARGETS, 128), F32),
            pltpu.VMEM((N_GRP, TARGETS, 128), F32),
            pltpu.VMEM((2, RANK, BLOCK), F32),
            pltpu.VMEM((2 * RANK, BLOCK), BF16),
            pltpu.VMEM((2 * RANK, BLOCK), BF16),
            pltpu.VMEM((2, 2 * TARGETS, LEAF), F32),
            pltpu.VMEM((TARGETS, BLOCK), F32),
            pltpu.VMEM((TARGETS, BLOCK), F32),
            pltpu.VMEM((KEPT, 2, LEAF, LEAF), BF16),
            dma((2,)),
            dma((messages,)),
            dma((messages,)),
            dma((2, messages)),
            dma((2, messages)),
            dma((N_LEAF,)),
            dma((N_LEAF,)),
            dma((N_GRP,)),
            dma((N_GRP,)),
            dma((2, N_LEAF)),
            dma((2, N_LEAF)),
            dma((2, N_GRP)),
            dma((2, N_GRP)),
            dma((N_LEAF,)),
            dma((N_LEAF,)),
            dma((N_GRP,)),
            dma((N_GRP,)),
        ],
        compiler_params=pltpu.CompilerParams(
            collective_id=0, has_side_effects=True, vmem_limit_bytes=62 * 2**20
        ),
    )(*operands)


def solution(mesh):
    placed = (
        P(None, ("grp", "leaf")),
        P(None, ("grp", "leaf")),
        P(("grp", "leaf"), None),
        P(("grp", "leaf")),
        P(("grp", "leaf"), None),
        P("grp", None),
        P(None, ("grp", "leaf")),
        P(None, ("grp", "leaf")),
        P(),
    )
    return jax.shard_map(
        on_device,
        mesh=mesh,
        in_specs=placed,
        out_specs=(P(None, ("grp", "leaf")), P(None, ("grp", "leaf"))),
        check_vma=False,
    )
```

```python
import math

import jax
import jax.numpy as jnp
from jax import lax
from jax.experimental import pallas as pl
from jax.experimental.pallas import tpu as pltpu
from jax.sharding import PartitionSpec as P

FEATURES = 32
TARGETS = 8
LEAF = 1024
RANK = 256
SLOTS = 8
SIDE = 4
N_LEAF = 16
N_GRP = 8
BLOCK = 2 * LEAF
CHUNK = 512
KEPT = 10
PIECES = ((0, 0, LEAF), (1, 0, LEAF // 2), (1, LEAF // 2, LEAF // 2))
MESH = pl.DeviceIdType.MESH
F32 = jnp.float32
BF16 = jnp.bfloat16
SCALE = math.log2(math.e) / 16.0

LABELS = (
    [(1, 0, None), (3, 0, None), (2, 0, 0), (2, 0, 1)]
    + [(df, ds, None) for df in range(4) for ds in (1, 3)]
    + [(df, 2, part) for df in range(4) for part in (0, 1)]
)
PLACE = {label: i for i, label in enumerate(LABELS)}


def dot(left, right):
    return jnp.dot(left, right, preferred_element_type=F32)


def dot_tn(left, right):
    return lax.dot_general(left, right, (((0,), (0,)), ((), ())), preferred_element_type=F32)


def dot_nt(left, right):
    return lax.dot_general(left, right, (((1,), (1,)), ((), ())), preferred_element_type=F32)


def halves(value):
    high = value.astype(BF16)
    return high, (value - high.astype(F32)).astype(BF16)


def stacked(value):
    high = value.astype(BF16).astype(F32)
    return jnp.concatenate([high, value - high], axis=0).astype(BF16)


def folded(value):
    return value[:TARGETS] + value[TARGETS:]


def thirds(coords):
    scaled = coords.astype(F32) * SCALE
    first = scaled.astype(BF16)
    rest = scaled - first.astype(F32)
    second = rest.astype(BF16)
    third = (rest - second.astype(F32)).astype(BF16)
    return jnp.concatenate([first, second, third], axis=0)


def self_scale(coords):
    wide = coords.astype(F32)
    return jnp.exp2(jnp.sum(wide * wide, axis=0, keepdims=True) * (-0.5 * SCALE))


def kernel_halves(rows, columns3):
    return halves(jnp.exp2(dot_tn(jnp.concatenate([rows, rows, rows], axis=0), columns3)))


def applied(field16, high, low):
    return dot(field16, high) + dot(field16, low)


class Gather:
    def __init__(self, half, me, slot, part, send, recv):
        first, second = lax.div(me, SIDE), lax.rem(me, SIDE)
        if half == 1:
            first, second = second, first
        self.half, self.first, self.second = half, first, second
        self.slot, self.part, self.send, self.recv = slot, part, send, recv
        self.sent = []

    def device(self, df, ds):
        f = lax.rem(self.first + SIDE - df, SIDE)
        s = lax.rem(self.second + SIDE - ds, SIDE)
        return f * SIDE + s if self.half == 0 else s * SIDE + f

    def ref(self, df, ds, part):
        block = self.slot(self.device(df, ds))
        return block if part is None else self.part(block, part)

    def copy(self, mine, label, part, to):
        place = self.half * len(LABELS) + PLACE[label]
        ref = self.ref(mine[0], mine[1], part)
        return pltpu.make_async_remote_copy(
            src_ref=ref,
            dst_ref=ref,
            send_sem=self.send.at[place],
            recv_sem=self.recv.at[place],
            device_id={"leaf": to},
            device_id_type=MESH,
        )

    def push(self, mine, label, to):
        copy = self.copy(mine, label, label[2], to)
        copy.start()
        self.sent.append(copy)

    def wait(self, *labels):
        for label in labels:
            self.copy(label[:2], label, label[2], self.device(1, 0)).wait_recv()

    def along_first(self, ahead):
        return self.device(3 if ahead else 1, 0)

    def along_second(self, ahead):
        return self.device(0, 3 if ahead else 1)

    def spread(self, df):
        self.push((df, 0), (df, 1, None), self.along_second(True))
        self.push((df, 0), (df, 3, None), self.along_second(False))

    def relay(self, df):
        self.wait((df, 1, None))
        self.push((df, 1), (df, 2, 0), self.along_second(True))
        self.wait((df, 3, None))
        self.push((df, 3), (df, 2, 1), self.along_second(False))

    def step0(self):
        self.push((0, 0), (1, 0, None), self.along_first(True))
        self.push((0, 0), (3, 0, None), self.along_first(False))
        self.spread(0)

    def step1(self):
        self.wait((1, 0, None))
        self.push((1, 0), (2, 0, 0), self.along_first(True))
        self.spread(1)
        self.wait((3, 0, None))
        self.push((3, 0), (2, 0, 1), self.along_first(False))
        self.spread(3)
        self.relay(0)

    def step2(self):
        self.wait((2, 0, 0), (2, 0, 1))
        self.spread(2)
        self.relay(1)
        self.relay(3)

    def step3(self):
        self.relay(2)

    def step4(self):
        self.wait(*[(df, 2, part) for df in (0, 1, 3, 2) for part in (0, 1)])

    def finish(self):
        for copy in self.sent:
            copy.wait_send()


class Exchange:
    def __init__(self, axis, size, me, block, send, recv):
        self.axis, self.size, self.me, self.block = axis, size, me, block
        self.send, self.recv = send, recv
        self.sent = []

    def copy(self, owner, step, to):
        ref = self.block(owner)
        return pltpu.make_async_remote_copy(
            src_ref=ref,
            dst_ref=ref,
            send_sem=self.send.at[step],
            recv_sem=self.recv.at[step],
            device_id={self.axis: to},
            device_id_type=MESH,
        )

    def start(self):
        for step in range(1, self.size):
            copy = self.copy(self.me, step, lax.rem(self.me + step, self.size))
            copy.start()
            self.sent.append(copy)

    def wait(self):
        for step in range(1, self.size):
            owner = lax.rem(self.me + self.size - step, self.size)
            self.copy(owner, step, owner).wait_recv()

    def finish(self):
        for copy in self.sent:
            copy.wait_send()


def body(
    points_ref,
    right_ref,
    listed_ref,
    count_ref,
    mid_pick_ref,
    top_pick_ref,
    mid_basis_ref,
    top_basis_ref,
    noise_ref,
    solution_ref,
    residual_ref,
    all_points,
    fields0,
    fields1,
    own3,
    mid_coords,
    top_coords,
    roots,
    weights,
    tops,
    sums_leaf,
    sums_grp,
    basis,
    basis_high,
    basis_low,
    near_sum,
    image,
    term,
    kept,
    basis_sem,
    points_send,
    points_recv,
    field_send,
    field_recv,
    image_send,
    image_recv,
    coords_send,
    coords_recv,
    roots_send,
    roots_recv,
    weights_send,
    weights_recv,
    tops_send,
    tops_recv,
    sums_leaf_send,
    sums_leaf_recv,
    sums_grp_send,
    sums_grp_recv,
):
    me, grp = lax.axis_index("leaf"), lax.axis_index("grp")
    all_fields = (fields0, fields1)

    loads = [
        pltpu.make_async_copy(ref, basis.at[i], basis_sem.at[i])
        for i, ref in enumerate((mid_basis_ref, top_basis_ref))
    ]
    for load in loads:
        load.start()

    barrier = pltpu.get_barrier_semaphore()
    for axis, own, size in (("leaf", me, N_LEAF), ("grp", grp, N_GRP)):
        for step in range(1, size):
            pl.semaphore_signal(
                barrier, inc=1, device_id={axis: lax.rem(own + step, size)}, device_id_type=MESH
            )

    points = points_ref[...]
    right = right_ref[...]
    scale = self_scale(points)
    field = right * scale
    for slot in range(2):
        columns = slice(slot * LEAF, (slot + 1) * LEAF)
        all_points[2 * me + slot] = points[:, columns]
        fields0[2 * me + slot] = field[:, columns]
        own3[slot] = thirds(points[:, columns])

    pl.semaphore_wait(barrier, N_LEAF + N_GRP - 2)

    def gathers(slot_of, part_of, send, recv):
        return [
            Gather(half, me, lambda dev, half=half: slot_of(half, dev), part_of, send, recv)
            for half in range(2)
        ]

    point_gathers = gathers(
        lambda half, dev: all_points.at[2 * dev + half],
        lambda block, part: block.at[pl.ds(16 * part, 16)],
        points_send,
        points_recv,
    )
    first_field_gathers = gathers(
        lambda half, dev: fields0.at[2 * dev + half],
        lambda block, part: block.at[:, pl.ds(512 * part, 512)],
        field_send,
        field_recv,
    )
    coord_gathers = gathers(
        lambda half, dev: (mid_coords, top_coords)[half].at[dev],
        lambda block, part: block.at[pl.ds(16 * part, 16)],
        coords_send,
        coords_recv,
    )
    first_gathers = [*point_gathers, *first_field_gathers]
    image_exchange = [
        Exchange(
            "leaf",
            N_LEAF,
            me,
            lambda dev, piece=piece: fields1.at[2 * dev + piece[0], :, pl.ds(piece[1], piece[2])],
            image_send.at[i],
            image_recv.at[i],
        )
        for i, piece in enumerate(PIECES)
    ]
    root_exchange = Exchange("grp", N_GRP, grp, lambda g: roots.at[g], roots_send, roots_recv)
    weight_exchange = [
        Exchange(
            "leaf",
            N_LEAF,
            me,
            lambda dev, it=it: weights.at[it, dev, pl.ds(0, 2 + it)],
            weights_send.at[it],
            weights_recv.at[it],
        )
        for it in range(2)
    ]
    top_exchange = [
        Exchange(
            "grp",
            N_GRP,
            grp,
            lambda g, it=it: tops.at[it, g, pl.ds(0, 1 + it)],
            tops_send.at[it],
            tops_recv.at[it],
        )
        for it in range(2)
    ]

    def step(gathered, name):
        for gather in gathered:
            getattr(gather, name)()

    def add_block(it, slot, place, rows_of, field16, start, width):
        columns = pl.ds(start, width)
        height = CHUNK * LEAF // width
        total = None
        for first in range(0, LEAF, height):
            rows = pl.ds(first, height)
            if it == 1 and place is not None:
                high, low = kept[place, 0, rows, columns], kept[place, 1, rows, columns]
            else:
                high, low = kernel_halves(rows_of(rows), own3[slot, :, columns])
                if place is not None:
                    kept[place, 0, rows, columns] = high
                    kept[place, 1, rows, columns] = low
            part = applied(field16[:, first : first + height], high, low)
            total = part if total is None else total + part
        near_sum[slot, :, columns] += total

    def near_self(it, slot):
        near_sum[slot] = jnp.zeros((2 * TARGETS, LEAF), F32)
        field16 = stacked(all_fields[it][2 * me + slot] * count_ref[slot].astype(F32))
        base = slot * LEAF
        rows_of = lambda rows: points_ref[:, pl.ds(base + rows.start, rows.size)]
        add_block(it, slot, None, rows_of, field16, 0, LEAF)

    def near_listed(it, slot, begin=1, end=SLOTS, start=0, width=LEAF):
        count = count_ref[slot]

        def run(low_end, high_end, keep):
            def one(k, carried):
                leaf = listed_ref[slot, k]
                active = jnp.where(k < count, 1.0, 0.0).astype(F32)
                field16 = stacked(all_fields[it][leaf] * active)
                place = slot * (SLOTS - 1) + k - 1 if keep else None
                rows_of = lambda rows: all_points[leaf, :, rows]
                add_block(it, slot, place, rows_of, field16, start, width)
                return carried

            if low_end < high_end:
                lax.fori_loop(low_end, high_end, one, 0)

        limit = min(max(KEPT - slot * (SLOTS - 1) + 1, 1), SLOTS)
        run(begin, min(end, limit), True)
        run(max(begin, limit), end, False)

    def near(slot, start, width):
        columns = pl.ds(start, width)
        base = slot * LEAF + start
        return folded(near_sum[slot, :, columns]) * (scale[:, base : base + width] * LEAF**-0.5)

    def project(value):
        value16 = stacked(value)
        return folded(dot_nt(value16, basis_high[...]) + dot_nt(value16, basis_low[...]))

    def side_by_side(blocks):
        return jnp.concatenate(blocks, axis=1)

    def skeleton_image(coords_of, weights_of, count, columns3):
        total = jnp.zeros((2 * TARGETS, RANK), F32)
        for start in range(0, count, 4):
            rows = side_by_side([coords_of(start + i) for i in range(4)])
            field16 = stacked(side_by_side([weights_of(start + i) for i in range(4)]))
            total = total + applied(field16, *kernel_halves(rows, columns3))
        return folded(total)

    step(first_gathers, "step0")

    def picked(pick, base):
        found = jnp.zeros((FEATURES, RANK), F32)
        for start in range(0, BLOCK, CHUNK):
            rows = lax.broadcasted_iota(jnp.int32, (CHUNK, RANK), 0) + (base + start)
            chosen = jnp.where(rows == pick, 1.0, 0.0).astype(BF16)
            found = found + dot(points[:, start : start + CHUNK], chosen)
        return found.astype(BF16)

    own_mid = picked(mid_pick_ref[...], 0)
    mid_coords[me] = own_mid
    top_coords[me] = picked(top_pick_ref[...], me * BLOCK)
    mid3, mid_scale = thirds(own_mid), self_scale(own_mid)

    step(coord_gathers, "step0")
    step(first_gathers, "step1")
    near_self(0, 0)
    step(first_gathers, "step2")
    step(coord_gathers, "step1")

    for load in loads:
        load.wait()
    for i in range(2):
        for start in range(0, RANK, 64):
            high, low = halves(basis[i, start : start + 64, :])
            basis_high[i * RANK + start : i * RANK + start + 64, :] = high
            basis_low[i * RANK + start : i * RANK + start + 64, :] = low

    def send_weights(it, value, sums):
        parts = project(value)
        weights[it, me, 0] = parts[:, :RANK] * mid_scale
        weights[it, me, 1] = parts[:, RANK:]
        if sums is not None:
            weights[it, me, 2] = sums
        weight_exchange[it].start()

    step(first_gathers, "step3")
    near_self(0, 1)
    step(coord_gathers, "step2")
    send_weights(0, right, None)
    step(coord_gathers, "step3")
    step(first_gathers, "step4")

    def mid_image(it):
        weight_exchange[it].wait()
        top = weights[it, 0, 1]
        for dev in range(1, N_LEAF):
            top = top + weights[it, dev, 1]
        tops[it, grp, 0] = top * root_scale
        if it == 1:
            sums = weights[it, 0, 2]
            for dev in range(1, N_LEAF):
                sums = sums + weights[it, dev, 2]
            tops[it, grp, 1] = sums
        top_exchange[it].start()
        found = skeleton_image(
            lambda dev: mid_coords[dev], lambda dev: weights[it, dev, 0], N_LEAF, mid3
        )
        return found * (mid_scale * RANK**-0.5)

    def expand(it, mid_part):
        top_exchange[it].wait()
        found = skeleton_image(lambda g: roots[g], lambda g: tops[it, g, 0], N_GRP, root3)
        top_part = found * (root_scale * RANK**-0.5)
        image16 = stacked(side_by_side([mid_part, top_part]))
        for start in range(0, BLOCK, CHUNK):
            columns = slice(start, start + CHUNK)
            term[:, columns] = folded(
                applied(image16, basis_high[:, columns], basis_low[:, columns])
            )

    noise = noise_ref[0]

    def finished(value, slot, start, width):
        base = slot * LEAF + start
        columns = slice(base, base + width)
        return noise * value[:, columns] + near(slot, start, width) + term[:, columns]

    near_listed(0, 0, 1, 4)
    step(coord_gathers, "step4")
    own_root = jnp.zeros((FEATURES, RANK), F32)
    for dev in range(N_LEAF):
        own_root = own_root + top_coords[dev].astype(F32)
    own_root = own_root.astype(BF16)
    roots[grp] = own_root
    root_exchange.start()
    root3, root_scale = thirds(own_root), self_scale(own_root)
    mid_part = mid_image(0)
    near_listed(0, 0, 4, 8)
    root_exchange.wait()
    expand(0, mid_part)

    for exchange, (slot, start, width) in zip(image_exchange, PIECES, strict=True):
        if slot == 1:
            near_listed(0, slot, start=start, width=width)
        found = finished(right, slot, start, width)
        base = slot * LEAF + start
        image[:, base : base + width] = found
        fields1[2 * me + slot, :, start : start + width] = found * scale[:, base : base + width]
        exchange.start()

    lane = lax.broadcasted_iota(jnp.int32, (TARGETS, RANK), 1)

    def summed(value):
        return jnp.sum(value, axis=1, keepdims=True)

    first_image = image[...]
    sums = jnp.where(
        lane == 0,
        summed(right * right),
        jnp.where(lane == 1, summed(right * first_image), summed(first_image * first_image)),
    )
    send_weights(1, first_image, sums)
    near_self(1, 0)
    near_self(1, 1)
    for exchange in image_exchange:
        exchange.wait()
    near_listed(1, 0)
    mid_part = mid_image(1)
    near_listed(1, 1)
    expand(1, mid_part)

    totals = tops[1, 0, 1]
    for g in range(1, N_GRP):
        totals = totals + tops[1, g, 1]
    norm0, curve0, square0 = totals[:, 0:1], totals[:, 1:2], totals[:, 2:3]
    alpha = norm0 / curve0
    norm1 = norm0 - 2.0 * alpha * curve0 + alpha * alpha * square0
    beta = norm1 / norm0
    second_image = jnp.concatenate(
        [finished(first_image, slot, 0, LEAF) for slot in range(2)], axis=1
    )
    residual = right - alpha * first_image
    direction = residual + beta * right
    image1 = (1.0 + beta) * first_image - alpha * second_image

    sums_leaf[me] = jnp.broadcast_to(summed(direction * image1), (TARGETS, 128))
    leaf_exchange = Exchange(
        "leaf", N_LEAF, me, lambda dev: sums_leaf.at[dev], sums_leaf_send, sums_leaf_recv
    )
    leaf_exchange.start()
    leaf_exchange.wait()
    total = sums_leaf[0]
    for dev in range(1, N_LEAF):
        total = total + sums_leaf[dev]
    sums_grp[grp] = total
    grp_exchange = Exchange(
        "grp", N_GRP, grp, lambda g: sums_grp.at[g], sums_grp_send, sums_grp_recv
    )
    grp_exchange.start()
    grp_exchange.wait()
    total = sums_grp[0]
    for g in range(1, N_GRP):
        total = total + sums_grp[g]
    alpha1 = norm1 / total[:, 0:1]
    solution_ref[...] = alpha * right + alpha1 * direction
    residual_ref[...] = residual - alpha1 * image1

    for sender in (
        *first_gathers,
        *coord_gathers,
        *image_exchange,
        root_exchange,
        *weight_exchange,
        *top_exchange,
        leaf_exchange,
        grp_exchange,
    ):
        sender.finish()


def on_device(*operands):
    vmem, smem, anywhere = (
        pl.BlockSpec(memory_space=space) for space in (pltpu.VMEM, pltpu.SMEM, pl.ANY)
    )
    messages = 2 * len(LABELS)
    dma = pltpu.SemaphoreType.DMA
    out = jax.ShapeDtypeStruct((TARGETS, BLOCK), F32)
    return pl.pallas_call(
        body,
        out_shape=(out, out),
        in_specs=[vmem, vmem, smem, smem, vmem, vmem, anywhere, anywhere, smem],
        out_specs=(vmem, vmem),
        scratch_shapes=[
            pltpu.VMEM((2 * N_LEAF, FEATURES, LEAF), BF16),
            pltpu.VMEM((2 * N_LEAF, TARGETS, LEAF), F32),
            pltpu.VMEM((2 * N_LEAF, TARGETS, LEAF), F32),
            pltpu.VMEM((2, 3 * FEATURES, LEAF), BF16),
            pltpu.VMEM((N_LEAF, FEATURES, RANK), BF16),
            pltpu.VMEM((N_LEAF, FEATURES, RANK), BF16),
            pltpu.VMEM((N_GRP, FEATURES, RANK), BF16),
            pltpu.VMEM((2, N_LEAF, 3, TARGETS, RANK), F32),
            pltpu.VMEM((2, N_GRP, 2, TARGETS, RANK), F32),
            pltpu.VMEM((N_LEAF, TARGETS, 128), F32),
            pltpu.VMEM((N_GRP, TARGETS, 128), F32),
            pltpu.VMEM((2, RANK, BLOCK), F32),
            pltpu.VMEM((2 * RANK, BLOCK), BF16),
            pltpu.VMEM((2 * RANK, BLOCK), BF16),
            pltpu.VMEM((2, 2 * TARGETS, LEAF), F32),
            pltpu.VMEM((TARGETS, BLOCK), F32),
            pltpu.VMEM((TARGETS, BLOCK), F32),
            pltpu.VMEM((KEPT, 2, LEAF, LEAF), BF16),
            dma((2,)),
            dma((messages,)),
            dma((messages,)),
            dma((messages,)),
            dma((messages,)),
            dma((len(PIECES), N_LEAF)),
            dma((len(PIECES), N_LEAF)),
            dma((messages,)),
            dma((messages,)),
            dma((N_GRP,)),
            dma((N_GRP,)),
            dma((2, N_LEAF)),
            dma((2, N_LEAF)),
            dma((2, N_GRP)),
            dma((2, N_GRP)),
            dma((N_LEAF,)),
            dma((N_LEAF,)),
            dma((N_GRP,)),
            dma((N_GRP,)),
        ],
        compiler_params=pltpu.CompilerParams(
            collective_id=0, has_side_effects=True, vmem_limit_bytes=62 * 2**20
        ),
    )(*operands)


def solution(mesh):
    placed = (
        P(None, ("grp", "leaf")),
        P(None, ("grp", "leaf")),
        P(("grp", "leaf"), None),
        P(("grp", "leaf")),
        P(("grp", "leaf"), None),
        P("grp", None),
        P(None, ("grp", "leaf")),
        P(None, ("grp", "leaf")),
        P(),
    )
    return jax.shard_map(
        on_device,
        mesh=mesh,
        in_specs=placed,
        out_specs=(P(None, ("grp", "leaf")), P(None, ("grp", "leaf"))),
        check_vma=False,
    )
```

```python
import math

import jax
import jax.numpy as jnp
from jax import lax
from jax.experimental import pallas as pl
from jax.experimental.pallas import tpu as pltpu
from jax.sharding import PartitionSpec as P

FEATURES = 32
TARGETS = 8
LEAF = 1024
RANK = 256
SLOTS = 8
SIDE = 4
N_LEAF = 16
N_GRP = 8
BLOCK = 2 * LEAF
CHUNK = 512
KEPT = 10
PIECES = ((0, 0, LEAF), (1, 0, LEAF // 2), (1, LEAF // 2, LEAF // 2))
MESH = pl.DeviceIdType.MESH
F32 = jnp.float32
BF16 = jnp.bfloat16
SCALE = math.log2(math.e) / 16.0

LABELS = (
    [(1, 0, None), (3, 0, None), (2, 0, 0), (2, 0, 1)]
    + [(df, ds, None) for df in range(4) for ds in (1, 3)]
    + [(df, 2, part) for df in range(4) for part in (0, 1)]
)
PLACE = {label: i for i, label in enumerate(LABELS)}


def dot(left, right):
    return jnp.dot(left, right, preferred_element_type=F32)


def dot_tn(left, right):
    return lax.dot_general(left, right, (((0,), (0,)), ((), ())), preferred_element_type=F32)


def dot_nt(left, right):
    return lax.dot_general(left, right, (((1,), (1,)), ((), ())), preferred_element_type=F32)


def halves(value):
    high = value.astype(BF16)
    return high, (value - high.astype(F32)).astype(BF16)


def stacked(value):
    high = value.astype(BF16).astype(F32)
    return jnp.concatenate([high, value - high], axis=0).astype(BF16)


def folded(value):
    return value[:TARGETS] + value[TARGETS:]


def thirds(coords):
    scaled = coords.astype(F32) * SCALE
    first = scaled.astype(BF16)
    rest = scaled - first.astype(F32)
    second = rest.astype(BF16)
    third = (rest - second.astype(F32)).astype(BF16)
    return jnp.concatenate([first, second, third], axis=0)


def self_scale(coords):
    wide = coords.astype(F32)
    return jnp.exp2(jnp.sum(wide * wide, axis=0, keepdims=True) * (-0.5 * SCALE))


def kernel_halves(rows, columns3):
    return halves(jnp.exp2(dot_tn(jnp.concatenate([rows, rows, rows], axis=0), columns3)))


def applied(field16, high, low):
    return dot(field16, high) + dot(field16, low)


class Gather:
    def __init__(self, half, me, slot, part, send, recv):
        first, second = lax.div(me, SIDE), lax.rem(me, SIDE)
        if half == 1:
            first, second = second, first
        self.half, self.first, self.second = half, first, second
        self.slot, self.part, self.send, self.recv = slot, part, send, recv
        self.sent = []

    def device(self, df, ds):
        f = lax.rem(self.first + SIDE - df, SIDE)
        s = lax.rem(self.second + SIDE - ds, SIDE)
        return f * SIDE + s if self.half == 0 else s * SIDE + f

    def ref(self, df, ds, part):
        block = self.slot(self.device(df, ds))
        return block if part is None else self.part(block, part)

    def copy(self, mine, label, part, to):
        place = self.half * len(LABELS) + PLACE[label]
        ref = self.ref(mine[0], mine[1], part)
        return pltpu.make_async_remote_copy(
            src_ref=ref,
            dst_ref=ref,
            send_sem=self.send.at[place],
            recv_sem=self.recv.at[place],
            device_id={"leaf": to},
            device_id_type=MESH,
        )

    def push(self, mine, label, to):
        copy = self.copy(mine, label, label[2], to)
        copy.start()
        self.sent.append(copy)

    def wait(self, *labels):
        for label in labels:
            self.copy(label[:2], label, label[2], self.device(1, 0)).wait_recv()

    def along_first(self, ahead):
        return self.device(3 if ahead else 1, 0)

    def along_second(self, ahead):
        return self.device(0, 3 if ahead else 1)

    def spread(self, df):
        self.push((df, 0), (df, 1, None), self.along_second(True))
        self.push((df, 0), (df, 3, None), self.along_second(False))

    def relay(self, df):
        self.wait((df, 1, None))
        self.push((df, 1), (df, 2, 0), self.along_second(True))
        self.wait((df, 3, None))
        self.push((df, 3), (df, 2, 1), self.along_second(False))

    def own_first(self):
        self.push((0, 0), (1, 0, None), self.along_first(True))
        self.push((0, 0), (3, 0, None), self.along_first(False))

    def own_second(self):
        self.spread(0)

    def relay_first(self):
        self.wait((1, 0, None))
        self.push((1, 0), (2, 0, 0), self.along_first(True))
        self.wait((3, 0, None))
        self.push((3, 0), (2, 0, 1), self.along_first(False))

    def spread_near(self):
        self.spread(1)
        self.spread(3)

    def spread_far(self):
        self.wait((2, 0, 0), (2, 0, 1))
        self.spread(2)

    def relay_own(self):
        self.relay(0)

    def relay_near(self):
        self.relay(1)
        self.relay(3)

    def relay_far(self):
        self.relay(2)

    def arrive(self):
        self.wait(*[(df, 2, part) for df in (0, 1, 3, 2) for part in (0, 1)])

    def finish(self):
        for copy in self.sent:
            copy.wait_send()


class Exchange:
    def __init__(self, axis, size, me, block, send, recv):
        self.axis, self.size, self.me, self.block = axis, size, me, block
        self.send, self.recv = send, recv
        self.sent = []

    def copy(self, owner, step, to):
        ref = self.block(owner)
        return pltpu.make_async_remote_copy(
            src_ref=ref,
            dst_ref=ref,
            send_sem=self.send.at[step],
            recv_sem=self.recv.at[step],
            device_id={self.axis: to},
            device_id_type=MESH,
        )

    def start(self):
        for step in range(1, self.size):
            copy = self.copy(self.me, step, lax.rem(self.me + step, self.size))
            copy.start()
            self.sent.append(copy)

    def wait(self):
        for step in range(1, self.size):
            owner = lax.rem(self.me + self.size - step, self.size)
            self.copy(owner, step, owner).wait_recv()

    def finish(self):
        for copy in self.sent:
            copy.wait_send()


def body(
    points_ref,
    right_ref,
    listed_ref,
    count_ref,
    mid_pick_ref,
    top_pick_ref,
    mid_basis_ref,
    top_basis_ref,
    noise_ref,
    solution_ref,
    residual_ref,
    direction_ref,
    image_ref,
    step_ref,
    all_points,
    fields0,
    fields1,
    own3,
    mid_coords,
    top_coords,
    roots,
    weights,
    tops,
    sums_leaf,
    sums_grp,
    basis,
    basis_high,
    basis_low,
    near_sum,
    image,
    term,
    kept,
    basis_sem,
    points_send,
    points_recv,
    field_send,
    field_recv,
    image_send,
    image_recv,
    coords_send,
    coords_recv,
    roots_send,
    roots_recv,
    weights_send,
    weights_recv,
    tops_send,
    tops_recv,
    sums_leaf_send,
    sums_leaf_recv,
    sums_grp_send,
    sums_grp_recv,
):
    me, grp = lax.axis_index("leaf"), lax.axis_index("grp")
    all_fields = (fields0, fields1)

    loads = [
        pltpu.make_async_copy(ref, basis.at[i], basis_sem.at[i])
        for i, ref in enumerate((mid_basis_ref, top_basis_ref))
    ]
    for load in loads:
        load.start()

    barrier = pltpu.get_barrier_semaphore()
    x, z = lax.div(me, SIDE), lax.rem(me, SIDE)
    beside = [{"leaf": lax.rem(x + step, SIDE) * SIDE + z} for step in (1, 3)]
    beside += [{"leaf": x * SIDE + lax.rem(z + step, SIDE)} for step in (1, 3)]
    beside += [{"grp": lax.rem(grp + step, N_GRP)} for step in range(1, N_GRP)]
    for device in beside:
        pl.semaphore_signal(barrier, inc=1, device_id=device, device_id_type=MESH)

    points = points_ref[...]
    right = right_ref[...]
    scale = self_scale(points)
    field = right * scale
    for slot in range(2):
        columns = slice(slot * LEAF, (slot + 1) * LEAF)
        all_points[2 * me + slot] = points[:, columns]
        fields0[2 * me + slot] = field[:, columns]
        own3[slot] = thirds(points[:, columns])

    pl.semaphore_wait(barrier, len(beside))

    def gathers(slot_of, part_of, send, recv):
        return [
            Gather(half, me, lambda dev, half=half: slot_of(half, dev), part_of, send, recv)
            for half in range(2)
        ]

    point_gathers = gathers(
        lambda half, dev: all_points.at[2 * dev + half],
        lambda block, part: block.at[pl.ds(16 * part, 16)],
        points_send,
        points_recv,
    )
    first_field_gathers = gathers(
        lambda half, dev: fields0.at[2 * dev + half],
        lambda block, part: block.at[:, pl.ds(512 * part, 512)],
        field_send,
        field_recv,
    )
    coord_gathers = gathers(
        lambda half, dev: (mid_coords, top_coords)[half].at[dev],
        lambda block, part: block.at[pl.ds(16 * part, 16)],
        coords_send,
        coords_recv,
    )
    first_gathers = [*point_gathers, *first_field_gathers]
    image_exchange = [
        Exchange(
            "leaf",
            N_LEAF,
            me,
            lambda dev, piece=piece: fields1.at[2 * dev + piece[0], :, pl.ds(piece[1], piece[2])],
            image_send.at[i],
            image_recv.at[i],
        )
        for i, piece in enumerate(PIECES)
    ]
    root_exchange = Exchange("grp", N_GRP, grp, lambda g: roots.at[g], roots_send, roots_recv)
    weight_exchange = [
        Exchange(
            "leaf",
            N_LEAF,
            me,
            lambda dev, it=it: weights.at[it, dev, pl.ds(0, 2 + it)],
            weights_send.at[it],
            weights_recv.at[it],
        )
        for it in range(2)
    ]
    top_exchange = [
        Exchange(
            "grp",
            N_GRP,
            grp,
            lambda g, it=it: tops.at[it, g, pl.ds(0, 1 + it)],
            tops_send.at[it],
            tops_recv.at[it],
        )
        for it in range(2)
    ]

    def step(gathered, *names):
        for name in names:
            for gather in gathered:
                getattr(gather, name)()

    def make_block(place, rows_of, slot):
        for first in range(0, LEAF, CHUNK):
            rows = pl.ds(first, CHUNK)
            high, low = kernel_halves(rows_of(rows), own3[slot])
            kept[place, 0, rows, :] = high
            kept[place, 1, rows, :] = low

    def add_block(ready, slot, place, rows_of, field16, start, width):
        columns = pl.ds(start, width)
        height = CHUNK * LEAF // width
        total = None
        for first in range(0, LEAF, height):
            rows = pl.ds(first, height)
            if ready and place is not None:
                high, low = kept[place, 0, rows, columns], kept[place, 1, rows, columns]
            else:
                high, low = kernel_halves(rows_of(rows), own3[slot, :, columns])
                if place is not None:
                    kept[place, 0, rows, columns] = high
                    kept[place, 1, rows, columns] = low
            part = applied(field16[:, first : first + height], high, low)
            total = part if total is None else total + part
        near_sum[slot, :, columns] += total

    def near_self(it, slot):
        near_sum[slot] = jnp.zeros((2 * TARGETS, LEAF), F32)
        field16 = stacked(all_fields[it][2 * me + slot] * count_ref[slot].astype(F32))
        base = slot * LEAF
        rows_of = lambda rows: points_ref[:, pl.ds(base + rows.start, rows.size)]
        add_block(False, slot, None, rows_of, field16, 0, LEAF)

    def near_listed(it, slot, begin=1, end=SLOTS, start=0, width=LEAF, ready=True):
        count = count_ref[slot]

        def run(low_end, high_end, keep):
            def one(k, carried):
                leaf = listed_ref[slot, k]
                active = jnp.where(k < count, 1.0, 0.0).astype(F32)
                field16 = stacked(all_fields[it][leaf] * active)
                place = slot * (SLOTS - 1) + k - 1 if keep else None
                rows_of = lambda rows: all_points[leaf, :, rows]
                add_block(ready, slot, place, rows_of, field16, start, width)
                return carried

            if low_end < high_end:
                lax.fori_loop(low_end, high_end, one, 0)

        limit = min(max(KEPT - slot * (SLOTS - 1) + 1, 1), SLOTS)
        run(begin, min(end, limit), True)
        run(max(begin, limit), end, False)

    def make_listed(slot):
        def one(k, carried):
            leaf = listed_ref[slot, k]
            make_block(slot * (SLOTS - 1) + k - 1, lambda rows: all_points[leaf, :, rows], slot)
            return carried

        lax.fori_loop(1, SLOTS, one, 0)

    def near(slot, start, width):
        columns = pl.ds(start, width)
        base = slot * LEAF + start
        return folded(near_sum[slot, :, columns]) * (scale[:, base : base + width] * LEAF**-0.5)

    def project(value):
        value16 = stacked(value)
        return folded(dot_nt(value16, basis_high[...]) + dot_nt(value16, basis_low[...]))

    def side_by_side(blocks):
        return jnp.concatenate(blocks, axis=1)

    def skeleton_image(coords_of, weights_of, count, columns3):
        total = jnp.zeros((2 * TARGETS, RANK), F32)
        for start in range(0, count, 4):
            rows = side_by_side([coords_of(start + i) for i in range(4)])
            field16 = stacked(side_by_side([weights_of(start + i) for i in range(4)]))
            total = total + applied(field16, *kernel_halves(rows, columns3))
        return folded(total)

    step(first_gathers, "own_first", "own_second")

    def picked(pick, base):
        found = jnp.zeros((FEATURES, RANK), F32)
        for start in range(0, BLOCK, CHUNK):
            rows = lax.broadcasted_iota(jnp.int32, (CHUNK, RANK), 0) + (base + start)
            chosen = jnp.where(rows == pick, 1.0, 0.0).astype(BF16)
            found = found + dot(points[:, start : start + CHUNK], chosen)
        return found.astype(BF16)

    own_mid = picked(mid_pick_ref[...], 0)
    mid_coords[me] = own_mid
    top_coords[me] = picked(top_pick_ref[...], me * BLOCK)
    mid3, mid_scale = thirds(own_mid), self_scale(own_mid)

    step(first_gathers, "relay_first", "spread_near")
    step(coord_gathers, "own_first", "own_second")
    near_self(0, 0)
    step(first_gathers, "spread_far", "relay_own", "relay_near")

    for load in loads:
        load.wait()
    for i in range(2):
        for start in range(0, RANK, 64):
            high, low = halves(basis[i, start : start + 64, :])
            basis_high[i * RANK + start : i * RANK + start + 64, :] = high
            basis_low[i * RANK + start : i * RANK + start + 64, :] = low

    def send_weights(it, value, sums):
        parts = project(value)
        weights[it, me, 0] = parts[:, :RANK] * mid_scale
        weights[it, me, 1] = parts[:, RANK:]
        if sums is not None:
            weights[it, me, 2] = sums
        weight_exchange[it].start()

    step(first_gathers, "relay_far")
    step(coord_gathers, "relay_first", "spread_near")
    near_self(0, 1)
    step(point_gathers, "arrive")
    send_weights(0, right, None)
    step(coord_gathers, "spread_far", "relay_own", "relay_near")
    make_listed(0)
    step(first_field_gathers, "arrive")
    step(coord_gathers, "relay_far")

    def mid_image(it):
        weight_exchange[it].wait()
        top = weights[it, 0, 1]
        for dev in range(1, N_LEAF):
            top = top + weights[it, dev, 1]
        tops[it, grp, 0] = top * root_scale
        if it == 1:
            sums = weights[it, 0, 2]
            for dev in range(1, N_LEAF):
                sums = sums + weights[it, dev, 2]
            tops[it, grp, 1] = sums
        top_exchange[it].start()
        found = skeleton_image(
            lambda dev: mid_coords[dev], lambda dev: weights[it, dev, 0], N_LEAF, mid3
        )
        return found * (mid_scale * RANK**-0.5)

    def expand(it, mid_part):
        top_exchange[it].wait()
        found = skeleton_image(lambda g: roots[g], lambda g: tops[it, g, 0], N_GRP, root3)
        top_part = found * (root_scale * RANK**-0.5)
        image16 = stacked(side_by_side([mid_part, top_part]))
        for start in range(0, BLOCK, CHUNK):
            columns = slice(start, start + CHUNK)
            term[:, columns] = folded(
                applied(image16, basis_high[:, columns], basis_low[:, columns])
            )

    noise = noise_ref[0]

    def finished(value, slot, start, width):
        base = slot * LEAF + start
        columns = slice(base, base + width)
        return noise * value[:, columns] + near(slot, start, width) + term[:, columns]

    near_listed(0, 0, 1, 4)
    step(coord_gathers, "arrive")
    own_root = jnp.zeros((FEATURES, RANK), F32)
    for dev in range(N_LEAF):
        own_root = own_root + top_coords[dev].astype(F32)
    own_root = own_root.astype(BF16)
    roots[grp] = own_root
    root_exchange.start()
    root3, root_scale = thirds(own_root), self_scale(own_root)
    mid_part = mid_image(0)
    near_listed(0, 0, 4, 8)
    root_exchange.wait()
    expand(0, mid_part)

    for exchange, (slot, start, width) in zip(image_exchange, PIECES, strict=True):
        if slot == 1:
            near_listed(0, slot, start=start, width=width, ready=False)
        found = finished(right, slot, start, width)
        base = slot * LEAF + start
        image[:, base : base + width] = found
        fields1[2 * me + slot, :, start : start + width] = found * scale[:, base : base + width]
        exchange.start()

    lane = lax.broadcasted_iota(jnp.int32, (TARGETS, RANK), 1)

    def summed(value):
        return jnp.sum(value, axis=1, keepdims=True)

    first_image = image[...]
    sums = jnp.where(
        lane == 0,
        summed(right * right),
        jnp.where(lane == 1, summed(right * first_image), summed(first_image * first_image)),
    )
    send_weights(1, first_image, sums)
    near_self(1, 0)
    near_self(1, 1)
    for exchange in image_exchange:
        exchange.wait()
    near_listed(1, 0)
    mid_part = mid_image(1)
    near_listed(1, 1)
    expand(1, mid_part)

    totals = tops[1, 0, 1]
    for g in range(1, N_GRP):
        totals = totals + tops[1, g, 1]
    norm0, curve0, square0 = totals[:, 0:1], totals[:, 1:2], totals[:, 2:3]
    alpha = norm0 / curve0
    norm1 = norm0 - 2.0 * alpha * curve0 + alpha * alpha * square0
    beta = norm1 / norm0
    second_image = jnp.concatenate(
        [finished(first_image, slot, 0, LEAF) for slot in range(2)], axis=1
    )
    residual = right - alpha * first_image
    direction = residual + beta * right
    image1 = (1.0 + beta) * first_image - alpha * second_image
    solution_ref[...] = alpha * right
    residual_ref[...] = residual
    direction_ref[...] = direction
    image_ref[...] = image1

    sums_leaf[me] = jnp.broadcast_to(summed(direction * image1), (TARGETS, 128))
    leaf_exchange = Exchange(
        "leaf", N_LEAF, me, lambda dev: sums_leaf.at[dev], sums_leaf_send, sums_leaf_recv
    )
    leaf_exchange.start()
    leaf_exchange.wait()
    total = sums_leaf[0]
    for dev in range(1, N_LEAF):
        total = total + sums_leaf[dev]
    sums_grp[grp] = total
    grp_exchange = Exchange(
        "grp", N_GRP, grp, lambda g: sums_grp.at[g], sums_grp_send, sums_grp_recv
    )
    grp_exchange.start()
    grp_exchange.wait()
    total = sums_grp[0]
    for g in range(1, N_GRP):
        total = total + sums_grp[g]
    step_ref[...] = jnp.broadcast_to(norm1 / total[:, 0:1], (TARGETS, BLOCK))

    for sender in (
        *first_gathers,
        *coord_gathers,
        *image_exchange,
        root_exchange,
        *weight_exchange,
        *top_exchange,
        leaf_exchange,
        grp_exchange,
    ):
        sender.finish()


def on_device(*operands):
    vmem, smem, anywhere = (
        pl.BlockSpec(memory_space=space) for space in (pltpu.VMEM, pltpu.SMEM, pl.ANY)
    )
    messages = 2 * len(LABELS)
    dma = pltpu.SemaphoreType.DMA
    out = jax.ShapeDtypeStruct((TARGETS, BLOCK), F32)
    solution1, residual1, direction, image1, step = pl.pallas_call(
        body,
        out_shape=(out,) * 5,
        in_specs=[vmem, vmem, smem, smem, vmem, vmem, anywhere, anywhere, smem],
        out_specs=(vmem,) * 5,
        scratch_shapes=[
            pltpu.VMEM((2 * N_LEAF, FEATURES, LEAF), BF16),
            pltpu.VMEM((2 * N_LEAF, TARGETS, LEAF), F32),
            pltpu.VMEM((2 * N_LEAF, TARGETS, LEAF), F32),
            pltpu.VMEM((2, 3 * FEATURES, LEAF), BF16),
            pltpu.VMEM((N_LEAF, FEATURES, RANK), BF16),
            pltpu.VMEM((N_LEAF, FEATURES, RANK), BF16),
            pltpu.VMEM((N_GRP, FEATURES, RANK), BF16),
            pltpu.VMEM((2, N_LEAF, 3, TARGETS, RANK), F32),
            pltpu.VMEM((2, N_GRP, 2, TARGETS, RANK), F32),
            pltpu.VMEM((N_LEAF, TARGETS, 128), F32),
            pltpu.VMEM((N_GRP, TARGETS, 128), F32),
            pltpu.VMEM((2, RANK, BLOCK), F32),
            pltpu.VMEM((2 * RANK, BLOCK), BF16),
            pltpu.VMEM((2 * RANK, BLOCK), BF16),
            pltpu.VMEM((2, 2 * TARGETS, LEAF), F32),
            pltpu.VMEM((TARGETS, BLOCK), F32),
            pltpu.VMEM((TARGETS, BLOCK), F32),
            pltpu.VMEM((KEPT, 2, LEAF, LEAF), BF16),
            dma((2,)),
            dma((messages,)),
            dma((messages,)),
            dma((messages,)),
            dma((messages,)),
            dma((len(PIECES), N_LEAF)),
            dma((len(PIECES), N_LEAF)),
            dma((messages,)),
            dma((messages,)),
            dma((N_GRP,)),
            dma((N_GRP,)),
            dma((2, N_LEAF)),
            dma((2, N_LEAF)),
            dma((2, N_GRP)),
            dma((2, N_GRP)),
            dma((N_LEAF,)),
            dma((N_LEAF,)),
            dma((N_GRP,)),
            dma((N_GRP,)),
        ],
        compiler_params=pltpu.CompilerParams(
            collective_id=0, has_side_effects=True, vmem_limit_bytes=62 * 2**20
        ),
    )(*operands)
    return solution1 + step * direction, residual1 - step * image1


def solution(mesh):
    placed = (
        P(None, ("grp", "leaf")),
        P(None, ("grp", "leaf")),
        P(("grp", "leaf"), None),
        P(("grp", "leaf")),
        P(("grp", "leaf"), None),
        P("grp", None),
        P(None, ("grp", "leaf")),
        P(None, ("grp", "leaf")),
        P(),
    )
    return jax.shard_map(
        on_device,
        mesh=mesh,
        in_specs=placed,
        out_specs=(P(None, ("grp", "leaf")), P(None, ("grp", "leaf"))),
        check_vma=False,
    )
```

```python
import math

import jax
import jax.numpy as jnp
from jax import lax
from jax.experimental import pallas as pl
from jax.experimental.pallas import tpu as pltpu
from jax.sharding import PartitionSpec as P

FEATURES = 32
TARGETS = 8
LEAF = 1024
RANK = 256
SLOTS = 8
SIDE = 4
N_LEAF = 16
N_GRP = 8
BLOCK = 2 * LEAF
CHUNK = 512
KEPT = 11
PIECES = ((0, 0, LEAF), (1, 0, LEAF // 2), (1, LEAF // 2, LEAF // 2))
MESH = pl.DeviceIdType.MESH
F32 = jnp.float32
BF16 = jnp.bfloat16
SCALE = math.log2(math.e) / 16.0

LABELS = (
    [(1, 0, None), (3, 0, None), (2, 0, 0), (2, 0, 1)]
    + [(df, ds, None) for df in range(4) for ds in (1, 3)]
    + [(df, 2, part) for df in range(4) for part in (0, 1)]
)
PLACE = {label: i for i, label in enumerate(LABELS)}


def dot(left, right):
    return jnp.dot(left, right, preferred_element_type=F32)


def dot_tn(left, right):
    return lax.dot_general(left, right, (((0,), (0,)), ((), ())), preferred_element_type=F32)


def dot_nt(left, right):
    return lax.dot_general(left, right, (((1,), (1,)), ((), ())), preferred_element_type=F32)


def halves(value):
    high = value.astype(BF16)
    return high, (value - high.astype(F32)).astype(BF16)


def stacked(value):
    high = value.astype(BF16).astype(F32)
    return jnp.concatenate([high, value - high], axis=0).astype(BF16)


def folded(value):
    return value[:TARGETS] + value[TARGETS:]


def thirds(coords):
    scaled = coords.astype(F32) * SCALE
    first = scaled.astype(BF16)
    rest = scaled - first.astype(F32)
    second = rest.astype(BF16)
    third = (rest - second.astype(F32)).astype(BF16)
    return jnp.concatenate([first, second, third], axis=0)


def self_scale(coords):
    wide = coords.astype(F32)
    return jnp.exp2(jnp.sum(wide * wide, axis=0, keepdims=True) * (-0.5 * SCALE))


def kernel_halves(rows, columns3):
    return halves(jnp.exp2(dot_tn(jnp.concatenate([rows, rows, rows], axis=0), columns3)))


def applied(field16, high, low):
    return dot(field16, high) + dot(field16, low)


class Gather:
    def __init__(self, half, me, slot, part, send, recv):
        first, second = lax.div(me, SIDE), lax.rem(me, SIDE)
        if half == 1:
            first, second = second, first
        self.half, self.first, self.second = half, first, second
        self.slot, self.part, self.send, self.recv = slot, part, send, recv
        self.sent = []

    def device(self, df, ds):
        f = lax.rem(self.first + SIDE - df, SIDE)
        s = lax.rem(self.second + SIDE - ds, SIDE)
        return f * SIDE + s if self.half == 0 else s * SIDE + f

    def ref(self, df, ds, part):
        block = self.slot(self.device(df, ds))
        return block if part is None else self.part(block, part)

    def copy(self, mine, label, part, to):
        place = self.half * len(LABELS) + PLACE[label]
        ref = self.ref(mine[0], mine[1], part)
        return pltpu.make_async_remote_copy(
            src_ref=ref,
            dst_ref=ref,
            send_sem=self.send.at[place],
            recv_sem=self.recv.at[place],
            device_id={"leaf": to},
            device_id_type=MESH,
        )

    def push(self, mine, label, to):
        copy = self.copy(mine, label, label[2], to)
        copy.start()
        self.sent.append(copy)

    def wait(self, *labels):
        for label in labels:
            self.copy(label[:2], label, label[2], self.device(1, 0)).wait_recv()

    def along_first(self, ahead):
        return self.device(3 if ahead else 1, 0)

    def along_second(self, ahead):
        return self.device(0, 3 if ahead else 1)

    def spread(self, df):
        self.push((df, 0), (df, 1, None), self.along_second(True))
        self.push((df, 0), (df, 3, None), self.along_second(False))

    def relay(self, df):
        self.wait((df, 1, None))
        self.push((df, 1), (df, 2, 0), self.along_second(True))
        self.wait((df, 3, None))
        self.push((df, 3), (df, 2, 1), self.along_second(False))

    def own_first(self):
        self.push((0, 0), (1, 0, None), self.along_first(True))
        self.push((0, 0), (3, 0, None), self.along_first(False))

    def own_second(self):
        self.spread(0)

    def relay_first(self):
        self.wait((1, 0, None))
        self.push((1, 0), (2, 0, 0), self.along_first(True))
        self.wait((3, 0, None))
        self.push((3, 0), (2, 0, 1), self.along_first(False))

    def spread_near(self):
        self.spread(1)
        self.spread(3)

    def spread_far(self):
        self.wait((2, 0, 0), (2, 0, 1))
        self.spread(2)

    def relay_own(self):
        self.relay(0)

    def relay_near(self):
        self.relay(1)
        self.relay(3)

    def relay_far(self):
        self.relay(2)

    def arrive(self):
        self.wait(*[(df, 2, part) for df in (0, 1, 3, 2) for part in (0, 1)])

    def finish(self):
        for copy in self.sent:
            copy.wait_send()


class Exchange:
    def __init__(self, axis, size, me, block, send, recv):
        self.axis, self.size, self.me, self.block = axis, size, me, block
        self.send, self.recv = send, recv
        self.sent = []

    def copy(self, owner, step, to):
        ref = self.block(owner)
        return pltpu.make_async_remote_copy(
            src_ref=ref,
            dst_ref=ref,
            send_sem=self.send.at[step],
            recv_sem=self.recv.at[step],
            device_id={self.axis: to},
            device_id_type=MESH,
        )

    def start(self):
        for step in range(1, self.size):
            copy = self.copy(self.me, step, lax.rem(self.me + step, self.size))
            copy.start()
            self.sent.append(copy)

    def wait(self):
        for step in range(1, self.size):
            owner = lax.rem(self.me + self.size - step, self.size)
            self.copy(owner, step, owner).wait_recv()

    def finish(self):
        for copy in self.sent:
            copy.wait_send()


def body(
    points_ref,
    right_ref,
    listed_ref,
    count_ref,
    mid_pick_ref,
    top_pick_ref,
    mid_basis_ref,
    top_basis_ref,
    noise_ref,
    solution_ref,
    residual_ref,
    direction_ref,
    image_ref,
    step_ref,
    all_points,
    fields0,
    fields1,
    own3,
    mid_coords,
    top_coords,
    roots,
    weights,
    tops,
    sums_leaf,
    sums_grp,
    basis,
    basis_high,
    basis_low,
    near_sum,
    image,
    term,
    kept,
    basis_sem,
    points_send,
    points_recv,
    field_send,
    field_recv,
    image_send,
    image_recv,
    coords_send,
    coords_recv,
    roots_send,
    roots_recv,
    weights_send,
    weights_recv,
    tops_send,
    tops_recv,
    sums_leaf_send,
    sums_leaf_recv,
    sums_grp_send,
    sums_grp_recv,
):
    me, grp = lax.axis_index("leaf"), lax.axis_index("grp")
    all_fields = (fields0, fields1)

    loads = [
        pltpu.make_async_copy(ref, basis.at[i], basis_sem.at[i])
        for i, ref in enumerate((mid_basis_ref, top_basis_ref))
    ]
    for load in loads:
        load.start()

    barrier = pltpu.get_barrier_semaphore()
    x, z = lax.div(me, SIDE), lax.rem(me, SIDE)
    beside = [{"leaf": lax.rem(x + step, SIDE) * SIDE + z} for step in (1, 3)]
    beside += [{"leaf": x * SIDE + lax.rem(z + step, SIDE)} for step in (1, 3)]
    beside += [{"grp": lax.rem(grp + step, N_GRP)} for step in range(1, N_GRP)]
    for device in beside:
        pl.semaphore_signal(barrier, inc=1, device_id=device, device_id_type=MESH)

    points = points_ref[...]
    right = right_ref[...]
    scale = self_scale(points)
    field = right * scale
    for slot in range(2):
        columns = slice(slot * LEAF, (slot + 1) * LEAF)
        all_points[2 * me + slot] = points[:, columns]
        fields0[2 * me + slot] = field[:, columns]
        own3[slot] = thirds(points[:, columns])

    pl.semaphore_wait(barrier, len(beside))

    def gathers(slot_of, part_of, send, recv):
        return [
            Gather(half, me, lambda dev, half=half: slot_of(half, dev), part_of, send, recv)
            for half in range(2)
        ]

    point_gathers = gathers(
        lambda half, dev: all_points.at[2 * dev + half],
        lambda block, part: block.at[pl.ds(16 * part, 16)],
        points_send,
        points_recv,
    )
    first_field_gathers = gathers(
        lambda half, dev: fields0.at[2 * dev + half],
        lambda block, part: block.at[:, pl.ds(512 * part, 512)],
        field_send,
        field_recv,
    )
    coord_gathers = gathers(
        lambda half, dev: (mid_coords, top_coords)[half].at[dev],
        lambda block, part: block.at[pl.ds(16 * part, 16)],
        coords_send,
        coords_recv,
    )
    first_gathers = [*point_gathers, *first_field_gathers]
    image_exchange = [
        Exchange(
            "leaf",
            N_LEAF,
            me,
            lambda dev, piece=piece: fields1.at[2 * dev + piece[0], :, pl.ds(piece[1], piece[2])],
            image_send.at[i],
            image_recv.at[i],
        )
        for i, piece in enumerate(PIECES)
    ]
    root_exchange = Exchange("grp", N_GRP, grp, lambda g: roots.at[g], roots_send, roots_recv)
    weight_exchange = [
        Exchange(
            "leaf",
            N_LEAF,
            me,
            lambda dev, it=it: weights.at[it, dev, pl.ds(0, 2 + it)],
            weights_send.at[it],
            weights_recv.at[it],
        )
        for it in range(2)
    ]
    top_exchange = [
        Exchange(
            "grp",
            N_GRP,
            grp,
            lambda g, it=it: tops.at[it, g, pl.ds(0, 1 + it)],
            tops_send.at[it],
            tops_recv.at[it],
        )
        for it in range(2)
    ]

    def step(gathered, *names):
        for name in names:
            for gather in gathered:
                getattr(gather, name)()

    def add_block(ready, slot, place, rows_of, field16, start, width):
        columns = pl.ds(start, width)
        height = CHUNK * LEAF // width
        total = None
        for first in range(0, LEAF, height):
            rows = pl.ds(first, height)
            if ready and place is not None:
                high, low = kept[place, 0, rows, columns], kept[place, 1, rows, columns]
            else:
                high, low = kernel_halves(rows_of(rows), own3[slot, :, columns])
                if place is not None:
                    kept[place, 0, rows, columns] = high
                    kept[place, 1, rows, columns] = low
            part = applied(field16[:, first : first + height], high, low)
            total = part if total is None else total + part
        near_sum[slot, :, columns] += total

    def near_self(it, slot):
        near_sum[slot] = jnp.zeros((2 * TARGETS, LEAF), F32)
        field16 = stacked(all_fields[it][2 * me + slot] * count_ref[slot].astype(F32))
        base = slot * LEAF
        rows_of = lambda rows: points_ref[:, pl.ds(base + rows.start, rows.size)]
        add_block(False, slot, None, rows_of, field16, 0, LEAF)

    def near_listed(it, slot, begin=1, end=SLOTS, start=0, width=LEAF):
        count = count_ref[slot]

        def run(low_end, high_end, keep):
            def one(k, carried):
                leaf = listed_ref[slot, k]
                active = jnp.where(k < count, 1.0, 0.0).astype(F32)
                field16 = stacked(all_fields[it][leaf] * active)
                place = slot * (SLOTS - 1) + k - 1 if keep else None
                rows_of = lambda rows: all_points[leaf, :, rows]
                add_block(it == 1, slot, place, rows_of, field16, start, width)
                return carried

            if low_end < high_end:
                lax.fori_loop(low_end, high_end, one, 0, unroll=True)

        limit = min(max(KEPT - slot * (SLOTS - 1) + 1, 1), SLOTS)
        run(begin, min(end, limit), True)
        run(max(begin, limit), end, False)

    def near(slot, start, width):
        columns = pl.ds(start, width)
        base = slot * LEAF + start
        return folded(near_sum[slot, :, columns]) * (scale[:, base : base + width] * LEAF**-0.5)

    def project(value):
        value16 = stacked(value)
        return folded(dot_nt(value16, basis_high[...]) + dot_nt(value16, basis_low[...]))

    def side_by_side(blocks):
        return jnp.concatenate(blocks, axis=1)

    def skeleton_image(coords_of, weights_of, count, columns3, scaled=True):
        total = jnp.zeros((2 * TARGETS, RANK), F32)
        for start in range(0, count, 4):
            rows = side_by_side([coords_of(start + i) for i in range(4)])
            weighted = side_by_side([weights_of(start + i) for i in range(4)])
            field16 = stacked(weighted if scaled else weighted * self_scale(rows))
            total = total + applied(field16, *kernel_halves(rows, columns3))
        return folded(total)

    step(first_gathers, "own_first", "own_second")

    def picked(pick, base):
        found = jnp.zeros((FEATURES, RANK), F32)
        for start in range(0, BLOCK, CHUNK):
            rows = lax.broadcasted_iota(jnp.int32, (CHUNK, RANK), 0) + (base + start)
            chosen = jnp.where(rows == pick, 1.0, 0.0).astype(BF16)
            found = found + dot(points[:, start : start + CHUNK], chosen)
        return found.astype(BF16)

    own_mid = picked(mid_pick_ref[...], 0)
    mid_coords[me] = own_mid
    top_coords[me] = picked(top_pick_ref[...], me * BLOCK)
    mid3, mid_scale = thirds(own_mid), self_scale(own_mid)

    step(first_gathers, "relay_first", "spread_near")
    step(coord_gathers, "own_first", "own_second")
    near_self(0, 0)
    step(first_gathers, "spread_far", "relay_own", "relay_near")
    step(coord_gathers, "relay_first", "spread_near")

    for load in loads:
        load.wait()
    for i in range(2):
        for start in range(0, RANK, 64):
            high, low = halves(basis[i, start : start + 64, :])
            basis_high[i * RANK + start : i * RANK + start + 64, :] = high
            basis_low[i * RANK + start : i * RANK + start + 64, :] = low

    def send_weights(it, value, sums):
        parts = project(value)
        weights[it, me, 0] = parts[:, :RANK] * mid_scale
        weights[it, me, 1] = parts[:, RANK:]
        if sums is not None:
            weights[it, me, 2] = sums
        weight_exchange[it].start()

    near_self(0, 1)
    step(first_gathers, "relay_far")
    step(coord_gathers, "spread_far")
    send_weights(0, right, None)
    step(coord_gathers, "relay_own", "relay_near")
    step(first_gathers, "arrive")

    def mid_image(it):
        weight_exchange[it].wait()
        top = weights[it, 0, 1]
        for dev in range(1, N_LEAF):
            top = top + weights[it, dev, 1]
        tops[it, grp, 0] = top
        if it == 1:
            sums = weights[it, 0, 2]
            for dev in range(1, N_LEAF):
                sums = sums + weights[it, dev, 2]
            tops[it, grp, 1] = sums
        top_exchange[it].start()
        found = skeleton_image(
            lambda dev: mid_coords[dev], lambda dev: weights[it, dev, 0], N_LEAF, mid3
        )
        return found * (mid_scale * RANK**-0.5)

    def expand(it, mid_part):
        top_exchange[it].wait()
        found = skeleton_image(
            lambda g: roots[g], lambda g: tops[it, g, 0], N_GRP, root3, scaled=False
        )
        top_part = found * (root_scale * RANK**-0.5)
        image16 = stacked(side_by_side([mid_part, top_part]))
        for start in range(0, BLOCK, CHUNK):
            columns = slice(start, start + CHUNK)
            term[:, columns] = folded(
                applied(image16, basis_high[:, columns], basis_low[:, columns])
            )

    noise = noise_ref[0]

    def finished(value, slot, start, width):
        base = slot * LEAF + start
        columns = slice(base, base + width)
        return noise * value[:, columns] + near(slot, start, width) + term[:, columns]

    near_listed(0, 0, 1, 3)
    step(coord_gathers, "relay_far")
    near_listed(0, 0, 3, 6)
    step(coord_gathers, "arrive")
    own_root = jnp.zeros((FEATURES, RANK), F32)
    for dev in range(N_LEAF):
        own_root = own_root + top_coords[dev].astype(F32)
    own_root = own_root.astype(BF16)
    roots[grp] = own_root
    root_exchange.start()
    root3, root_scale = thirds(own_root), self_scale(own_root)
    mid_part = mid_image(0)
    near_listed(0, 0, 6, SLOTS)
    near_listed(0, 1, 1, 3)
    root_exchange.wait()
    expand(0, mid_part)

    for exchange, (slot, start, width) in zip(image_exchange, PIECES, strict=True):
        if slot == 1:
            near_listed(0, slot, 3, SLOTS, start, width)
        found = finished(right, slot, start, width)
        base = slot * LEAF + start
        image[:, base : base + width] = found
        fields1[2 * me + slot, :, start : start + width] = found * scale[:, base : base + width]
        exchange.start()

    lane = lax.broadcasted_iota(jnp.int32, (TARGETS, RANK), 1)

    def summed(value):
        return jnp.sum(value, axis=1, keepdims=True)

    first_image = image[...]
    sums = jnp.where(
        lane == 0,
        summed(right * right),
        jnp.where(lane == 1, summed(right * first_image), summed(first_image * first_image)),
    )
    send_weights(1, first_image, sums)
    near_self(1, 0)
    near_self(1, 1)
    for exchange in image_exchange:
        exchange.wait()
    near_listed(1, 0)
    mid_part = mid_image(1)
    near_listed(1, 1)
    expand(1, mid_part)

    totals = tops[1, 0, 1]
    for g in range(1, N_GRP):
        totals = totals + tops[1, g, 1]
    norm0, curve0, square0 = totals[:, 0:1], totals[:, 1:2], totals[:, 2:3]
    alpha = norm0 / curve0
    norm1 = norm0 - 2.0 * alpha * curve0 + alpha * alpha * square0
    beta = norm1 / norm0
    second_image = jnp.concatenate(
        [finished(first_image, slot, 0, LEAF) for slot in range(2)], axis=1
    )
    residual = right - alpha * first_image
    direction = residual + beta * right
    image1 = (1.0 + beta) * first_image - alpha * second_image
    solution_ref[...] = alpha * right
    residual_ref[...] = residual
    direction_ref[...] = direction
    image_ref[...] = image1

    diagonal = lax.broadcasted_iota(jnp.int32, (TARGETS, 128), 0) == lax.broadcasted_iota(
        jnp.int32, (TARGETS, 128), 1
    )
    curve1 = jnp.where(diagonal, summed(direction * image1), 0.0)
    sums_leaf[me] = jnp.sum(curve1, axis=0, keepdims=True)
    leaf_exchange = Exchange(
        "leaf", N_LEAF, me, lambda dev: sums_leaf.at[dev], sums_leaf_send, sums_leaf_recv
    )
    leaf_exchange.start()
    leaf_exchange.wait()
    total = sums_leaf[0]
    for dev in range(1, N_LEAF):
        total = total + sums_leaf[dev]
    sums_grp[grp] = total
    grp_exchange = Exchange(
        "grp", N_GRP, grp, lambda g: sums_grp.at[g], sums_grp_send, sums_grp_recv
    )
    grp_exchange.start()
    grp_exchange.wait()
    total = sums_grp[0]
    for g in range(1, N_GRP):
        total = total + sums_grp[g]
    curve1 = summed(jnp.where(diagonal, total, 0.0))
    step_ref[...] = jnp.broadcast_to(norm1 / curve1, (TARGETS, BLOCK))

    for sender in (
        *first_gathers,
        *coord_gathers,
        *image_exchange,
        root_exchange,
        *weight_exchange,
        *top_exchange,
        leaf_exchange,
        grp_exchange,
    ):
        sender.finish()


def on_device(*operands):
    vmem, smem, anywhere = (
        pl.BlockSpec(memory_space=space) for space in (pltpu.VMEM, pltpu.SMEM, pl.ANY)
    )
    messages = 2 * len(LABELS)
    dma = pltpu.SemaphoreType.DMA
    out = jax.ShapeDtypeStruct((TARGETS, BLOCK), F32)
    solution1, residual1, direction, image1, step = pl.pallas_call(
        body,
        out_shape=(out,) * 5,
        in_specs=[vmem, vmem, smem, smem, vmem, vmem, anywhere, anywhere, smem],
        out_specs=(vmem,) * 5,
        scratch_shapes=[
            pltpu.VMEM((2 * N_LEAF, FEATURES, LEAF), BF16),
            pltpu.VMEM((2 * N_LEAF, TARGETS, LEAF), F32),
            pltpu.VMEM((2 * N_LEAF, TARGETS, LEAF), F32),
            pltpu.VMEM((2, 3 * FEATURES, LEAF), BF16),
            pltpu.VMEM((N_LEAF, FEATURES, RANK), BF16),
            pltpu.VMEM((N_LEAF, FEATURES, RANK), BF16),
            pltpu.VMEM((N_GRP, FEATURES, RANK), BF16),
            pltpu.VMEM((2, N_LEAF, 3, TARGETS, RANK), F32),
            pltpu.VMEM((2, N_GRP, 2, TARGETS, RANK), F32),
            pltpu.VMEM((N_LEAF, 1, 128), F32),
            pltpu.VMEM((N_GRP, 1, 128), F32),
            pltpu.VMEM((2, RANK, BLOCK), F32),
            pltpu.VMEM((2 * RANK, BLOCK), BF16),
            pltpu.VMEM((2 * RANK, BLOCK), BF16),
            pltpu.VMEM((2, 2 * TARGETS, LEAF), F32),
            pltpu.VMEM((TARGETS, BLOCK), F32),
            pltpu.VMEM((TARGETS, BLOCK), F32),
            pltpu.VMEM((KEPT, 2, LEAF, LEAF), BF16),
            dma((2,)),
            dma((messages,)),
            dma((messages,)),
            dma((messages,)),
            dma((messages,)),
            dma((len(PIECES), N_LEAF)),
            dma((len(PIECES), N_LEAF)),
            dma((messages,)),
            dma((messages,)),
            dma((N_GRP,)),
            dma((N_GRP,)),
            dma((2, N_LEAF)),
            dma((2, N_LEAF)),
            dma((2, N_GRP)),
            dma((2, N_GRP)),
            dma((N_LEAF,)),
            dma((N_LEAF,)),
            dma((N_GRP,)),
            dma((N_GRP,)),
        ],
        compiler_params=pltpu.CompilerParams(
            collective_id=0, has_side_effects=True, vmem_limit_bytes=62 * 2**20
        ),
    )(*operands)
    return solution1 + step * direction, residual1 - step * image1


def solution(mesh):
    placed = (
        P(None, ("grp", "leaf")),
        P(None, ("grp", "leaf")),
        P(("grp", "leaf"), None),
        P(("grp", "leaf")),
        P(("grp", "leaf"), None),
        P("grp", None),
        P(None, ("grp", "leaf")),
        P(None, ("grp", "leaf")),
        P(),
    )
    return jax.shard_map(
        on_device,
        mesh=mesh,
        in_specs=placed,
        out_specs=(P(None, ("grp", "leaf")), P(None, ("grp", "leaf"))),
        check_vma=False,
    )
```

```python
import math

import jax
import jax.numpy as jnp
from jax import lax
from jax.experimental import pallas as pl
from jax.experimental.pallas import tpu as pltpu
from jax.sharding import PartitionSpec as P

FEATURES = 32
TARGETS = 8
LEAF = 1024
RANK = 256
SLOTS = 8
SIDE = 4
N_LEAF = 16
N_GRP = 8
BLOCK = 2 * LEAF
CHUNK = 512
KEPT = 11
PIECES = ((0, LEAF // 2), (LEAF // 2, LEAF // 2))
MESH = pl.DeviceIdType.MESH
F32 = jnp.float32
BF16 = jnp.bfloat16
SCALE = math.log2(math.e) / 16.0

LABELS = (
    [(1, 0, None), (3, 0, None), (2, 0, 0), (2, 0, 1)]
    + [(df, ds, None) for df in range(4) for ds in (1, 3)]
    + [(df, 2, part) for df in range(4) for part in (0, 1)]
)
PLACE = {label: i for i, label in enumerate(LABELS)}


def dot(left, right):
    return jnp.dot(left, right, preferred_element_type=F32)


def dot_tn(left, right):
    return lax.dot_general(left, right, (((0,), (0,)), ((), ())), preferred_element_type=F32)


def dot_nt(left, right):
    return lax.dot_general(left, right, (((1,), (1,)), ((), ())), preferred_element_type=F32)


def halves(value):
    high = value.astype(BF16)
    return high, (value - high.astype(F32)).astype(BF16)


def stacked(value):
    high = value.astype(BF16).astype(F32)
    return jnp.concatenate([high, value - high], axis=0).astype(BF16)


def folded(value):
    return value[:TARGETS] + value[TARGETS:]


def thirds(coords):
    scaled = coords.astype(F32) * SCALE
    first = scaled.astype(BF16)
    rest = scaled - first.astype(F32)
    second = rest.astype(BF16)
    third = (rest - second.astype(F32)).astype(BF16)
    return jnp.concatenate([first, second, third], axis=0)


def self_scale(coords):
    wide = coords.astype(F32)
    return jnp.exp2(jnp.sum(wide * wide, axis=0, keepdims=True) * (-0.5 * SCALE))


def kernel_halves(rows, columns3):
    return halves(jnp.exp2(dot_tn(jnp.concatenate([rows, rows, rows], axis=0), columns3)))


def applied(field16, high, low):
    return dot(field16, high) + dot(field16, low)


class Gather:
    def __init__(self, half, me, slot, part, send, recv):
        first, second = lax.div(me, SIDE), lax.rem(me, SIDE)
        if half == 1:
            first, second = second, first
        self.half, self.first, self.second = half, first, second
        self.slot, self.part, self.send, self.recv = slot, part, send, recv
        self.sent = []

    def device(self, df, ds):
        f = lax.rem(self.first + SIDE - df, SIDE)
        s = lax.rem(self.second + SIDE - ds, SIDE)
        return f * SIDE + s if self.half == 0 else s * SIDE + f

    def ref(self, df, ds, part):
        block = self.slot(self.device(df, ds))
        return block if part is None else self.part(block, part)

    def copy(self, mine, label, part, to):
        place = self.half * len(LABELS) + PLACE[label]
        ref = self.ref(mine[0], mine[1], part)
        return pltpu.make_async_remote_copy(
            src_ref=ref,
            dst_ref=ref,
            send_sem=self.send.at[place],
            recv_sem=self.recv.at[place],
            device_id={"leaf": to},
            device_id_type=MESH,
        )

    def push(self, mine, label, to):
        copy = self.copy(mine, label, label[2], to)
        copy.start()
        self.sent.append(copy)

    def wait(self, *labels):
        for label in labels:
            self.copy(label[:2], label, label[2], self.device(1, 0)).wait_recv()

    def along_first(self, ahead):
        return self.device(3 if ahead else 1, 0)

    def along_second(self, ahead):
        return self.device(0, 3 if ahead else 1)

    def spread(self, df):
        self.push((df, 0), (df, 1, None), self.along_second(True))
        self.push((df, 0), (df, 3, None), self.along_second(False))

    def relay(self, df):
        self.wait((df, 1, None))
        self.push((df, 1), (df, 2, 0), self.along_second(True))
        self.wait((df, 3, None))
        self.push((df, 3), (df, 2, 1), self.along_second(False))

    def own_first(self):
        self.push((0, 0), (1, 0, None), self.along_first(True))
        self.push((0, 0), (3, 0, None), self.along_first(False))

    def own_second(self):
        self.spread(0)

    def relay_first(self):
        self.wait((1, 0, None))
        self.push((1, 0), (2, 0, 0), self.along_first(True))
        self.wait((3, 0, None))
        self.push((3, 0), (2, 0, 1), self.along_first(False))

    def spread_near(self):
        self.spread(1)
        self.spread(3)

    def spread_far(self):
        self.wait((2, 0, 0), (2, 0, 1))
        self.spread(2)

    def relay_own(self):
        self.relay(0)

    def relay_near(self):
        self.relay(1)
        self.relay(3)

    def relay_far(self):
        self.relay(2)

    def arrive(self):
        self.wait(*[(df, 2, part) for df in (0, 1, 3, 2) for part in (0, 1)])

    def finish(self):
        for copy in self.sent:
            copy.wait_send()


class Exchange:
    def __init__(self, axis, size, me, block, send, recv):
        self.axis, self.size, self.me, self.block = axis, size, me, block
        self.send, self.recv = send, recv
        self.sent = []

    def copy(self, owner, step, to):
        ref = self.block(owner)
        return pltpu.make_async_remote_copy(
            src_ref=ref,
            dst_ref=ref,
            send_sem=self.send.at[step],
            recv_sem=self.recv.at[step],
            device_id={self.axis: to},
            device_id_type=MESH,
        )

    def start(self):
        for step in range(1, self.size):
            copy = self.copy(self.me, step, lax.rem(self.me + step, self.size))
            copy.start()
            self.sent.append(copy)

    def wait(self):
        for step in range(1, self.size):
            owner = lax.rem(self.me + self.size - step, self.size)
            self.copy(owner, step, owner).wait_recv()

    def finish(self):
        for copy in self.sent:
            copy.wait_send()


def body(
    points_ref,
    right_ref,
    listed_ref,
    count_ref,
    mid_pick_ref,
    top_pick_ref,
    mid_basis_ref,
    top_basis_ref,
    noise_ref,
    solution_ref,
    residual_ref,
    direction_ref,
    image_ref,
    step_ref,
    all_points,
    fields0,
    fields1,
    own3,
    mid_coords,
    top_coords,
    roots,
    mid_weights,
    top_weights,
    weights,
    tops,
    sums_leaf,
    sums_grp,
    basis,
    basis_high,
    basis_low,
    near_sum,
    image,
    term,
    kept,
    basis_sem,
    points_send,
    points_recv,
    field_send,
    field_recv,
    image0_send,
    image0_recv,
    image_send,
    image_recv,
    coords_send,
    coords_recv,
    roots_send,
    roots_recv,
    weights0_send,
    weights0_recv,
    weights_send,
    weights_recv,
    tops_send,
    tops_recv,
    sums_leaf_send,
    sums_leaf_recv,
    sums_grp_send,
    sums_grp_recv,
):
    me, grp = lax.axis_index("leaf"), lax.axis_index("grp")
    all_fields = (fields0, fields1)

    loads = [
        pltpu.make_async_copy(ref, basis.at[i], basis_sem.at[i])
        for i, ref in enumerate((mid_basis_ref, top_basis_ref))
    ]
    for load in loads:
        load.start()

    barrier = pltpu.get_barrier_semaphore()
    x, z = lax.div(me, SIDE), lax.rem(me, SIDE)
    beside = [{"leaf": lax.rem(x + step, SIDE) * SIDE + z} for step in (1, 3)]
    beside += [{"leaf": x * SIDE + lax.rem(z + step, SIDE)} for step in (1, 3)]
    beside += [{"grp": lax.rem(grp + step, N_GRP)} for step in range(1, N_GRP)]
    for device in beside:
        pl.semaphore_signal(barrier, inc=1, device_id=device, device_id_type=MESH)

    points = points_ref[...]
    right = right_ref[...]
    scale = self_scale(points)
    field = right * scale
    for slot in range(2):
        columns = slice(slot * LEAF, (slot + 1) * LEAF)
        all_points[2 * me + slot] = points[:, columns]
        fields0[2 * me + slot] = field[:, columns]
        own3[slot] = thirds(points[:, columns])

    pl.semaphore_wait(barrier, len(beside))

    def gathers(slot_of, part_of, send, recv):
        return [
            Gather(half, me, lambda dev, half=half: slot_of(half, dev), part_of, send, recv)
            for half in range(2)
        ]

    point_gathers = gathers(
        lambda half, dev: all_points.at[2 * dev + half],
        lambda block, part: block.at[pl.ds(16 * part, 16)],
        points_send,
        points_recv,
    )
    first_field_gathers = gathers(
        lambda half, dev: fields0.at[2 * dev + half],
        lambda block, part: block.at[:, pl.ds(512 * part, 512)],
        field_send,
        field_recv,
    )
    coord_gathers = gathers(
        lambda half, dev: (mid_coords, top_coords)[half].at[dev],
        lambda block, part: block.at[pl.ds(16 * part, 16)],
        coords_send,
        coords_recv,
    )
    first_gathers = [*point_gathers, *first_field_gathers]
    first_weight_gathers = gathers(
        lambda half, dev: (mid_weights, top_weights)[half].at[dev],
        lambda block, part: block.at[:, pl.ds(128 * part, 128)],
        weights0_send,
        weights0_recv,
    )
    small_gathers = [*coord_gathers, *first_weight_gathers]
    image_gather = gathers(
        lambda half, dev: fields1.at[2 * dev + half],
        lambda block, part: block.at[:, pl.ds(512 * part, 512)],
        image0_send,
        image0_recv,
    )[:1]
    image_exchange = [
        Exchange(
            "leaf",
            N_LEAF,
            me,
            lambda dev, piece=piece: fields1.at[2 * dev + 1, :, pl.ds(*piece)],
            image_send.at[i],
            image_recv.at[i],
        )
        for i, piece in enumerate(PIECES)
    ]
    root_exchange = Exchange("grp", N_GRP, grp, lambda g: roots.at[g], roots_send, roots_recv)
    weight_exchange = Exchange(
        "leaf", N_LEAF, me, lambda dev: weights.at[dev], weights_send, weights_recv
    )
    top_exchange = [
        Exchange(
            "grp", N_GRP, grp, lambda g, it=it: tops.at[it, g], tops_send.at[it], tops_recv.at[it]
        )
        for it in range(2)
    ]
    leaf_exchange = [
        Exchange(
            "leaf",
            N_LEAF,
            me,
            lambda dev, i=i: sums_leaf.at[i, dev],
            sums_leaf_send.at[i],
            sums_leaf_recv.at[i],
        )
        for i in range(2)
    ]
    grp_exchange = [
        Exchange(
            "grp",
            N_GRP,
            grp,
            lambda g, i=i: sums_grp.at[i, g],
            sums_grp_send.at[i],
            sums_grp_recv.at[i],
        )
        for i in range(2)
    ]

    def step(gathered, *names):
        for name in names:
            for gather in gathered:
                getattr(gather, name)()

    def add_block(ready, slot, place, rows_of, field16, start, width):
        columns = pl.ds(start, width)
        height = CHUNK * LEAF // width
        total = None
        for first in range(0, LEAF, height):
            rows = pl.ds(first, height)
            if ready and place is not None:
                high, low = kept[place, 0, rows, columns], kept[place, 1, rows, columns]
            else:
                high, low = kernel_halves(rows_of(rows), own3[slot, :, columns])
                if place is not None:
                    kept[place, 0, rows, columns] = high
                    kept[place, 1, rows, columns] = low
            part = applied(field16[:, first : first + height], high, low)
            total = part if total is None else total + part
        near_sum[slot, :, columns] += total

    def near_self(it, slot):
        near_sum[slot] = jnp.zeros((2 * TARGETS, LEAF), F32)
        field16 = stacked(all_fields[it][2 * me + slot] * count_ref[slot].astype(F32))
        base = slot * LEAF
        rows_of = lambda rows: points_ref[:, pl.ds(base + rows.start, rows.size)]
        add_block(False, slot, None, rows_of, field16, 0, LEAF)

    def near_listed(it, slot, begin=1, end=SLOTS, start=0, width=LEAF):
        count = count_ref[slot]

        def run(low_end, high_end, keep):
            def one(k, carried):
                leaf = listed_ref[slot, k]
                active = jnp.where(k < count, 1.0, 0.0).astype(F32)
                field16 = stacked(all_fields[it][leaf] * active)
                place = slot * (SLOTS - 1) + k - 1 if keep else None
                rows_of = lambda rows: all_points[leaf, :, rows]
                add_block(it == 1, slot, place, rows_of, field16, start, width)
                return carried

            if low_end < high_end:
                lax.fori_loop(low_end, high_end, one, 0, unroll=True)

        limit = min(max(KEPT - slot * (SLOTS - 1) + 1, 1), SLOTS)
        run(begin, min(end, limit), True)
        run(max(begin, limit), end, False)

    def near(slot, start, width):
        columns = pl.ds(start, width)
        base = slot * LEAF + start
        return folded(near_sum[slot, :, columns]) * (scale[:, base : base + width] * LEAF**-0.5)

    def project(value):
        value16 = stacked(value)
        return folded(dot_nt(value16, basis_high[...]) + dot_nt(value16, basis_low[...]))

    def side_by_side(blocks):
        return jnp.concatenate(blocks, axis=1)

    def skeleton_image(coords_of, weights_of, count, columns3, scaled=True):
        total = jnp.zeros((2 * TARGETS, RANK), F32)
        for start in range(0, count, 4):
            rows = side_by_side([coords_of(start + i) for i in range(4)])
            weighted = side_by_side([weights_of(start + i) for i in range(4)])
            field16 = stacked(weighted if scaled else weighted * self_scale(rows))
            total = total + applied(field16, *kernel_halves(rows, columns3))
        return folded(total)

    step(first_gathers, "own_first", "own_second")

    def picked(pick, base):
        found = jnp.zeros((FEATURES, RANK), F32)
        for start in range(0, BLOCK, CHUNK):
            rows = lax.broadcasted_iota(jnp.int32, (CHUNK, RANK), 0) + (base + start)
            chosen = jnp.where(rows == pick, 1.0, 0.0).astype(BF16)
            found = found + dot(points[:, start : start + CHUNK], chosen)
        return found.astype(BF16)

    own_mid = picked(mid_pick_ref[...], 0)
    mid_coords[me] = own_mid
    top_coords[me] = picked(top_pick_ref[...], me * BLOCK)
    mid3, mid_scale = thirds(own_mid), self_scale(own_mid)

    step(coord_gathers, "own_first", "own_second")

    for load in loads:
        load.wait()
    for i in range(2):
        for start in range(0, RANK, 64):
            high, low = halves(basis[i, start : start + 64, :])
            basis_high[i * RANK + start : i * RANK + start + 64, :] = high
            basis_low[i * RANK + start : i * RANK + start + 64, :] = low
    parts = project(right)
    mid_weights[me] = parts[:, :RANK] * mid_scale
    top_weights[me] = parts[:, RANK:]
    step(first_weight_gathers, "own_first", "own_second")

    step(first_gathers, "relay_first", "spread_near")
    step(small_gathers, "relay_first", "spread_near")
    near_self(0, 0)
    step(first_gathers, "spread_far", "relay_own", "relay_near")
    step(small_gathers, "spread_far", "relay_own", "relay_near")
    near_self(0, 1)
    step(first_gathers, "relay_far")
    step(small_gathers, "relay_far")
    step(first_gathers, "arrive")

    def start_tops(it, weight_of):
        top = weight_of(0)
        for dev in range(1, N_LEAF):
            top = top + weight_of(dev)
        tops[it, grp] = top
        top_exchange[it].start()

    def mid_image(weight_of):
        found = skeleton_image(lambda dev: mid_coords[dev], weight_of, N_LEAF, mid3)
        return found * (mid_scale * RANK**-0.5)

    def expand(it, mid_part):
        top_exchange[it].wait()
        found = skeleton_image(
            lambda g: roots[g], lambda g: tops[it, g], N_GRP, root3, scaled=False
        )
        top_part = found * (root_scale * RANK**-0.5)
        image16 = stacked(side_by_side([mid_part, top_part]))
        for start in range(0, BLOCK, CHUNK):
            columns = slice(start, start + CHUNK)
            term[:, columns] = folded(
                applied(image16, basis_high[:, columns], basis_low[:, columns])
            )

    noise = noise_ref[0]

    def finished(value, slot, start, width):
        base = slot * LEAF + start
        columns = slice(base, base + width)
        return noise * value[:, columns] + near(slot, start, width) + term[:, columns]

    near_listed(0, 0, 1, 3)
    step(small_gathers, "arrive")
    own_root = jnp.zeros((FEATURES, RANK), F32)
    for dev in range(N_LEAF):
        own_root = own_root + top_coords[dev].astype(F32)
    own_root = own_root.astype(BF16)
    roots[grp] = own_root
    root_exchange.start()
    root3, root_scale = thirds(own_root), self_scale(own_root)
    start_tops(0, lambda dev: top_weights[dev])
    mid_part = mid_image(lambda dev: mid_weights[dev])
    near_listed(0, 0, 3, SLOTS)
    root_exchange.wait()
    expand(0, mid_part)

    def finish_image(slot, start, width):
        found = finished(right, slot, start, width)
        base = slot * LEAF + start
        image[:, base : base + width] = found
        fields1[2 * me + slot, :, start : start + width] = found * scale[:, base : base + width]

    finish_image(0, 0, LEAF)
    step(image_gather, "own_first", "own_second")
    near_listed(0, 1, 1, SLOTS, *PIECES[0])
    finish_image(1, *PIECES[0])
    step(image_gather, "relay_first", "spread_near")
    image_exchange[0].start()
    near_listed(0, 1, 1, SLOTS, *PIECES[1])
    finish_image(1, *PIECES[1])
    image_exchange[1].start()
    step(image_gather, "spread_far", "relay_own", "relay_near")

    def summed(value):
        return jnp.sum(value, axis=1, keepdims=True)

    across = lax.broadcasted_iota(jnp.int32, (TARGETS, 128), 1)
    down = lax.broadcasted_iota(jnp.int32, (TARGETS, 128), 0)

    def to_row(columns):
        row = jnp.zeros((TARGETS, 128), F32)
        for i, column in enumerate(columns):
            row = jnp.where(across == down + TARGETS * i, column, row)
        return jnp.sum(row, axis=0, keepdims=True)

    def from_row(row, i):
        return summed(jnp.where(across == down + TARGETS * i, row, 0.0))

    def over_grp(i):
        leaf_exchange[i].wait()
        total = sums_leaf[i, 0]
        for dev in range(1, N_LEAF):
            total = total + sums_leaf[i, dev]
        sums_grp[i, grp] = total
        grp_exchange[i].start()

    def over_all(i):
        grp_exchange[i].wait()
        total = sums_grp[i, 0]
        for g in range(1, N_GRP):
            total = total + sums_grp[i, g]
        return total

    first_image = image[...]
    parts = project(first_image)
    weights[me, 0] = parts[:, :RANK] * mid_scale
    weights[me, 1] = parts[:, RANK:]
    weight_exchange.start()
    near_self(1, 0)
    step(image_gather, "relay_far")
    near_self(1, 1)
    sums_leaf[0, me] = to_row(
        [summed(right * right), summed(right * first_image), summed(first_image * first_image)]
    )
    leaf_exchange[0].start()
    step(image_gather, "arrive")
    for exchange in image_exchange:
        exchange.wait()
    near_listed(1, 0)
    weight_exchange.wait()
    start_tops(1, lambda dev: weights[dev, 1])
    over_grp(0)
    mid_part = mid_image(lambda dev: weights[dev, 0])
    near_listed(1, 1)
    expand(1, mid_part)

    totals = over_all(0)
    norm0, curve0, square0 = (from_row(totals, i) for i in range(3))
    alpha = norm0 / curve0
    norm1 = norm0 - 2.0 * alpha * curve0 + alpha * alpha * square0
    beta = norm1 / norm0
    second_image = jnp.concatenate(
        [finished(first_image, slot, 0, LEAF) for slot in range(2)], axis=1
    )
    residual = right - alpha * first_image
    direction = residual + beta * right
    image1 = (1.0 + beta) * first_image - alpha * second_image
    solution_ref[...] = alpha * right
    residual_ref[...] = residual
    direction_ref[...] = direction
    image_ref[...] = image1

    sums_leaf[1, me] = to_row([summed(direction * image1)])
    leaf_exchange[1].start()
    over_grp(1)
    curve1 = from_row(over_all(1), 0)
    step_ref[...] = jnp.broadcast_to(norm1 / curve1, (TARGETS, BLOCK))

    for sender in (
        *first_gathers,
        *small_gathers,
        *image_gather,
        *image_exchange,
        root_exchange,
        weight_exchange,
        *top_exchange,
        *leaf_exchange,
        *grp_exchange,
    ):
        sender.finish()


def on_device(*operands):
    vmem, smem, anywhere = (
        pl.BlockSpec(memory_space=space) for space in (pltpu.VMEM, pltpu.SMEM, pl.ANY)
    )
    messages = 2 * len(LABELS)
    dma = pltpu.SemaphoreType.DMA
    out = jax.ShapeDtypeStruct((TARGETS, BLOCK), F32)
    solution1, residual1, direction, image1, step = pl.pallas_call(
        body,
        out_shape=(out,) * 5,
        in_specs=[vmem, vmem, smem, smem, vmem, vmem, anywhere, anywhere, smem],
        out_specs=(vmem,) * 5,
        scratch_shapes=[
            pltpu.VMEM((2 * N_LEAF, FEATURES, LEAF), BF16),
            pltpu.VMEM((2 * N_LEAF, TARGETS, LEAF), F32),
            pltpu.VMEM((2 * N_LEAF, TARGETS, LEAF), F32),
            pltpu.VMEM((2, 3 * FEATURES, LEAF), BF16),
            pltpu.VMEM((N_LEAF, FEATURES, RANK), BF16),
            pltpu.VMEM((N_LEAF, FEATURES, RANK), BF16),
            pltpu.VMEM((N_GRP, FEATURES, RANK), BF16),
            pltpu.VMEM((N_LEAF, TARGETS, RANK), F32),
            pltpu.VMEM((N_LEAF, TARGETS, RANK), F32),
            pltpu.VMEM((N_LEAF, 2, TARGETS, RANK), F32),
            pltpu.VMEM((2, N_GRP, TARGETS, RANK), F32),
            pltpu.VMEM((2, N_LEAF, 1, 128), F32),
            pltpu.VMEM((2, N_GRP, 1, 128), F32),
            pltpu.VMEM((2, RANK, BLOCK), F32),
            pltpu.VMEM((2 * RANK, BLOCK), BF16),
            pltpu.VMEM((2 * RANK, BLOCK), BF16),
            pltpu.VMEM((2, 2 * TARGETS, LEAF), F32),
            pltpu.VMEM((TARGETS, BLOCK), F32),
            pltpu.VMEM((TARGETS, BLOCK), F32),
            pltpu.VMEM((KEPT, 2, LEAF, LEAF), BF16),
            dma((2,)),
            dma((messages,)),
            dma((messages,)),
            dma((messages,)),
            dma((messages,)),
            dma((messages,)),
            dma((messages,)),
            dma((len(PIECES), N_LEAF)),
            dma((len(PIECES), N_LEAF)),
            dma((messages,)),
            dma((messages,)),
            dma((N_GRP,)),
            dma((N_GRP,)),
            dma((messages,)),
            dma((messages,)),
            dma((N_LEAF,)),
            dma((N_LEAF,)),
            dma((2, N_GRP)),
            dma((2, N_GRP)),
            dma((2, N_LEAF)),
            dma((2, N_LEAF)),
            dma((2, N_GRP)),
            dma((2, N_GRP)),
        ],
        compiler_params=pltpu.CompilerParams(
            collective_id=0, has_side_effects=True, vmem_limit_bytes=62 * 2**20
        ),
    )(*operands)
    return solution1 + step * direction, residual1 - step * image1


def solution(mesh):
    placed = (
        P(None, ("grp", "leaf")),
        P(None, ("grp", "leaf")),
        P(("grp", "leaf"), None),
        P(("grp", "leaf")),
        P(("grp", "leaf"), None),
        P("grp", None),
        P(None, ("grp", "leaf")),
        P(None, ("grp", "leaf")),
        P(),
    )
    return jax.shard_map(
        on_device,
        mesh=mesh,
        in_specs=placed,
        out_specs=(P(None, ("grp", "leaf")), P(None, ("grp", "leaf"))),
        check_vma=False,
    )
```

```python
import math

import jax
import jax.numpy as jnp
from jax import lax
from jax.experimental import pallas as pl
from jax.experimental.pallas import tpu as pltpu
from jax.sharding import PartitionSpec as P

FEATURES = 32
TARGETS = 8
WIDE = FEATURES + 2 * TARGETS
LEAF = 1024
RANK = 256
SLOTS = 8
SIDE = 4
N_LEAF = 16
N_GRP = 8
BLOCK = 2 * LEAF
CHUNK = 512
KEPT = 11
MESH = pl.DeviceIdType.MESH
F32 = jnp.float32
BF16 = jnp.bfloat16
SCALE = math.log2(math.e) / 16.0

LABELS = [(1, 0), (3, 0), (2, 0)] + [(df, ds) for df in range(4) for ds in (1, 3, 2)]
PLACE = {label: i for i, label in enumerate(LABELS)}


def dot(left, right):
    return jnp.dot(left, right, preferred_element_type=F32)


def dot_tn(left, right):
    return lax.dot_general(left, right, (((0,), (0,)), ((), ())), preferred_element_type=F32)


def dot_nt(left, right):
    return lax.dot_general(left, right, (((1,), (1,)), ((), ())), preferred_element_type=F32)


def halves(value):
    high = value.astype(BF16)
    return high, (value - high.astype(F32)).astype(BF16)


def stacked(value):
    high = value.astype(BF16).astype(F32)
    return jnp.concatenate([high, value - high], axis=0).astype(BF16)


def folded(value):
    return value[:TARGETS] + value[TARGETS:]


def thirds(coords):
    scaled = coords.astype(F32) * SCALE
    first = scaled.astype(BF16)
    rest = scaled - first.astype(F32)
    second = rest.astype(BF16)
    third = (rest - second.astype(F32)).astype(BF16)
    return jnp.concatenate([first, second, third], axis=0)


def self_scale(coords):
    wide = coords.astype(F32)
    return jnp.exp2(jnp.sum(wide * wide, axis=0, keepdims=True) * (-0.5 * SCALE))


def kernel_halves(rows, columns3):
    return halves(jnp.exp2(dot_tn(jnp.concatenate([rows, rows, rows], axis=0), columns3)))


def applied(field16, high, low):
    return dot(field16, high) + dot(field16, low)


class Gather:
    def __init__(self, half, me, slot, send, recv):
        first, second = lax.div(me, SIDE), lax.rem(me, SIDE)
        if half == 1:
            first, second = second, first
        self.half, self.first, self.second = half, first, second
        self.slot, self.send, self.recv = slot, send, recv
        self.sent = []

    def device(self, df, ds):
        f = lax.rem(self.first + SIDE - df, SIDE)
        s = lax.rem(self.second + SIDE - ds, SIDE)
        return f * SIDE + s if self.half == 0 else s * SIDE + f

    def copy(self, mine, label, to):
        place = self.half * len(LABELS) + PLACE[label]
        ref = self.slot(self.device(*mine))
        return pltpu.make_async_remote_copy(
            src_ref=ref,
            dst_ref=ref,
            send_sem=self.send.at[place],
            recv_sem=self.recv.at[place],
            device_id={"leaf": to},
            device_id_type=MESH,
        )

    def push(self, mine, label, to):
        copy = self.copy(mine, label, to)
        copy.start()
        self.sent.append(copy)

    def wait(self, *labels):
        for label in labels:
            self.copy(label, label, self.device(1, 0)).wait_recv()

    def along_first(self, ahead):
        return self.device(3 if ahead else 1, 0)

    def along_second(self, ahead):
        return self.device(0, 3 if ahead else 1)

    def spread(self, df):
        self.push((df, 0), (df, 1), self.along_second(True))
        self.push((df, 0), (df, 3), self.along_second(False))

    def relay(self, df):
        came = (df, 1 if df % 2 == 0 else 3)
        self.wait(came)
        self.push(came, (df, 2), self.along_second(df % 2 == 0))

    def own(self):
        self.push((0, 0), (1, 0), self.along_first(True))
        self.push((0, 0), (3, 0), self.along_first(False))
        self.spread(0)

    def near(self):
        self.wait((1, 0))
        self.push((1, 0), (2, 0), self.along_first(True))
        self.spread(1)
        self.wait((3, 0))
        self.spread(3)
        self.relay(0)

    def far(self):
        self.wait((2, 0))
        self.spread(2)
        self.relay(1)
        self.relay(3)

    def last(self):
        self.relay(2)

    def arrive(self):
        self.wait((0, 3), (1, 1), (3, 1), (2, 3), (0, 2), (1, 2), (3, 2), (2, 2))

    def finish(self):
        for copy in self.sent:
            copy.wait_send()


class Exchange:
    def __init__(self, axis, size, me, block, send, recv):
        self.axis, self.size, self.me, self.block = axis, size, me, block
        self.send, self.recv = send, recv
        self.sent = []

    def copy(self, owner, step, to):
        ref = self.block(owner)
        return pltpu.make_async_remote_copy(
            src_ref=ref,
            dst_ref=ref,
            send_sem=self.send.at[step],
            recv_sem=self.recv.at[step],
            device_id={self.axis: to},
            device_id_type=MESH,
        )

    def start(self):
        for step in range(1, self.size):
            copy = self.copy(self.me, step, lax.rem(self.me + step, self.size))
            copy.start()
            self.sent.append(copy)

    def wait(self):
        for step in range(1, self.size):
            owner = lax.rem(self.me + self.size - step, self.size)
            self.copy(owner, step, owner).wait_recv()

    def finish(self):
        for copy in self.sent:
            copy.wait_send()


def body(
    points_ref,
    right_ref,
    listed_ref,
    count_ref,
    mid_pick_ref,
    top_pick_ref,
    mid_basis_ref,
    top_basis_ref,
    noise_ref,
    solution_ref,
    residual_ref,
    direction_ref,
    image_ref,
    step_ref,
    blocks,
    fields1,
    own3,
    smalls,
    roots,
    weights,
    tops,
    sums_leaf,
    sums_grp,
    basis,
    basis_high,
    basis_low,
    near_sum,
    image,
    term,
    kept,
    basis_sem,
    blocks_send,
    blocks_recv,
    smalls_send,
    smalls_recv,
    image0_send,
    image0_recv,
    image1_send,
    image1_recv,
    roots_send,
    roots_recv,
    weights_send,
    weights_recv,
    tops_send,
    tops_recv,
    sums_leaf_send,
    sums_leaf_recv,
    sums_grp_send,
    sums_grp_recv,
):
    me, grp = lax.axis_index("leaf"), lax.axis_index("grp")

    loads = [
        pltpu.make_async_copy(ref, basis.at[i], basis_sem.at[i])
        for i, ref in enumerate((mid_basis_ref, top_basis_ref))
    ]
    for load in loads:
        load.start()

    barrier = pltpu.get_barrier_semaphore()
    x, z = lax.div(me, SIDE), lax.rem(me, SIDE)
    beside = [{"leaf": lax.rem(x + step, SIDE) * SIDE + z} for step in (1, 3)]
    beside += [{"leaf": x * SIDE + lax.rem(z + step, SIDE)} for step in (1, 3)]
    beside += [{"grp": lax.rem(grp + step, N_GRP)} for step in range(1, N_GRP)]
    for device in beside:
        pl.semaphore_signal(barrier, inc=1, device_id=device, device_id_type=MESH)

    points = points_ref[...]
    right = right_ref[...]
    scale = self_scale(points)
    field = right * scale
    for slot in range(2):
        columns = slice(slot * LEAF, (slot + 1) * LEAF)
        blocks[2 * me + slot, 0:FEATURES] = points[:, columns]
        blocks[2 * me + slot, FEATURES:WIDE] = stacked(field[:, columns])
        own3[slot] = thirds(points[:, columns])

    pl.semaphore_wait(barrier, len(beside))

    def gathers(slot_of, send, recv):
        return [
            Gather(half, me, lambda dev, half=half: slot_of(half, dev), send, recv)
            for half in range(2)
        ]

    block_gathers = gathers(
        lambda half, dev: blocks.at[2 * dev + half], blocks_send, blocks_recv
    )
    small_gathers = gathers(lambda half, dev: smalls.at[half, dev], smalls_send, smalls_recv)
    image_gather = gathers(
        lambda half, dev: fields1.at[2 * dev + half], image0_send, image0_recv
    )[:1]
    image_exchange = Exchange(
        "leaf", N_LEAF, me, lambda dev: fields1.at[2 * dev + 1], image1_send, image1_recv
    )
    root_exchange = Exchange("grp", N_GRP, grp, lambda g: roots.at[g], roots_send, roots_recv)
    weight_exchange = Exchange(
        "leaf", N_LEAF, me, lambda dev: weights.at[dev], weights_send, weights_recv
    )
    top_exchange = Exchange("grp", N_GRP, grp, lambda g: tops.at[g], tops_send, tops_recv)
    leaf_exchange = Exchange(
        "leaf", N_LEAF, me, lambda dev: sums_leaf.at[dev], sums_leaf_send, sums_leaf_recv
    )
    grp_exchange = Exchange(
        "grp", N_GRP, grp, lambda g: sums_grp.at[g], sums_grp_send, sums_grp_recv
    )

    def step(gathered, *names):
        for name in names:
            for gather in gathered:
                getattr(gather, name)()

    def field_of(it, leaf):
        return blocks[leaf, FEATURES:WIDE, :] if it == 0 else fields1[leaf]

    def add_block(it, slot, place, rows_of, field16, weight):
        total = None
        for first in range(0, LEAF, CHUNK):
            rows = pl.ds(first, CHUNK)
            if it == 1 and place is not None:
                high, low = kept[place, 0, rows, :], kept[place, 1, rows, :]
            else:
                high, low = kernel_halves(rows_of(rows), own3[slot])
                if place is not None:
                    kept[place, 0, rows, :] = high
                    kept[place, 1, rows, :] = low
            part = applied(field16[:, first : first + CHUNK], high, low)
            total = part if total is None else total + part
        near_sum[slot] += total * weight

    def near_self(it, slot):
        near_sum[slot] = jnp.zeros((2 * TARGETS, LEAF), F32)
        base = slot * LEAF
        rows_of = lambda rows: points_ref[:, pl.ds(base + rows.start, rows.size)]
        field16 = field_of(it, 2 * me + slot)
        add_block(it, slot, None, rows_of, field16, count_ref[slot].astype(F32))

    def near_listed(it, slot, begin=1, end=SLOTS):
        count = count_ref[slot]

        def run(low_end, high_end, keep):
            def one(k, carried):
                leaf = listed_ref[slot, k]
                active = jnp.where(k < count, 1.0, 0.0).astype(F32)
                place = slot * (SLOTS - 1) + k - 1 if keep else None
                rows_of = lambda rows: blocks[leaf, 0:FEATURES, rows]
                add_block(it, slot, place, rows_of, field_of(it, leaf), active)
                return carried

            if low_end < high_end:
                lax.fori_loop(low_end, high_end, one, 0, unroll=True)

        limit = min(max(KEPT - slot * (SLOTS - 1) + 1, 1), SLOTS)
        run(begin, min(end, limit), True)
        run(max(begin, limit), end, False)

    def near(slot):
        return folded(near_sum[slot]) * (scale[:, slot * LEAF : (slot + 1) * LEAF] * LEAF**-0.5)

    def project(value):
        value16 = stacked(value)
        return folded(dot_nt(value16, basis_high[...]) + dot_nt(value16, basis_low[...]))

    def side_by_side(blocks):
        return jnp.concatenate(blocks, axis=1)

    def skeleton_image(coords_of, fields_of, count, columns3):
        total = jnp.zeros((2 * TARGETS, RANK), F32)
        for start in range(0, count, 4):
            rows = side_by_side([coords_of(start + i) for i in range(4)])
            field16 = side_by_side([fields_of(start + i) for i in range(4)])
            total = total + applied(field16, *kernel_halves(rows, columns3))
        return folded(total)

    step(block_gathers, "own")

    def picked(pick, base):
        found = jnp.zeros((FEATURES, RANK), F32)
        for start in range(0, BLOCK, CHUNK):
            rows = lax.broadcasted_iota(jnp.int32, (CHUNK, RANK), 0) + (base + start)
            chosen = jnp.where(rows == pick, 1.0, 0.0).astype(BF16)
            found = found + dot(points[:, start : start + CHUNK], chosen)
        return found.astype(BF16)

    own_mid = picked(mid_pick_ref[...], 0)
    mid3, mid_scale = thirds(own_mid), self_scale(own_mid)
    smalls[0, me, 0:FEATURES] = own_mid
    smalls[1, me, 0:FEATURES] = picked(top_pick_ref[...], me * BLOCK)

    for load in loads:
        load.wait()
    for i in range(2):
        for start in range(0, RANK, 64):
            high, low = halves(basis[i, start : start + 64, :])
            basis_high[i * RANK + start : i * RANK + start + 64, :] = high
            basis_low[i * RANK + start : i * RANK + start + 64, :] = low
    parts = project(right)
    smalls[0, me, FEATURES:WIDE] = stacked(parts[:, :RANK] * mid_scale)
    smalls[1, me, FEATURES:WIDE] = stacked(parts[:, RANK:])

    step(block_gathers, "near")
    step(small_gathers, "own")
    near_self(0, 0)
    step(block_gathers, "far")
    step(small_gathers, "near")
    near_self(0, 1)
    step(block_gathers, "last")
    step(small_gathers, "far")
    step(block_gathers, "arrive")

    def mid_image(fields_of):
        found = skeleton_image(
            lambda dev: smalls[0, dev, 0:FEATURES, :], fields_of, N_LEAF, mid3
        )
        return found * (mid_scale * RANK**-0.5)

    def expand(mid_part, fields_of):
        found = skeleton_image(
            lambda g: roots[g, 0:FEATURES, :], fields_of, N_GRP, root3
        )
        top_part = found * (root_scale * RANK**-0.5)
        image16 = stacked(side_by_side([mid_part, top_part]))
        for start in range(0, BLOCK, CHUNK):
            columns = slice(start, start + CHUNK)
            term[:, columns] = folded(
                applied(image16, basis_high[:, columns], basis_low[:, columns])
            )

    noise = noise_ref[0]

    def finished(value, slot):
        columns = slice(slot * LEAF, (slot + 1) * LEAF)
        return noise * value[:, columns] + near(slot) + term[:, columns]

    near_listed(0, 0, 1, 3)
    step(small_gathers, "last", "arrive")
    own_root, top = jnp.zeros((FEATURES, RANK), F32), jnp.zeros((2 * TARGETS, RANK), F32)
    for dev in range(N_LEAF):
        own_root = own_root + smalls[1, dev, 0:FEATURES, :].astype(F32)
        top = top + smalls[1, dev, FEATURES:WIDE, :].astype(F32)
    own_root = own_root.astype(BF16)
    root3, root_scale = thirds(own_root), self_scale(own_root)
    roots[grp, 0:FEATURES] = own_root
    roots[grp, FEATURES:WIDE] = stacked(folded(top) * root_scale)
    root_exchange.start()
    mid_part = mid_image(lambda dev: smalls[0, dev, FEATURES:WIDE, :])
    near_listed(0, 0, 3, SLOTS)
    root_exchange.wait()
    expand(mid_part, lambda g: roots[g, FEATURES:WIDE, :])

    def finish_image(slot):
        columns = slice(slot * LEAF, (slot + 1) * LEAF)
        found = finished(right, slot)
        image[:, columns] = found
        fields1[2 * me + slot] = stacked(found * scale[:, columns])

    finish_image(0)
    step(image_gather, "own")
    near_listed(0, 1, 1, 4)
    step(image_gather, "near")
    near_listed(0, 1, 4, 7)
    step(image_gather, "far")
    near_listed(0, 1, 7, SLOTS)
    finish_image(1)
    image_exchange.start()

    def summed(value):
        return jnp.sum(value, axis=1, keepdims=True)

    first_image = image[...]
    parts = project(first_image)
    lane = lax.broadcasted_iota(jnp.int32, (TARGETS, RANK), 1)
    weights[me, 0:8] = parts[:, :RANK] * mid_scale
    weights[me, 8:16] = parts[:, RANK:]
    weights[me, 16:24] = jnp.where(
        lane == 0,
        summed(right * right),
        jnp.where(lane == 1, summed(right * first_image), summed(first_image * first_image)),
    )
    weight_exchange.start()
    near_self(1, 0)
    step(image_gather, "last")
    near_self(1, 1)
    step(image_gather, "arrive")
    image_exchange.wait()
    near_listed(1, 0)
    weight_exchange.wait()
    sums = weights[0, 8:24]
    for dev in range(1, N_LEAF):
        sums = sums + weights[dev, 8:24]
    tops[grp, 0:8] = sums[0:8] * root_scale
    tops[grp, 8:16] = sums[8:16]
    top_exchange.start()
    mid_part = mid_image(lambda dev: stacked(weights[dev, 0:8]))
    near_listed(1, 1)
    top_exchange.wait()
    expand(mid_part, lambda g: stacked(tops[g, 0:8]))

    totals = tops[0, 8:16]
    for g in range(1, N_GRP):
        totals = totals + tops[g, 8:16]
    norm0, curve0, square0 = totals[:, 0:1], totals[:, 1:2], totals[:, 2:3]
    alpha = norm0 / curve0
    norm1 = norm0 - 2.0 * alpha * curve0 + alpha * alpha * square0
    beta = norm1 / norm0
    second_image = jnp.concatenate(
        [finished(first_image, slot) for slot in range(2)], axis=1
    )
    residual = right - alpha * first_image
    direction = residual + beta * right
    image1 = (1.0 + beta) * first_image - alpha * second_image
    solution_ref[...] = alpha * right
    residual_ref[...] = residual
    direction_ref[...] = direction
    image_ref[...] = image1

    diagonal = lax.broadcasted_iota(jnp.int32, (TARGETS, 128), 0) == lax.broadcasted_iota(
        jnp.int32, (TARGETS, 128), 1
    )
    curve1 = jnp.where(diagonal, summed(direction * image1), 0.0)
    sums_leaf[me] = jnp.sum(curve1, axis=0, keepdims=True)
    leaf_exchange.start()
    leaf_exchange.wait()
    total = sums_leaf[0]
    for dev in range(1, N_LEAF):
        total = total + sums_leaf[dev]
    sums_grp[grp] = total
    grp_exchange.start()
    grp_exchange.wait()
    total = sums_grp[0]
    for g in range(1, N_GRP):
        total = total + sums_grp[g]
    curve1 = summed(jnp.where(diagonal, total, 0.0))
    step_ref[...] = jnp.broadcast_to(norm1 / curve1, (TARGETS, BLOCK))

    for sender in (
        *block_gathers,
        *small_gathers,
        *image_gather,
        image_exchange,
        root_exchange,
        weight_exchange,
        top_exchange,
        leaf_exchange,
        grp_exchange,
    ):
        sender.finish()


def on_device(*operands):
    vmem, smem, anywhere = (
        pl.BlockSpec(memory_space=space) for space in (pltpu.VMEM, pltpu.SMEM, pl.ANY)
    )
    messages = 2 * len(LABELS)
    dma = pltpu.SemaphoreType.DMA
    out = jax.ShapeDtypeStruct((TARGETS, BLOCK), F32)
    solution1, residual1, direction, image1, step = pl.pallas_call(
        body,
        out_shape=(out,) * 5,
        in_specs=[vmem, vmem, smem, smem, vmem, vmem, anywhere, anywhere, smem],
        out_specs=(vmem,) * 5,
        scratch_shapes=[
            pltpu.VMEM((2 * N_LEAF, WIDE, LEAF), BF16),
            pltpu.VMEM((2 * N_LEAF, 2 * TARGETS, LEAF), BF16),
            pltpu.VMEM((2, 3 * FEATURES, LEAF), BF16),
            pltpu.VMEM((2, N_LEAF, WIDE, RANK), BF16),
            pltpu.VMEM((N_GRP, WIDE, RANK), BF16),
            pltpu.VMEM((N_LEAF, 3 * TARGETS, RANK), F32),
            pltpu.VMEM((N_GRP, 2 * TARGETS, RANK), F32),
            pltpu.VMEM((N_LEAF, 1, 128), F32),
            pltpu.VMEM((N_GRP, 1, 128), F32),
            pltpu.VMEM((2, RANK, BLOCK), F32),
            pltpu.VMEM((2 * RANK, BLOCK), BF16),
            pltpu.VMEM((2 * RANK, BLOCK), BF16),
            pltpu.VMEM((2, 2 * TARGETS, LEAF), F32),
            pltpu.VMEM((TARGETS, BLOCK), F32),
            pltpu.VMEM((TARGETS, BLOCK), F32),
            pltpu.VMEM((KEPT, 2, LEAF, LEAF), BF16),
            dma((2,)),
            dma((messages,)),
            dma((messages,)),
            dma((messages,)),
            dma((messages,)),
            dma((messages,)),
            dma((messages,)),
            dma((N_LEAF,)),
            dma((N_LEAF,)),
            dma((N_GRP,)),
            dma((N_GRP,)),
            dma((N_LEAF,)),
            dma((N_LEAF,)),
            dma((N_GRP,)),
            dma((N_GRP,)),
            dma((N_LEAF,)),
            dma((N_LEAF,)),
            dma((N_GRP,)),
            dma((N_GRP,)),
        ],
        compiler_params=pltpu.CompilerParams(
            collective_id=0, has_side_effects=True, vmem_limit_bytes=62 * 2**20
        ),
    )(*operands)
    return solution1 + step * direction, residual1 - step * image1


def solution(mesh):
    placed = (
        P(None, ("grp", "leaf")),
        P(None, ("grp", "leaf")),
        P(("grp", "leaf"), None),
        P(("grp", "leaf")),
        P(("grp", "leaf"), None),
        P("grp", None),
        P(None, ("grp", "leaf")),
        P(None, ("grp", "leaf")),
        P(),
    )
    return jax.shard_map(
        on_device,
        mesh=mesh,
        in_specs=placed,
        out_specs=(P(None, ("grp", "leaf")), P(None, ("grp", "leaf"))),
        check_vma=False,
    )
```

```python
import math

import jax
import jax.numpy as jnp
from jax import lax
from jax.experimental import pallas as pl
from jax.experimental.pallas import tpu as pltpu
from jax.sharding import PartitionSpec as P

FEATURES = 32
TARGETS = 8
WIDE = FEATURES + 2 * TARGETS
LEAF = 1024
RANK = 256
SLOTS = 8
SIDE = 4
N_LEAF = 16
N_GRP = 8
BLOCK = 2 * LEAF
CHUNK = 512
KEPT = 11
MESH = pl.DeviceIdType.MESH
F32 = jnp.float32
BF16 = jnp.bfloat16
SCALE = math.log2(math.e) / 16.0

LABELS = [(1, 0), (3, 0), (2, 0)] + [(df, ds) for df in range(4) for ds in (1, 3, 2)]
PLACE = {label: i for i, label in enumerate(LABELS)}


def dot(left, right):
    return jnp.dot(left, right, preferred_element_type=F32)


def dot_tn(left, right):
    return lax.dot_general(left, right, (((0,), (0,)), ((), ())), preferred_element_type=F32)


def dot_nt(left, right):
    return lax.dot_general(left, right, (((1,), (1,)), ((), ())), preferred_element_type=F32)


def halves(value):
    high = value.astype(BF16)
    return high, (value - high.astype(F32)).astype(BF16)


def stacked(value):
    high = value.astype(BF16).astype(F32)
    return jnp.concatenate([high, value - high], axis=0).astype(BF16)


def folded(value):
    return value[:TARGETS] + value[TARGETS:]


def thirds(coords):
    scaled = coords.astype(F32) * SCALE
    first = scaled.astype(BF16)
    rest = scaled - first.astype(F32)
    second = rest.astype(BF16)
    third = (rest - second.astype(F32)).astype(BF16)
    return jnp.concatenate([first, second, third], axis=0)


def self_scale(coords):
    wide = coords.astype(F32)
    return jnp.exp2(jnp.sum(wide * wide, axis=0, keepdims=True) * (-0.5 * SCALE))


def kernel_halves(rows, columns3):
    return halves(jnp.exp2(dot_tn(jnp.concatenate([rows, rows, rows], axis=0), columns3)))


def applied(field16, high, low):
    return dot(field16, high) + dot(field16, low)


class Gather:
    def __init__(self, half, me, slot, send, recv, turn=0):
        first, second = lax.div(me, SIDE), lax.rem(me, SIDE)
        if half == 1:
            first, second = second, first
        self.half, self.first, self.second = half, first, second
        self.slot, self.send, self.recv, self.turn = slot, send, recv, turn
        self.sent = []

    def device(self, df, ds):
        f = lax.rem(self.first + SIDE - df, SIDE)
        s = lax.rem(self.second + SIDE - ds, SIDE)
        return f * SIDE + s if self.half == 0 else s * SIDE + f

    def copy(self, mine, label, to):
        place = self.half * len(LABELS) + PLACE[label]
        ref = self.slot(self.device(*mine))
        return pltpu.make_async_remote_copy(
            src_ref=ref,
            dst_ref=ref,
            send_sem=self.send.at[place],
            recv_sem=self.recv.at[place],
            device_id={"leaf": to},
            device_id_type=MESH,
        )

    def push(self, mine, label, to):
        copy = self.copy(mine, label, to)
        copy.start()
        self.sent.append(copy)

    def wait(self, *labels):
        for label in labels:
            self.copy(label, label, self.device(1, 0)).wait_recv()

    def along_first(self, ahead):
        return self.device(3 if ahead else 1, 0)

    def along_second(self, ahead):
        return self.device(0, 3 if ahead else 1)

    def spread(self, df):
        self.push((df, 0), (df, 1), self.along_second(True))
        self.push((df, 0), (df, 3), self.along_second(False))

    def ahead(self, df):
        return (df + self.turn) % 2 == 0

    def relay(self, df):
        came = (df, 1 if self.ahead(df) else 3)
        self.wait(came)
        self.push(came, (df, 2), self.along_second(self.ahead(df)))

    def own(self):
        self.push((0, 0), (1, 0), self.along_first(True))
        self.push((0, 0), (3, 0), self.along_first(False))
        self.spread(0)

    def near(self):
        came, other = (1, 3) if self.turn == 0 else (3, 1)
        self.wait((came, 0))
        self.push((came, 0), (2, 0), self.along_first(self.turn == 0))
        self.spread(came)
        self.wait((other, 0))
        self.spread(other)
        self.relay(0)

    def far(self):
        self.wait((2, 0))
        self.spread(2)
        self.relay(1)
        self.relay(3)

    def last(self):
        self.relay(2)

    def arrive(self):
        for df in (0, 1, 3, 2):
            self.wait((df, 3 if self.ahead(df) else 1), (df, 2))

    def finish(self):
        for copy in self.sent:
            copy.wait_send()


class Exchange:
    def __init__(self, axis, size, me, block, send, recv):
        inner = size // SIDE
        self.axis, self.me, self.block = axis, me, block
        self.send, self.recv, self.inner = send, recv, inner
        self.outer_at, self.inner_at = lax.div(me, inner), lax.rem(me, inner)
        steps = [(o, i) for o in range(SIDE) for i in range(inner) if (o, i) != (0, 0)]
        self.steps = sorted(steps, key=lambda s: -(min(s[0], SIDE - s[0]) + min(s[1], inner - s[1])))
        self.sent = []

    def device(self, outer, inner):
        o = lax.rem(self.outer_at + SIDE + outer, SIDE)
        return o * self.inner + lax.rem(self.inner_at + self.inner + inner, self.inner)

    def copy(self, owner, place, to):
        ref = self.block(owner)
        return pltpu.make_async_remote_copy(
            src_ref=ref,
            dst_ref=ref,
            send_sem=self.send.at[place],
            recv_sem=self.recv.at[place],
            device_id={self.axis: to},
            device_id_type=MESH,
        )

    def start(self):
        for place, (outer, inner) in enumerate(self.steps):
            copy = self.copy(self.me, place, self.device(outer, inner))
            copy.start()
            self.sent.append(copy)

    def wait(self):
        for place, (outer, inner) in enumerate(self.steps):
            owner = self.device(-outer, -inner)
            self.copy(owner, place, owner).wait_recv()

    def finish(self):
        for copy in self.sent:
            copy.wait_send()


def body(
    points_ref,
    right_ref,
    listed_ref,
    count_ref,
    mid_pick_ref,
    top_pick_ref,
    mid_basis_ref,
    top_basis_ref,
    noise_ref,
    solution_ref,
    residual_ref,
    direction_ref,
    image_ref,
    step_ref,
    blocks,
    fields1,
    own3,
    smalls,
    roots,
    weights,
    tops,
    sums_leaf,
    sums_grp,
    basis,
    basis_high,
    basis_low,
    near_sum,
    image,
    term,
    kept,
    basis_sem,
    blocks_send,
    blocks_recv,
    smalls_send,
    smalls_recv,
    image0_send,
    image0_recv,
    image1_send,
    image1_recv,
    roots_send,
    roots_recv,
    weights_send,
    weights_recv,
    tops_send,
    tops_recv,
    sums_leaf_send,
    sums_leaf_recv,
    sums_grp_send,
    sums_grp_recv,
):
    me, grp = lax.axis_index("leaf"), lax.axis_index("grp")

    loads = [
        pltpu.make_async_copy(ref, basis.at[i], basis_sem.at[i])
        for i, ref in enumerate((mid_basis_ref, top_basis_ref))
    ]
    for load in loads:
        load.start()

    barrier = pltpu.get_barrier_semaphore()
    x, z = lax.div(me, SIDE), lax.rem(me, SIDE)
    beside = [{"leaf": lax.rem(x + step, SIDE) * SIDE + z} for step in (1, 3)]
    beside += [{"leaf": x * SIDE + lax.rem(z + step, SIDE)} for step in (1, 3)]
    beside += [{"grp": lax.rem(grp + step, N_GRP)} for step in range(1, N_GRP)]
    for device in beside:
        pl.semaphore_signal(barrier, inc=1, device_id=device, device_id_type=MESH)

    points = points_ref[...]
    right = right_ref[...]
    scale = self_scale(points)
    field = right * scale
    for slot in range(2):
        columns = slice(slot * LEAF, (slot + 1) * LEAF)
        blocks[2 * me + slot, 0:FEATURES] = points[:, columns]
        blocks[2 * me + slot, FEATURES:WIDE] = stacked(field[:, columns])
        own3[slot] = thirds(points[:, columns])

    pl.semaphore_wait(barrier, len(beside))

    def gathers(slot_of, send, recv, turn=0):
        return [
            Gather(half, me, lambda dev, half=half: slot_of(half, dev), send, recv, turn)
            for half in range(2)
        ]

    block_gathers = [
        gather
        for part in range(2)
        for gather in gathers(
            lambda half, dev, part=part: blocks.at[
                2 * dev + half, :, pl.ds(part * (LEAF // 2), LEAF // 2)
            ],
            blocks_send.at[part],
            blocks_recv.at[part],
            part,
        )
    ]
    small_gathers = gathers(lambda half, dev: smalls.at[half, dev], smalls_send, smalls_recv)
    image_gather = gathers(
        lambda half, dev: fields1.at[2 * dev + half], image0_send, image0_recv
    )[:1]
    image_exchange = Exchange(
        "leaf", N_LEAF, me, lambda dev: fields1.at[2 * dev + 1], image1_send, image1_recv
    )
    root_exchange = Exchange("grp", N_GRP, grp, lambda g: roots.at[g], roots_send, roots_recv)
    weight_exchange = Exchange(
        "leaf", N_LEAF, me, lambda dev: weights.at[dev], weights_send, weights_recv
    )
    top_exchange = Exchange("grp", N_GRP, grp, lambda g: tops.at[g], tops_send, tops_recv)
    leaf_exchange = Exchange(
        "leaf", N_LEAF, me, lambda dev: sums_leaf.at[dev], sums_leaf_send, sums_leaf_recv
    )
    grp_exchange = Exchange(
        "grp", N_GRP, grp, lambda g: sums_grp.at[g], sums_grp_send, sums_grp_recv
    )

    def step(gathered, *names):
        for name in names:
            for gather in gathered:
                getattr(gather, name)()

    def field_of(it, leaf):
        return blocks[leaf, FEATURES:WIDE, :] if it == 0 else fields1[leaf]

    def add_block(it, slot, place, rows_of, field16, weight):
        total = None
        for first in range(0, LEAF, CHUNK):
            rows = pl.ds(first, CHUNK)
            if it == 1 and place is not None:
                high, low = kept[place, 0, rows, :], kept[place, 1, rows, :]
            else:
                high, low = kernel_halves(rows_of(rows), own3[slot])
                if place is not None:
                    kept[place, 0, rows, :] = high
                    kept[place, 1, rows, :] = low
            part = applied(field16[:, first : first + CHUNK], high, low)
            total = part if total is None else total + part
        near_sum[slot] += total * weight

    def near_self(it, slot):
        near_sum[slot] = jnp.zeros((2 * TARGETS, LEAF), F32)
        base = slot * LEAF
        rows_of = lambda rows: points_ref[:, pl.ds(base + rows.start, rows.size)]
        field16 = field_of(it, 2 * me + slot)
        add_block(it, slot, None, rows_of, field16, count_ref[slot].astype(F32))

    def near_listed(it, slot, begin=1, end=SLOTS):
        count = count_ref[slot]

        def run(low_end, high_end, keep):
            def one(k, carried):
                leaf = listed_ref[slot, k]
                active = jnp.where(k < count, 1.0, 0.0).astype(F32)
                place = slot * (SLOTS - 1) + k - 1 if keep else None
                rows_of = lambda rows: blocks[leaf, 0:FEATURES, rows]
                add_block(it, slot, place, rows_of, field_of(it, leaf), active)
                return carried

            if low_end < high_end:
                lax.fori_loop(low_end, high_end, one, 0, unroll=True)

        limit = min(max(KEPT - slot * (SLOTS - 1) + 1, 1), SLOTS)
        run(begin, min(end, limit), True)
        run(max(begin, limit), end, False)

    def near(slot):
        return folded(near_sum[slot]) * (scale[:, slot * LEAF : (slot + 1) * LEAF] * LEAF**-0.5)

    def project(value):
        value16 = stacked(value)
        return folded(dot_nt(value16, basis_high[...]) + dot_nt(value16, basis_low[...]))

    def side_by_side(blocks):
        return jnp.concatenate(blocks, axis=1)

    def skeleton_image(coords_of, fields_of, count, columns3):
        total = jnp.zeros((2 * TARGETS, RANK), F32)
        for start in range(0, count, 4):
            rows = side_by_side([coords_of(start + i) for i in range(4)])
            field16 = side_by_side([fields_of(start + i) for i in range(4)])
            total = total + applied(field16, *kernel_halves(rows, columns3))
        return folded(total)

    step(block_gathers, "own")

    def picked(pick, base):
        found = jnp.zeros((FEATURES, RANK), F32)
        for start in range(0, BLOCK, CHUNK):
            rows = lax.broadcasted_iota(jnp.int32, (CHUNK, RANK), 0) + (base + start)
            chosen = jnp.where(rows == pick, 1.0, 0.0).astype(BF16)
            found = found + dot(points[:, start : start + CHUNK], chosen)
        return found.astype(BF16)

    own_mid = picked(mid_pick_ref[...], 0)
    mid3, mid_scale = thirds(own_mid), self_scale(own_mid)
    smalls[0, me, 0:FEATURES] = own_mid
    smalls[1, me, 0:FEATURES] = picked(top_pick_ref[...], me * BLOCK)

    for load in loads:
        load.wait()
    for i in range(2):
        for start in range(0, RANK, 64):
            high, low = halves(basis[i, start : start + 64, :])
            basis_high[i * RANK + start : i * RANK + start + 64, :] = high
            basis_low[i * RANK + start : i * RANK + start + 64, :] = low
    parts = project(right)
    smalls[0, me, FEATURES:WIDE] = stacked(parts[:, :RANK] * mid_scale)
    smalls[1, me, FEATURES:WIDE] = stacked(parts[:, RANK:])

    step(block_gathers, "near")
    step(small_gathers, "own")
    near_self(0, 0)
    step(block_gathers, "far")
    step(small_gathers, "near")
    near_self(0, 1)
    step(block_gathers, "last")
    step(small_gathers, "far")
    step(block_gathers, "arrive")

    def mid_image(fields_of):
        found = skeleton_image(
            lambda dev: smalls[0, dev, 0:FEATURES, :], fields_of, N_LEAF, mid3
        )
        return found * (mid_scale * RANK**-0.5)

    def expand(mid_part, fields_of):
        found = skeleton_image(
            lambda g: roots[g, 0:FEATURES, :], fields_of, N_GRP, root3
        )
        top_part = found * (root_scale * RANK**-0.5)
        image16 = stacked(side_by_side([mid_part, top_part]))
        for start in range(0, BLOCK, CHUNK):
            columns = slice(start, start + CHUNK)
            term[:, columns] = folded(
                applied(image16, basis_high[:, columns], basis_low[:, columns])
            )

    noise = noise_ref[0]

    def finished(value, slot):
        columns = slice(slot * LEAF, (slot + 1) * LEAF)
        return noise * value[:, columns] + near(slot) + term[:, columns]

    near_listed(0, 0, 1, 3)
    step(small_gathers, "last", "arrive")
    own_root, top = jnp.zeros((FEATURES, RANK), F32), jnp.zeros((2 * TARGETS, RANK), F32)
    for dev in range(N_LEAF):
        own_root = own_root + smalls[1, dev, 0:FEATURES, :].astype(F32)
        top = top + smalls[1, dev, FEATURES:WIDE, :].astype(F32)
    own_root = own_root.astype(BF16)
    root3, root_scale = thirds(own_root), self_scale(own_root)
    roots[grp, 0:FEATURES] = own_root
    roots[grp, FEATURES:WIDE] = stacked(folded(top) * root_scale)
    root_exchange.start()
    mid_part = mid_image(lambda dev: smalls[0, dev, FEATURES:WIDE, :])
    near_listed(0, 0, 3, SLOTS)
    root_exchange.wait()
    expand(mid_part, lambda g: roots[g, FEATURES:WIDE, :])

    def finish_image(slot):
        columns = slice(slot * LEAF, (slot + 1) * LEAF)
        found = finished(right, slot)
        image[:, columns] = found
        fields1[2 * me + slot] = stacked(found * scale[:, columns])

    finish_image(0)
    step(image_gather, "own")
    near_listed(0, 1, 1, 4)
    step(image_gather, "near")
    near_listed(0, 1, 4, 7)
    step(image_gather, "far")
    near_listed(0, 1, 7, SLOTS)
    finish_image(1)
    image_exchange.start()

    def summed(value):
        return jnp.sum(value, axis=1, keepdims=True)

    first_image = image[...]
    parts = project(first_image)
    lane = lax.broadcasted_iota(jnp.int32, (TARGETS, RANK), 1)
    weights[me, 0:8] = parts[:, :RANK] * mid_scale
    weights[me, 8:16] = parts[:, RANK:]
    weights[me, 16:24] = jnp.where(
        lane == 0,
        summed(right * right),
        jnp.where(lane == 1, summed(right * first_image), summed(first_image * first_image)),
    )
    weight_exchange.start()
    near_self(1, 0)
    step(image_gather, "last")
    near_self(1, 1)
    step(image_gather, "arrive")
    image_exchange.wait()
    near_listed(1, 0)
    weight_exchange.wait()
    sums = weights[0, 8:24]
    for dev in range(1, N_LEAF):
        sums = sums + weights[dev, 8:24]
    tops[grp, 0:8] = sums[0:8] * root_scale
    tops[grp, 8:16] = sums[8:16]
    top_exchange.start()
    mid_part = mid_image(lambda dev: stacked(weights[dev, 0:8]))
    near_listed(1, 1)
    top_exchange.wait()
    expand(mid_part, lambda g: stacked(tops[g, 0:8]))

    totals = tops[0, 8:16]
    for g in range(1, N_GRP):
        totals = totals + tops[g, 8:16]
    norm0, curve0, square0 = totals[:, 0:1], totals[:, 1:2], totals[:, 2:3]
    alpha = norm0 / curve0
    norm1 = norm0 - 2.0 * alpha * curve0 + alpha * alpha * square0
    beta = norm1 / norm0
    second_image = jnp.concatenate(
        [finished(first_image, slot) for slot in range(2)], axis=1
    )
    residual = right - alpha * first_image
    direction = residual + beta * right
    image1 = (1.0 + beta) * first_image - alpha * second_image
    solution_ref[...] = alpha * right
    residual_ref[...] = residual
    direction_ref[...] = direction
    image_ref[...] = image1

    diagonal = lax.broadcasted_iota(jnp.int32, (TARGETS, 128), 0) == lax.broadcasted_iota(
        jnp.int32, (TARGETS, 128), 1
    )
    curve1 = jnp.where(diagonal, summed(direction * image1), 0.0)
    sums_leaf[me] = jnp.sum(curve1, axis=0, keepdims=True)
    leaf_exchange.start()
    leaf_exchange.wait()
    total = sums_leaf[0]
    for dev in range(1, N_LEAF):
        total = total + sums_leaf[dev]
    sums_grp[grp] = total
    grp_exchange.start()
    grp_exchange.wait()
    total = sums_grp[0]
    for g in range(1, N_GRP):
        total = total + sums_grp[g]
    curve1 = summed(jnp.where(diagonal, total, 0.0))
    step_ref[...] = jnp.broadcast_to(norm1 / curve1, (TARGETS, BLOCK))

    for sender in (
        *block_gathers,
        *small_gathers,
        *image_gather,
        image_exchange,
        root_exchange,
        weight_exchange,
        top_exchange,
        leaf_exchange,
        grp_exchange,
    ):
        sender.finish()


def on_device(*operands):
    vmem, smem, anywhere = (
        pl.BlockSpec(memory_space=space) for space in (pltpu.VMEM, pltpu.SMEM, pl.ANY)
    )
    messages = 2 * len(LABELS)
    dma = pltpu.SemaphoreType.DMA
    out = jax.ShapeDtypeStruct((TARGETS, BLOCK), F32)
    solution1, residual1, direction, image1, step = pl.pallas_call(
        body,
        out_shape=(out,) * 5,
        in_specs=[vmem, vmem, smem, smem, vmem, vmem, anywhere, anywhere, smem],
        out_specs=(vmem,) * 5,
        scratch_shapes=[
            pltpu.VMEM((2 * N_LEAF, WIDE, LEAF), BF16),
            pltpu.VMEM((2 * N_LEAF, 2 * TARGETS, LEAF), BF16),
            pltpu.VMEM((2, 3 * FEATURES, LEAF), BF16),
            pltpu.VMEM((2, N_LEAF, WIDE, RANK), BF16),
            pltpu.VMEM((N_GRP, WIDE, RANK), BF16),
            pltpu.VMEM((N_LEAF, 3 * TARGETS, RANK), F32),
            pltpu.VMEM((N_GRP, 2 * TARGETS, RANK), F32),
            pltpu.VMEM((N_LEAF, 1, 128), F32),
            pltpu.VMEM((N_GRP, 1, 128), F32),
            pltpu.VMEM((2, RANK, BLOCK), F32),
            pltpu.VMEM((2 * RANK, BLOCK), BF16),
            pltpu.VMEM((2 * RANK, BLOCK), BF16),
            pltpu.VMEM((2, 2 * TARGETS, LEAF), F32),
            pltpu.VMEM((TARGETS, BLOCK), F32),
            pltpu.VMEM((TARGETS, BLOCK), F32),
            pltpu.VMEM((KEPT, 2, LEAF, LEAF), BF16),
            dma((2,)),
            dma((2, messages)),
            dma((2, messages)),
            dma((messages,)),
            dma((messages,)),
            dma((messages,)),
            dma((messages,)),
            dma((N_LEAF,)),
            dma((N_LEAF,)),
            dma((N_GRP,)),
            dma((N_GRP,)),
            dma((N_LEAF,)),
            dma((N_LEAF,)),
            dma((N_GRP,)),
            dma((N_GRP,)),
            dma((N_LEAF,)),
            dma((N_LEAF,)),
            dma((N_GRP,)),
            dma((N_GRP,)),
        ],
        compiler_params=pltpu.CompilerParams(
            collective_id=0, has_side_effects=True, vmem_limit_bytes=62 * 2**20
        ),
    )(*operands)
    return solution1 + step * direction, residual1 - step * image1


def solution(mesh):
    placed = (
        P(None, ("grp", "leaf")),
        P(None, ("grp", "leaf")),
        P(("grp", "leaf"), None),
        P(("grp", "leaf")),
        P(("grp", "leaf"), None),
        P("grp", None),
        P(None, ("grp", "leaf")),
        P(None, ("grp", "leaf")),
        P(),
    )
    return jax.shard_map(
        on_device,
        mesh=mesh,
        in_specs=placed,
        out_specs=(P(None, ("grp", "leaf")), P(None, ("grp", "leaf"))),
        check_vma=False,
    )
```

```python
import math

import jax
import jax.numpy as jnp
from jax import lax
from jax.experimental import pallas as pl
from jax.experimental.pallas import tpu as pltpu
from jax.sharding import PartitionSpec as P

FEATURES = 32
TARGETS = 8
WIDE = FEATURES + 2 * TARGETS
LEAF = 1024
RANK = 256
SLOTS = 8
SIDE = 4
N_LEAF = 16
N_GRP = 8
BLOCK = 2 * LEAF
CHUNK = 512
KEPT = 11
MESH = pl.DeviceIdType.MESH
F32 = jnp.float32
BF16 = jnp.bfloat16
SCALE = math.log2(math.e) / 16.0

LABELS = [(1, 0), (3, 0), (2, 0)] + [(df, ds) for df in range(4) for ds in (1, 3, 2)]
PLACE = {label: i for i, label in enumerate(LABELS)}


def dot(left, right):
    return jnp.dot(left, right, preferred_element_type=F32)


def dot_tn(left, right):
    return lax.dot_general(left, right, (((0,), (0,)), ((), ())), preferred_element_type=F32)


def dot_nt(left, right):
    return lax.dot_general(left, right, (((1,), (1,)), ((), ())), preferred_element_type=F32)


def halves(value):
    high = value.astype(BF16)
    return high, (value - high.astype(F32)).astype(BF16)


def stacked(value):
    high = value.astype(BF16).astype(F32)
    return jnp.concatenate([high, value - high], axis=0).astype(BF16)


def folded(value):
    return value[:TARGETS] + value[TARGETS:]


def thirds(coords):
    scaled = coords.astype(F32) * SCALE
    first = scaled.astype(BF16)
    rest = scaled - first.astype(F32)
    second = rest.astype(BF16)
    third = (rest - second.astype(F32)).astype(BF16)
    return jnp.concatenate([first, second, third], axis=0)


def self_scale(coords):
    wide = coords.astype(F32)
    return jnp.exp2(jnp.sum(wide * wide, axis=0, keepdims=True) * (-0.5 * SCALE))


def kernel_halves(rows, columns3):
    return halves(jnp.exp2(dot_tn(jnp.concatenate([rows, rows, rows], axis=0), columns3)))


def applied(field16, high, low):
    return dot(field16, high) + dot(field16, low)


class Gather:
    def __init__(self, half, me, slot, send, recv, turn=0):
        first, second = lax.div(me, SIDE), lax.rem(me, SIDE)
        if half == 1:
            first, second = second, first
        self.half, self.first, self.second = half, first, second
        self.slot, self.send, self.recv, self.turn = slot, send, recv, turn
        self.sent = []

    def device(self, df, ds):
        f = lax.rem(self.first + SIDE - df, SIDE)
        s = lax.rem(self.second + SIDE - ds, SIDE)
        return f * SIDE + s if self.half == 0 else s * SIDE + f

    def copy(self, mine, label, to):
        place = self.half * len(LABELS) + PLACE[label]
        ref = self.slot(self.device(*mine))
        return pltpu.make_async_remote_copy(
            src_ref=ref,
            dst_ref=ref,
            send_sem=self.send.at[place],
            recv_sem=self.recv.at[place],
            device_id={"leaf": to},
            device_id_type=MESH,
        )

    def push(self, mine, label, to):
        copy = self.copy(mine, label, to)
        copy.start()
        self.sent.append(copy)

    def wait(self, *labels):
        for label in labels:
            self.copy(label, label, self.device(1, 0)).wait_recv()

    def along_first(self, ahead):
        return self.device(3 if ahead else 1, 0)

    def along_second(self, ahead):
        return self.device(0, 3 if ahead else 1)

    def spread(self, df):
        self.push((df, 0), (df, 1), self.along_second(True))
        self.push((df, 0), (df, 3), self.along_second(False))

    def ahead(self, df):
        return (df + self.turn) % 2 == 0

    def relay(self, df):
        came = (df, 1 if self.ahead(df) else 3)
        self.wait(came)
        self.push(came, (df, 2), self.along_second(self.ahead(df)))

    def own(self):
        self.push((0, 0), (1, 0), self.along_first(True))
        self.push((0, 0), (3, 0), self.along_first(False))
        self.spread(0)

    def near(self):
        came, other = (1, 3) if self.turn == 0 else (3, 1)
        self.wait((came, 0))
        self.push((came, 0), (2, 0), self.along_first(self.turn == 0))
        self.spread(came)
        self.wait((other, 0))
        self.spread(other)
        self.relay(0)

    def far(self):
        self.wait((2, 0))
        self.spread(2)
        self.relay(1)
        self.relay(3)

    def last(self):
        self.relay(2)

    def arrive(self):
        for df in (0, 1, 3, 2):
            self.wait((df, 3 if self.ahead(df) else 1), (df, 2))

    def finish(self):
        for copy in self.sent:
            copy.wait_send()


class ShortGather(Gather):
    def own(self):
        self.push((0, 0), (2, 0), self.device(2, 0))
        super().own()

    def near(self):
        self.wait((1, 0))
        self.spread(1)
        self.wait((3, 0))
        self.spread(3)
        self.wait((2, 0))
        self.spread(2)
        self.relay(0)

    def far(self):
        for df in (1, 3, 2):
            self.relay(df)


class Exchange:
    def __init__(self, axis, size, me, block, send, recv):
        inner = size // SIDE
        self.axis, self.me, self.block = axis, me, block
        self.send, self.recv, self.inner = send, recv, inner
        self.outer_at, self.inner_at = lax.div(me, inner), lax.rem(me, inner)
        steps = [(o, i) for o in range(SIDE) for i in range(inner) if (o, i) != (0, 0)]
        self.steps = sorted(steps, key=lambda s: -(min(s[0], SIDE - s[0]) + min(s[1], inner - s[1])))
        self.sent = []

    def device(self, outer, inner):
        o = lax.rem(self.outer_at + SIDE + outer, SIDE)
        return o * self.inner + lax.rem(self.inner_at + self.inner + inner, self.inner)

    def copy(self, owner, place, to):
        ref = self.block(owner)
        return pltpu.make_async_remote_copy(
            src_ref=ref,
            dst_ref=ref,
            send_sem=self.send.at[place],
            recv_sem=self.recv.at[place],
            device_id={self.axis: to},
            device_id_type=MESH,
        )

    def start(self):
        for place, (outer, inner) in enumerate(self.steps):
            copy = self.copy(self.me, place, self.device(outer, inner))
            copy.start()
            self.sent.append(copy)

    def wait(self):
        for place, (outer, inner) in enumerate(self.steps):
            owner = self.device(-outer, -inner)
            self.copy(owner, place, owner).wait_recv()

    def finish(self):
        for copy in self.sent:
            copy.wait_send()


def body(
    points_ref,
    right_ref,
    listed_ref,
    count_ref,
    mid_pick_ref,
    top_pick_ref,
    mid_basis_ref,
    top_basis_ref,
    noise_ref,
    solution_ref,
    residual_ref,
    direction_ref,
    image_ref,
    step_ref,
    blocks,
    fields1,
    own3,
    smalls,
    roots,
    weights,
    tops,
    sums_leaf,
    sums_grp,
    basis,
    basis_high,
    basis_low,
    near_sum,
    image,
    term,
    kept,
    basis_sem,
    blocks_send,
    blocks_recv,
    smalls_send,
    smalls_recv,
    image0_send,
    image0_recv,
    image1_send,
    image1_recv,
    roots_send,
    roots_recv,
    weights_send,
    weights_recv,
    tops_send,
    tops_recv,
    sums_leaf_send,
    sums_leaf_recv,
    sums_grp_send,
    sums_grp_recv,
):
    me, grp = lax.axis_index("leaf"), lax.axis_index("grp")

    loads = [
        pltpu.make_async_copy(ref, basis.at[i], basis_sem.at[i])
        for i, ref in enumerate((mid_basis_ref, top_basis_ref))
    ]
    for load in loads:
        load.start()

    barrier = pltpu.get_barrier_semaphore()
    x, z = lax.div(me, SIDE), lax.rem(me, SIDE)
    beside = [{"leaf": lax.rem(x + step, SIDE) * SIDE + z} for step in (1, 3)]
    beside += [{"leaf": x * SIDE + lax.rem(z + step, SIDE)} for step in (1, 3)]
    beside += [{"grp": lax.rem(grp + step, N_GRP)} for step in range(1, N_GRP)]
    for device in beside:
        pl.semaphore_signal(barrier, inc=1, device_id=device, device_id_type=MESH)

    points = points_ref[...]
    right = right_ref[...]
    scale = self_scale(points)
    field = right * scale
    for slot in range(2):
        columns = slice(slot * LEAF, (slot + 1) * LEAF)
        blocks[2 * me + slot, 0:FEATURES] = points[:, columns]
        blocks[2 * me + slot, FEATURES:WIDE] = stacked(field[:, columns])
        own3[slot] = thirds(points[:, columns])

    pl.semaphore_wait(barrier, len(beside))

    def gathers(slot_of, send, recv, turn=0, kind=Gather):
        return [
            kind(half, me, lambda dev, half=half: slot_of(half, dev), send, recv, turn)
            for half in range(2)
        ]

    block_gathers = [
        gather
        for part in range(2)
        for gather in gathers(
            lambda half, dev, part=part: blocks.at[
                2 * dev + half, :, pl.ds(part * (LEAF // 2), LEAF // 2)
            ],
            blocks_send.at[part],
            blocks_recv.at[part],
            part,
        )
    ]
    small_gathers = gathers(
        lambda half, dev: smalls.at[half, dev], smalls_send, smalls_recv, kind=ShortGather
    )
    image_gather = gathers(
        lambda half, dev: fields1.at[2 * dev + half], image0_send, image0_recv, kind=ShortGather
    )[:1]
    image_exchange = Exchange(
        "leaf", N_LEAF, me, lambda dev: fields1.at[2 * dev + 1], image1_send, image1_recv
    )
    root_exchange = Exchange("grp", N_GRP, grp, lambda g: roots.at[g], roots_send, roots_recv)
    weight_exchange = Exchange(
        "leaf", N_LEAF, me, lambda dev: weights.at[dev], weights_send, weights_recv
    )
    top_exchange = Exchange("grp", N_GRP, grp, lambda g: tops.at[g], tops_send, tops_recv)
    leaf_exchange = Exchange(
        "leaf", N_LEAF, me, lambda dev: sums_leaf.at[dev], sums_leaf_send, sums_leaf_recv
    )
    grp_exchange = Exchange(
        "grp", N_GRP, grp, lambda g: sums_grp.at[g], sums_grp_send, sums_grp_recv
    )

    def step(gathered, *names):
        for name in names:
            for gather in gathered:
                getattr(gather, name)()

    def field_of(it, leaf):
        return blocks[leaf, FEATURES:WIDE, :] if it == 0 else fields1[leaf]

    def add_block(it, slot, place, rows_of, field16, weight):
        total = None
        for first in range(0, LEAF, CHUNK):
            rows = pl.ds(first, CHUNK)
            if it == 1 and place is not None:
                high, low = kept[place, 0, rows, :], kept[place, 1, rows, :]
            else:
                high, low = kernel_halves(rows_of(rows), own3[slot])
                if place is not None:
                    kept[place, 0, rows, :] = high
                    kept[place, 1, rows, :] = low
            part = applied(field16[:, first : first + CHUNK], high, low)
            total = part if total is None else total + part
        near_sum[slot] += total * weight

    def near_self(it, slot):
        near_sum[slot] = jnp.zeros((2 * TARGETS, LEAF), F32)
        base = slot * LEAF
        rows_of = lambda rows: points_ref[:, pl.ds(base + rows.start, rows.size)]
        field16 = field_of(it, 2 * me + slot)
        add_block(it, slot, None, rows_of, field16, count_ref[slot].astype(F32))

    def near_listed(it, slot, begin=1, end=SLOTS):
        count = count_ref[slot]

        def run(low_end, high_end, keep):
            def one(k, carried):
                leaf = listed_ref[slot, k]
                active = jnp.where(k < count, 1.0, 0.0).astype(F32)
                place = slot * (SLOTS - 1) + k - 1 if keep else None
                rows_of = lambda rows: blocks[leaf, 0:FEATURES, rows]
                add_block(it, slot, place, rows_of, field_of(it, leaf), active)
                return carried

            if low_end < high_end:
                lax.fori_loop(low_end, high_end, one, 0, unroll=True)

        limit = min(max(KEPT - slot * (SLOTS - 1) + 1, 1), SLOTS)
        run(begin, min(end, limit), True)
        run(max(begin, limit), end, False)

    def near(slot):
        return folded(near_sum[slot]) * (scale[:, slot * LEAF : (slot + 1) * LEAF] * LEAF**-0.5)

    def project(value):
        value16 = stacked(value)
        return folded(dot_nt(value16, basis_high[...]) + dot_nt(value16, basis_low[...]))

    def side_by_side(blocks):
        return jnp.concatenate(blocks, axis=1)

    def skeleton_image(coords_of, fields_of, count, columns3):
        total = jnp.zeros((2 * TARGETS, RANK), F32)
        for start in range(0, count, 4):
            rows = side_by_side([coords_of(start + i) for i in range(4)])
            field16 = side_by_side([fields_of(start + i) for i in range(4)])
            total = total + applied(field16, *kernel_halves(rows, columns3))
        return folded(total)

    step(block_gathers, "own")

    def picked(pick, base):
        found = jnp.zeros((FEATURES, RANK), F32)
        for start in range(0, BLOCK, CHUNK):
            rows = lax.broadcasted_iota(jnp.int32, (CHUNK, RANK), 0) + (base + start)
            chosen = jnp.where(rows == pick, 1.0, 0.0).astype(BF16)
            found = found + dot(points[:, start : start + CHUNK], chosen)
        return found.astype(BF16)

    own_mid = picked(mid_pick_ref[...], 0)
    mid3, mid_scale = thirds(own_mid), self_scale(own_mid)
    smalls[0, me, 0:FEATURES] = own_mid
    smalls[1, me, 0:FEATURES] = picked(top_pick_ref[...], me * BLOCK)

    for load in loads:
        load.wait()
    for i in range(2):
        for start in range(0, RANK, 64):
            high, low = halves(basis[i, start : start + 64, :])
            basis_high[i * RANK + start : i * RANK + start + 64, :] = high
            basis_low[i * RANK + start : i * RANK + start + 64, :] = low
    parts = project(right)
    smalls[0, me, FEATURES:WIDE] = stacked(parts[:, :RANK] * mid_scale)
    smalls[1, me, FEATURES:WIDE] = stacked(parts[:, RANK:])

    step(block_gathers, "near")
    step(small_gathers, "own")
    near_self(0, 0)
    step(block_gathers, "far")
    step(small_gathers, "near")
    near_self(0, 1)
    step(block_gathers, "last")
    step(small_gathers, "far")
    step(block_gathers, "arrive")

    def mid_image(fields_of):
        found = skeleton_image(
            lambda dev: smalls[0, dev, 0:FEATURES, :], fields_of, N_LEAF, mid3
        )
        return found * (mid_scale * RANK**-0.5)

    def expand(mid_part, fields_of):
        found = skeleton_image(
            lambda g: roots[g, 0:FEATURES, :], fields_of, N_GRP, root3
        )
        top_part = found * (root_scale * RANK**-0.5)
        image16 = stacked(side_by_side([mid_part, top_part]))
        for start in range(0, BLOCK, CHUNK):
            columns = slice(start, start + CHUNK)
            term[:, columns] = folded(
                applied(image16, basis_high[:, columns], basis_low[:, columns])
            )

    noise = noise_ref[0]

    def finished(value, slot):
        columns = slice(slot * LEAF, (slot + 1) * LEAF)
        return noise * value[:, columns] + near(slot) + term[:, columns]

    near_listed(0, 0, 1, 3)
    step(small_gathers, "arrive")
    own_root, top = jnp.zeros((FEATURES, RANK), F32), jnp.zeros((2 * TARGETS, RANK), F32)
    for dev in range(N_LEAF):
        own_root = own_root + smalls[1, dev, 0:FEATURES, :].astype(F32)
        top = top + smalls[1, dev, FEATURES:WIDE, :].astype(F32)
    own_root = own_root.astype(BF16)
    root3, root_scale = thirds(own_root), self_scale(own_root)
    roots[grp, 0:FEATURES] = own_root
    roots[grp, FEATURES:WIDE] = stacked(folded(top) * root_scale)
    root_exchange.start()
    mid_part = mid_image(lambda dev: smalls[0, dev, FEATURES:WIDE, :])
    near_listed(0, 0, 3, SLOTS)
    root_exchange.wait()
    expand(mid_part, lambda g: roots[g, FEATURES:WIDE, :])

    def finish_image(slot):
        columns = slice(slot * LEAF, (slot + 1) * LEAF)
        found = finished(right, slot)
        image[:, columns] = found
        fields1[2 * me + slot] = stacked(found * scale[:, columns])

    finish_image(0)
    step(image_gather, "own")
    near_listed(0, 1, 1, 5)
    step(image_gather, "near")
    near_listed(0, 1, 5, SLOTS)
    finish_image(1)
    step(image_gather, "far")
    image_exchange.start()

    def summed(value):
        return jnp.sum(value, axis=1, keepdims=True)

    first_image = image[...]
    parts = project(first_image)
    lane = lax.broadcasted_iota(jnp.int32, (TARGETS, RANK), 1)
    weights[me, 0:8] = parts[:, :RANK] * mid_scale
    weights[me, 8:16] = parts[:, RANK:]
    weights[me, 16:24] = jnp.where(
        lane == 0,
        summed(right * right),
        jnp.where(lane == 1, summed(right * first_image), summed(first_image * first_image)),
    )
    weight_exchange.start()
    near_self(1, 0)
    near_self(1, 1)
    step(image_gather, "arrive")
    image_exchange.wait()
    near_listed(1, 0)
    weight_exchange.wait()
    sums = weights[0, 8:24]
    for dev in range(1, N_LEAF):
        sums = sums + weights[dev, 8:24]
    tops[grp, 0:8] = sums[0:8] * root_scale
    tops[grp, 8:16] = sums[8:16]
    top_exchange.start()
    mid_part = mid_image(lambda dev: stacked(weights[dev, 0:8]))
    near_listed(1, 1)
    top_exchange.wait()
    expand(mid_part, lambda g: stacked(tops[g, 0:8]))

    totals = tops[0, 8:16]
    for g in range(1, N_GRP):
        totals = totals + tops[g, 8:16]
    norm0, curve0, square0 = totals[:, 0:1], totals[:, 1:2], totals[:, 2:3]
    alpha = norm0 / curve0
    norm1 = norm0 - 2.0 * alpha * curve0 + alpha * alpha * square0
    beta = norm1 / norm0
    second_image = jnp.concatenate(
        [finished(first_image, slot) for slot in range(2)], axis=1
    )
    residual = right - alpha * first_image
    direction = residual + beta * right
    image1 = (1.0 + beta) * first_image - alpha * second_image
    solution_ref[...] = alpha * right
    residual_ref[...] = residual
    direction_ref[...] = direction
    image_ref[...] = image1

    diagonal = lax.broadcasted_iota(jnp.int32, (TARGETS, 128), 0) == lax.broadcasted_iota(
        jnp.int32, (TARGETS, 128), 1
    )
    curve1 = jnp.where(diagonal, summed(direction * image1), 0.0)
    sums_leaf[me] = jnp.sum(curve1, axis=0, keepdims=True)
    leaf_exchange.start()
    leaf_exchange.wait()
    total = sums_leaf[0]
    for dev in range(1, N_LEAF):
        total = total + sums_leaf[dev]
    sums_grp[grp] = total
    grp_exchange.start()
    grp_exchange.wait()
    total = sums_grp[0]
    for g in range(1, N_GRP):
        total = total + sums_grp[g]
    curve1 = summed(jnp.where(diagonal, total, 0.0))
    step_ref[...] = jnp.broadcast_to(norm1 / curve1, (TARGETS, BLOCK))

    for sender in (
        *block_gathers,
        *small_gathers,
        *image_gather,
        image_exchange,
        root_exchange,
        weight_exchange,
        top_exchange,
        leaf_exchange,
        grp_exchange,
    ):
        sender.finish()


def on_device(*operands):
    vmem, smem, anywhere = (
        pl.BlockSpec(memory_space=space) for space in (pltpu.VMEM, pltpu.SMEM, pl.ANY)
    )
    messages = 2 * len(LABELS)
    dma = pltpu.SemaphoreType.DMA
    out = jax.ShapeDtypeStruct((TARGETS, BLOCK), F32)
    solution1, residual1, direction, image1, step = pl.pallas_call(
        body,
        out_shape=(out,) * 5,
        in_specs=[vmem, vmem, smem, smem, vmem, vmem, anywhere, anywhere, smem],
        out_specs=(vmem,) * 5,
        scratch_shapes=[
            pltpu.VMEM((2 * N_LEAF, WIDE, LEAF), BF16),
            pltpu.VMEM((2 * N_LEAF, 2 * TARGETS, LEAF), BF16),
            pltpu.VMEM((2, 3 * FEATURES, LEAF), BF16),
            pltpu.VMEM((2, N_LEAF, WIDE, RANK), BF16),
            pltpu.VMEM((N_GRP, WIDE, RANK), BF16),
            pltpu.VMEM((N_LEAF, 3 * TARGETS, RANK), F32),
            pltpu.VMEM((N_GRP, 2 * TARGETS, RANK), F32),
            pltpu.VMEM((N_LEAF, 1, 128), F32),
            pltpu.VMEM((N_GRP, 1, 128), F32),
            pltpu.VMEM((2, RANK, BLOCK), F32),
            pltpu.VMEM((2 * RANK, BLOCK), BF16),
            pltpu.VMEM((2 * RANK, BLOCK), BF16),
            pltpu.VMEM((2, 2 * TARGETS, LEAF), F32),
            pltpu.VMEM((TARGETS, BLOCK), F32),
            pltpu.VMEM((TARGETS, BLOCK), F32),
            pltpu.VMEM((KEPT, 2, LEAF, LEAF), BF16),
            dma((2,)),
            dma((2, messages)),
            dma((2, messages)),
            dma((messages,)),
            dma((messages,)),
            dma((messages,)),
            dma((messages,)),
            dma((N_LEAF,)),
            dma((N_LEAF,)),
            dma((N_GRP,)),
            dma((N_GRP,)),
            dma((N_LEAF,)),
            dma((N_LEAF,)),
            dma((N_GRP,)),
            dma((N_GRP,)),
            dma((N_LEAF,)),
            dma((N_LEAF,)),
            dma((N_GRP,)),
            dma((N_GRP,)),
        ],
        compiler_params=pltpu.CompilerParams(
            collective_id=0, has_side_effects=True, vmem_limit_bytes=62 * 2**20
        ),
    )(*operands)
    return solution1 + step * direction, residual1 - step * image1


def solution(mesh):
    placed = (
        P(None, ("grp", "leaf")),
        P(None, ("grp", "leaf")),
        P(("grp", "leaf"), None),
        P(("grp", "leaf")),
        P(("grp", "leaf"), None),
        P("grp", None),
        P(None, ("grp", "leaf")),
        P(None, ("grp", "leaf")),
        P(),
    )
    return jax.shard_map(
        on_device,
        mesh=mesh,
        in_specs=placed,
        out_specs=(P(None, ("grp", "leaf")), P(None, ("grp", "leaf"))),
        check_vma=False,
    )
```

```python
import math

import jax
import jax.numpy as jnp
from jax import lax
from jax.experimental import pallas as pl
from jax.experimental.pallas import tpu as pltpu
from jax.sharding import PartitionSpec as P

FEATURES = 32
TARGETS = 8
WIDE = FEATURES + 2 * TARGETS
LEAF = 1024
RANK = 256
SLOTS = 8
SIDE = 4
N_LEAF = 16
N_GRP = 8
BLOCK = 2 * LEAF
CHUNK = 512
KEPT = 11
MESH = pl.DeviceIdType.MESH
F32 = jnp.float32
BF16 = jnp.bfloat16
SCALE = math.log2(math.e) / 16.0

LABELS = [(1, 0), (3, 0), (2, 0)] + [(df, ds) for df in range(4) for ds in (1, 3, 2)]
PLACE = {label: i for i, label in enumerate(LABELS)}


def dot(left, right):
    return jnp.dot(left, right, preferred_element_type=F32)


def dot_tn(left, right):
    return lax.dot_general(left, right, (((0,), (0,)), ((), ())), preferred_element_type=F32)


def dot_nt(left, right):
    return lax.dot_general(left, right, (((1,), (1,)), ((), ())), preferred_element_type=F32)


def halves(value):
    high = value.astype(BF16)
    return high, (value - high.astype(F32)).astype(BF16)


def stacked(value):
    high = value.astype(BF16).astype(F32)
    return jnp.concatenate([high, value - high], axis=0).astype(BF16)


def folded(value):
    return value[:TARGETS] + value[TARGETS:]


def thirds(coords):
    scaled = coords.astype(F32) * SCALE
    first = scaled.astype(BF16)
    rest = scaled - first.astype(F32)
    second = rest.astype(BF16)
    third = (rest - second.astype(F32)).astype(BF16)
    return jnp.concatenate([first, second, third], axis=0)


def self_scale(coords):
    wide = coords.astype(F32)
    return jnp.exp2(jnp.sum(wide * wide, axis=0, keepdims=True) * (-0.5 * SCALE))


def kernel_halves(rows, columns3):
    return halves(jnp.exp2(dot_tn(jnp.concatenate([rows, rows, rows], axis=0), columns3)))


def applied(field16, high, low):
    return dot(field16, high) + dot(field16, low)


class Gather:
    def __init__(self, half, me, slot, send, recv, turn=0):
        first, second = lax.div(me, SIDE), lax.rem(me, SIDE)
        if half == 1:
            first, second = second, first
        self.half, self.first, self.second = half, first, second
        self.slot, self.send, self.recv, self.turn = slot, send, recv, turn
        self.sent = []

    def device(self, df, ds):
        f = lax.rem(self.first + SIDE - df, SIDE)
        s = lax.rem(self.second + SIDE - ds, SIDE)
        return f * SIDE + s if self.half == 0 else s * SIDE + f

    def copy(self, mine, label, to):
        place = self.half * len(LABELS) + PLACE[label]
        ref = self.slot(self.device(*mine))
        return pltpu.make_async_remote_copy(
            src_ref=ref,
            dst_ref=ref,
            send_sem=self.send.at[place],
            recv_sem=self.recv.at[place],
            device_id={"leaf": to},
            device_id_type=MESH,
        )

    def push(self, mine, label, to):
        copy = self.copy(mine, label, to)
        copy.start()
        self.sent.append(copy)

    def wait(self, *labels):
        for label in labels:
            self.copy(label, label, self.device(1, 0)).wait_recv()

    def along_first(self, ahead):
        return self.device(3 if ahead else 1, 0)

    def along_second(self, ahead):
        return self.device(0, 3 if ahead else 1)

    def spread(self, df):
        self.push((df, 0), (df, 1), self.along_second(True))
        self.push((df, 0), (df, 3), self.along_second(False))

    def ahead(self, df):
        return (df + self.turn) % 2 == 0

    def relay(self, df):
        came = (df, 1 if self.ahead(df) else 3)
        self.wait(came)
        self.push(came, (df, 2), self.along_second(self.ahead(df)))

    def own(self):
        self.push((0, 0), (1, 0), self.along_first(True))
        self.push((0, 0), (3, 0), self.along_first(False))
        self.spread(0)

    def near(self):
        came, other = (1, 3) if self.turn == 0 else (3, 1)
        self.wait((came, 0))
        self.push((came, 0), (2, 0), self.along_first(self.turn == 0))
        self.spread(came)
        self.wait((other, 0))
        self.spread(other)
        self.relay(0)

    def far(self):
        self.wait((2, 0))
        self.spread(2)
        self.relay(1)
        self.relay(3)

    def last(self):
        self.relay(2)

    def arrive(self):
        for df in (0, 1, 3, 2):
            self.wait((df, 3 if self.ahead(df) else 1), (df, 2))

    def finish(self):
        for copy in self.sent:
            copy.wait_send()


class ShortGather(Gather):
    def own(self):
        self.push((0, 0), (2, 0), self.device(2, 0))
        super().own()

    def near(self):
        self.wait((1, 0))
        self.spread(1)
        self.wait((3, 0))
        self.spread(3)
        self.wait((2, 0))
        self.spread(2)
        self.relay(0)

    def far(self):
        for df in (1, 3, 2):
            self.relay(df)


class Exchange:
    def __init__(self, axis, size, me, block, send, recv):
        inner = size // SIDE
        self.axis, self.me, self.block = axis, me, block
        self.send, self.recv, self.inner = send, recv, inner
        self.outer_at, self.inner_at = lax.div(me, inner), lax.rem(me, inner)
        steps = [(o, i) for o in range(SIDE) for i in range(inner) if (o, i) != (0, 0)]
        self.steps = sorted(steps, key=lambda s: -(min(s[0], SIDE - s[0]) + min(s[1], inner - s[1])))
        self.sent = []

    def device(self, outer, inner):
        o = lax.rem(self.outer_at + SIDE + outer, SIDE)
        return o * self.inner + lax.rem(self.inner_at + self.inner + inner, self.inner)

    def copy(self, owner, place, to):
        ref = self.block(owner)
        return pltpu.make_async_remote_copy(
            src_ref=ref,
            dst_ref=ref,
            send_sem=self.send.at[place],
            recv_sem=self.recv.at[place],
            device_id={self.axis: to},
            device_id_type=MESH,
        )

    def start(self):
        for place, (outer, inner) in enumerate(self.steps):
            copy = self.copy(self.me, place, self.device(outer, inner))
            copy.start()
            self.sent.append(copy)

    def wait(self):
        for place, (outer, inner) in enumerate(self.steps):
            owner = self.device(-outer, -inner)
            self.copy(owner, place, owner).wait_recv()

    def finish(self):
        for copy in self.sent:
            copy.wait_send()


def body(
    points_ref,
    right_ref,
    listed_ref,
    count_ref,
    mid_pick_ref,
    top_pick_ref,
    mid_basis_ref,
    top_basis_ref,
    noise_ref,
    solution_ref,
    residual_ref,
    direction_ref,
    image_ref,
    step_ref,
    blocks,
    fields1,
    own3,
    smalls,
    roots,
    weights,
    tops,
    sums_leaf,
    sums_grp,
    basis,
    basis_high,
    basis_low,
    near_sum,
    image,
    term,
    kept,
    basis_sem,
    blocks_send,
    blocks_recv,
    smalls_send,
    smalls_recv,
    image0_send,
    image0_recv,
    image1_send,
    image1_recv,
    roots_send,
    roots_recv,
    weights_send,
    weights_recv,
    tops_send,
    tops_recv,
    sums_leaf_send,
    sums_leaf_recv,
    sums_grp_send,
    sums_grp_recv,
):
    me, grp = lax.axis_index("leaf"), lax.axis_index("grp")

    loads = [
        pltpu.make_async_copy(ref, basis.at[i], basis_sem.at[i])
        for i, ref in enumerate((mid_basis_ref, top_basis_ref))
    ]
    for load in loads:
        load.start()

    barrier = pltpu.get_barrier_semaphore()
    x, z = lax.div(me, SIDE), lax.rem(me, SIDE)
    beside = [{"leaf": lax.rem(x + step, SIDE) * SIDE + z} for step in (1, 3)]
    beside += [{"leaf": x * SIDE + lax.rem(z + step, SIDE)} for step in (1, 3)]
    beside += [{"grp": lax.rem(grp + step, N_GRP)} for step in range(1, N_GRP)]
    for device in beside:
        pl.semaphore_signal(barrier, inc=1, device_id=device, device_id_type=MESH)

    points = points_ref[...]
    right = right_ref[...]
    scale = self_scale(points)
    field = right * scale
    for slot in range(2):
        columns = slice(slot * LEAF, (slot + 1) * LEAF)
        blocks[2 * me + slot, 0:FEATURES] = points[:, columns]
        blocks[2 * me + slot, FEATURES:WIDE] = stacked(field[:, columns])
        own3[slot] = thirds(points[:, columns])

    pl.semaphore_wait(barrier, len(beside))

    def gathers(slot_of, send, recv, turn=0, kind=Gather):
        return [
            kind(half, me, lambda dev, half=half: slot_of(half, dev), send, recv, turn)
            for half in range(2)
        ]

    block_gathers = [
        gather
        for part in range(2)
        for gather in gathers(
            lambda half, dev, part=part: blocks.at[
                2 * dev + half, :, pl.ds(part * (LEAF // 2), LEAF // 2)
            ],
            blocks_send.at[part],
            blocks_recv.at[part],
            part,
        )
    ]
    small_gathers = gathers(
        lambda half, dev: smalls.at[half, dev], smalls_send, smalls_recv, kind=ShortGather
    )
    image_gather = gathers(
        lambda half, dev: fields1.at[2 * dev + half], image0_send, image0_recv, kind=ShortGather
    )[:1]
    image_exchange = Exchange(
        "leaf", N_LEAF, me, lambda dev: fields1.at[2 * dev + 1], image1_send, image1_recv
    )
    root_exchange = Exchange("grp", N_GRP, grp, lambda g: roots.at[g], roots_send, roots_recv)
    weight_exchange = Exchange(
        "leaf", N_LEAF, me, lambda dev: weights.at[dev], weights_send, weights_recv
    )
    top_exchange = Exchange("grp", N_GRP, grp, lambda g: tops.at[g], tops_send, tops_recv)
    leaf_exchange = Exchange(
        "leaf", N_LEAF, me, lambda dev: sums_leaf.at[dev], sums_leaf_send, sums_leaf_recv
    )
    grp_exchange = Exchange(
        "grp", N_GRP, grp, lambda g: sums_grp.at[g], sums_grp_send, sums_grp_recv
    )

    def step(gathered, *names):
        for name in names:
            for gather in gathered:
                getattr(gather, name)()

    def field_of(it, leaf):
        return blocks[leaf, FEATURES:WIDE, :] if it == 0 else fields1[leaf]

    def add_block(it, slot, place, rows_of, field16, weight):
        total = None
        for first in range(0, LEAF, CHUNK):
            rows = pl.ds(first, CHUNK)
            if it == 1 and place is not None:
                high, low = kept[place, 0, rows, :], kept[place, 1, rows, :]
            else:
                high, low = kernel_halves(rows_of(rows), own3[slot])
                if place is not None:
                    kept[place, 0, rows, :] = high
                    kept[place, 1, rows, :] = low
            part = applied(field16[:, first : first + CHUNK], high, low)
            total = part if total is None else total + part
        near_sum[slot] += total * weight

    def near_self(it, slot):
        near_sum[slot] = jnp.zeros((2 * TARGETS, LEAF), F32)
        base = slot * LEAF
        rows_of = lambda rows: points_ref[:, pl.ds(base + rows.start, rows.size)]
        field16 = field_of(it, 2 * me + slot)
        add_block(it, slot, None, rows_of, field16, count_ref[slot].astype(F32))

    def near_listed(it, slot, begin=1, end=SLOTS):
        count = count_ref[slot]

        def run(low_end, high_end, keep):
            def one(k, carried):
                leaf = listed_ref[slot, k]
                active = jnp.where(k < count, 1.0, 0.0).astype(F32)
                place = slot * (SLOTS - 1) + k - 1 if keep else None
                rows_of = lambda rows: blocks[leaf, 0:FEATURES, rows]
                add_block(it, slot, place, rows_of, field_of(it, leaf), active)
                return carried

            if low_end < high_end:
                lax.fori_loop(low_end, high_end, one, 0, unroll=True)

        limit = min(max(KEPT - slot * (SLOTS - 1) + 1, 1), SLOTS)
        run(begin, min(end, limit), True)
        run(max(begin, limit), end, False)

    def near(slot):
        return folded(near_sum[slot]) * (scale[:, slot * LEAF : (slot + 1) * LEAF] * LEAF**-0.5)

    def project(value):
        value16 = stacked(value)
        return folded(dot_nt(value16, basis_high[...]) + dot_nt(value16, basis_low[...]))

    def side_by_side(blocks):
        return jnp.concatenate(blocks, axis=1)

    def skeleton_image(coords_of, fields_of, count, columns3):
        total = jnp.zeros((2 * TARGETS, RANK), F32)
        for start in range(0, count, 4):
            rows = side_by_side([coords_of(start + i) for i in range(4)])
            field16 = side_by_side([fields_of(start + i) for i in range(4)])
            total = total + applied(field16, *kernel_halves(rows, columns3))
        return folded(total)

    step(block_gathers, "own")

    def picked(pick, base):
        found = jnp.zeros((FEATURES, RANK), F32)
        for start in range(0, BLOCK, CHUNK):
            rows = lax.broadcasted_iota(jnp.int32, (CHUNK, RANK), 0) + (base + start)
            chosen = jnp.where(rows == pick, 1.0, 0.0).astype(BF16)
            found = found + dot(points[:, start : start + CHUNK], chosen)
        return found.astype(BF16)

    own_mid = picked(mid_pick_ref[...], 0)
    mid3, mid_scale = thirds(own_mid), self_scale(own_mid)
    smalls[0, me, 0:FEATURES] = own_mid
    smalls[1, me, 0:FEATURES] = picked(top_pick_ref[...], me * BLOCK)

    for load in loads:
        load.wait()
    for i in range(2):
        for start in range(0, RANK, 64):
            high, low = halves(basis[i, start : start + 64, :])
            basis_high[i * RANK + start : i * RANK + start + 64, :] = high
            basis_low[i * RANK + start : i * RANK + start + 64, :] = low
    parts = project(right)
    smalls[0, me, FEATURES:WIDE] = stacked(parts[:, :RANK] * mid_scale)
    smalls[1, me, FEATURES:WIDE] = stacked(parts[:, RANK:])

    step(block_gathers, "near")
    step(small_gathers, "own")
    near_self(0, 0)
    step(block_gathers, "far")
    step(small_gathers, "near")
    near_self(0, 1)
    step(block_gathers, "last")
    step(small_gathers, "far")
    step(block_gathers, "arrive")

    def mid_image(fields_of):
        found = skeleton_image(
            lambda dev: smalls[0, dev, 0:FEATURES, :], fields_of, N_LEAF, mid3
        )
        return found * (mid_scale * RANK**-0.5)

    def expand(mid_part, fields_of):
        found = skeleton_image(
            lambda g: roots[g, 0:FEATURES, :], fields_of, N_GRP, root3
        )
        top_part = found * (root_scale * RANK**-0.5)
        image16 = stacked(side_by_side([mid_part, top_part]))
        for start in range(0, BLOCK, CHUNK):
            columns = slice(start, start + CHUNK)
            term[:, columns] = folded(
                applied(image16, basis_high[:, columns], basis_low[:, columns])
            )

    noise = noise_ref[0]

    def finished(value, slot):
        columns = slice(slot * LEAF, (slot + 1) * LEAF)
        return noise * value[:, columns] + near(slot) + term[:, columns]

    near_listed(0, 0, 1, 3)
    step(small_gathers, "arrive")
    own_root, top = jnp.zeros((FEATURES, RANK), F32), jnp.zeros((2 * TARGETS, RANK), F32)
    for dev in range(N_LEAF):
        own_root = own_root + smalls[1, dev, 0:FEATURES, :].astype(F32)
        top = top + smalls[1, dev, FEATURES:WIDE, :].astype(F32)
    own_root = own_root.astype(BF16)
    root3, root_scale = thirds(own_root), self_scale(own_root)
    roots[grp, 0:FEATURES] = own_root
    roots[grp, FEATURES:WIDE] = stacked(folded(top) * root_scale)
    root_exchange.start()
    mid_part = mid_image(lambda dev: smalls[0, dev, FEATURES:WIDE, :])
    near_listed(0, 0, 3, SLOTS)
    root_exchange.wait()
    expand(mid_part, lambda g: roots[g, FEATURES:WIDE, :])

    def finish_image(slot):
        columns = slice(slot * LEAF, (slot + 1) * LEAF)
        found = finished(right, slot)
        image[:, columns] = found
        fields1[2 * me + slot] = stacked(found * scale[:, columns])

    finish_image(0)
    step(image_gather, "own")
    near_listed(0, 1, 1, 5)
    step(image_gather, "near")
    near_listed(0, 1, 5, SLOTS)
    finish_image(1)
    step(image_gather, "far")
    image_exchange.start()

    def summed(value):
        return jnp.sum(value, axis=1, keepdims=True)

    first_image = image[...]
    parts = project(first_image)
    lane = lax.broadcasted_iota(jnp.int32, (TARGETS, RANK), 1)
    weights[me, 0:8] = parts[:, :RANK] * mid_scale
    weights[me, 8:16] = parts[:, RANK:]
    weights[me, 16:24] = jnp.where(
        lane == 0,
        summed(right * right),
        jnp.where(lane == 1, summed(right * first_image), summed(first_image * first_image)),
    )
    weight_exchange.start()
    near_self(1, 0)
    near_self(1, 1)
    step(image_gather, "arrive")
    image_exchange.wait()
    near_listed(1, 0)
    near_listed(1, 1, 1, 3)
    weight_exchange.wait()
    sums = weights[0, 8:24]
    for dev in range(1, N_LEAF):
        sums = sums + weights[dev, 8:24]
    tops[grp, 0:8] = sums[0:8] * root_scale
    tops[grp, 8:16] = sums[8:16]
    top_exchange.start()
    mid_part = mid_image(lambda dev: stacked(weights[dev, 0:8]))
    near_listed(1, 1, 3, SLOTS)
    top_exchange.wait()
    expand(mid_part, lambda g: stacked(tops[g, 0:8]))

    totals = tops[0, 8:16]
    for g in range(1, N_GRP):
        totals = totals + tops[g, 8:16]
    norm0, curve0, square0 = totals[:, 0:1], totals[:, 1:2], totals[:, 2:3]
    alpha = norm0 / curve0
    norm1 = norm0 - 2.0 * alpha * curve0 + alpha * alpha * square0
    beta = norm1 / norm0
    second_image = jnp.concatenate(
        [finished(first_image, slot) for slot in range(2)], axis=1
    )
    residual = right - alpha * first_image
    direction = residual + beta * right
    image1 = (1.0 + beta) * first_image - alpha * second_image
    solution_ref[...] = alpha * right
    residual_ref[...] = residual
    direction_ref[...] = direction
    image_ref[...] = image1

    diagonal = lax.broadcasted_iota(jnp.int32, (TARGETS, 128), 0) == lax.broadcasted_iota(
        jnp.int32, (TARGETS, 128), 1
    )
    curve1 = jnp.where(diagonal, summed(direction * image1), 0.0)
    sums_leaf[me] = jnp.sum(curve1, axis=0, keepdims=True)
    leaf_exchange.start()
    leaf_exchange.wait()
    total = sums_leaf[0]
    for dev in range(1, N_LEAF):
        total = total + sums_leaf[dev]
    sums_grp[grp] = total
    grp_exchange.start()
    grp_exchange.wait()
    total = sums_grp[0]
    for g in range(1, N_GRP):
        total = total + sums_grp[g]
    curve1 = summed(jnp.where(diagonal, total, 0.0))
    step_ref[...] = jnp.broadcast_to(norm1 / curve1, (TARGETS, BLOCK))

    for sender in (
        *block_gathers,
        *small_gathers,
        *image_gather,
        image_exchange,
        root_exchange,
        weight_exchange,
        top_exchange,
        leaf_exchange,
        grp_exchange,
    ):
        sender.finish()


def on_device(*operands):
    vmem, smem, anywhere = (
        pl.BlockSpec(memory_space=space) for space in (pltpu.VMEM, pltpu.SMEM, pl.ANY)
    )
    messages = 2 * len(LABELS)
    dma = pltpu.SemaphoreType.DMA
    out = jax.ShapeDtypeStruct((TARGETS, BLOCK), F32)
    solution1, residual1, direction, image1, step = pl.pallas_call(
        body,
        out_shape=(out,) * 5,
        in_specs=[vmem, vmem, smem, smem, vmem, vmem, anywhere, anywhere, smem],
        out_specs=(vmem,) * 5,
        scratch_shapes=[
            pltpu.VMEM((2 * N_LEAF, WIDE, LEAF), BF16),
            pltpu.VMEM((2 * N_LEAF, 2 * TARGETS, LEAF), BF16),
            pltpu.VMEM((2, 3 * FEATURES, LEAF), BF16),
            pltpu.VMEM((2, N_LEAF, WIDE, RANK), BF16),
            pltpu.VMEM((N_GRP, WIDE, RANK), BF16),
            pltpu.VMEM((N_LEAF, 3 * TARGETS, RANK), F32),
            pltpu.VMEM((N_GRP, 2 * TARGETS, RANK), F32),
            pltpu.VMEM((N_LEAF, 1, 128), F32),
            pltpu.VMEM((N_GRP, 1, 128), F32),
            pltpu.VMEM((2, RANK, BLOCK), F32),
            pltpu.VMEM((2 * RANK, BLOCK), BF16),
            pltpu.VMEM((2 * RANK, BLOCK), BF16),
            pltpu.VMEM((2, 2 * TARGETS, LEAF), F32),
            pltpu.VMEM((TARGETS, BLOCK), F32),
            pltpu.VMEM((TARGETS, BLOCK), F32),
            pltpu.VMEM((KEPT, 2, LEAF, LEAF), BF16),
            dma((2,)),
            dma((2, messages)),
            dma((2, messages)),
            dma((messages,)),
            dma((messages,)),
            dma((messages,)),
            dma((messages,)),
            dma((N_LEAF,)),
            dma((N_LEAF,)),
            dma((N_GRP,)),
            dma((N_GRP,)),
            dma((N_LEAF,)),
            dma((N_LEAF,)),
            dma((N_GRP,)),
            dma((N_GRP,)),
            dma((N_LEAF,)),
            dma((N_LEAF,)),
            dma((N_GRP,)),
            dma((N_GRP,)),
        ],
        compiler_params=pltpu.CompilerParams(
            collective_id=0, has_side_effects=True, vmem_limit_bytes=62 * 2**20
        ),
    )(*operands)
    return solution1 + step * direction, residual1 - step * image1


def solution(mesh):
    placed = (
        P(None, ("grp", "leaf")),
        P(None, ("grp", "leaf")),
        P(("grp", "leaf"), None),
        P(("grp", "leaf")),
        P(("grp", "leaf"), None),
        P("grp", None),
        P(None, ("grp", "leaf")),
        P(None, ("grp", "leaf")),
        P(),
    )
    return jax.shard_map(
        on_device,
        mesh=mesh,
        in_specs=placed,
        out_specs=(P(None, ("grp", "leaf")), P(None, ("grp", "leaf"))),
        check_vma=False,
    )
```
